32 devices in a mesh: dp: 4 (over y, x), row: 2 (over core), col: 4 (over z).
Axes of the slice: x: 2, y: 2, z: 4, core: 2. Of those that a mesh axis runs over, the one named last changes fastest.
Arguments:
- pixels: bfloat16 [2, 6304, 768], P(None, ('dp', 'col'), 'row'), may hold values from -6 to 6
- patch_mask: int32 [2, 6304], P(None, 'dp'), may hold values from 0 to 1
- class_ids: int32 [2, 32], P(None, 'dp'), may hold values from 0 to 999
- class_counts: int32 [1000], replicated, may hold values from 16 to 64
- step_count: int32 [], replicated, may hold values from 1 to 20
- weight_qkv: bfloat16 [2, 768, 2304], P(None, 'col', 'row'), may hold values from -0.21875 to 0.21875
- weight_out: bfloat16 [2, 768, 768], P(None, 'row', 'col'), may hold values from -1 to 1
- weight_up: bfloat16 [2, 768, 3072], P(None, 'col', 'row'), may hold values from -0.21875 to 0.21875
- weight_down: bfloat16 [2, 3072, 768], P(None, 'row', 'col'), may hold values from -0.109375 to 0.109375
- weight_ends: bfloat16 [2, 768, 768], P(None, 'row', 'col'), may hold values from -0.21875 to 0.21875
- vectors: float32 [227, 768], replicated, may hold values from -3 to 3
- vector_moment: float32 [227, 768], replicated, may hold values from -2.861023e-06 to 2.861023e-06
- vector_second: float32 [227, 768], replicated, may hold values from 2.8765455e-15 to 1.1506182e-14
- ends_moment: float32 [2, 768, 768], P(None, 'row', 'col'), may hold values from -9.536743e-07 to 9.536743e-07
- ends_second: float32 [2, 768, 768], P(None, 'row', 'col'), may hold values from 3.1961616e-16 to 1.2784646e-15
- stat_left: float32 [8, 192, 96, 96], P(('row', 'col'), 'dp'), may hold values from -4.602473e-12 to 1.2886924e-10, as said below
- stat_right: float32 [8, 192, 96, 96], P(('row', 'col'), 'dp'), may hold values from -4.602473e-12 to 1.2886924e-10, as said below
- root_left: float32 [8, 192, 96, 96], P(('row', 'col'), 'dp'), may hold values from -42.488853 to 892.2659
- root_right: float32 [8, 192, 96, 96], P(('row', 'col'), 'dp'), may hold values from -42.488853 to 892.2659
- owner_map: int32 [8, 192], P(('row', 'col')), may hold values from 0 to 191, each once within a row
Outputs:
- loss_total: float32 [], replicated
- grad_norm: float32 [], replicated
- vector_next: float32 [227, 768], replicated
- moment_vector: float32 [227, 768], replicated
- second_vector: float32 [227, 768], replicated
- ends_next: float32 [2, 768, 768], P(None, 'row', 'col')
- moment_ends: float32 [2, 768, 768], P(None, 'row', 'col')
- second_ends: float32 [2, 768, 768], P(None, 'row', 'col')
- block_grad: float32 [8, 192, 96, 96], P(('row', 'col'), 'dp')
- left_next: float32 [8, 192, 96, 96], P(('row', 'col'), 'dp')
- right_next: float32 [8, 192, 96, 96], P(('row', 'col'), 'dp')
- block_next: float32 [8, 192, 96, 96], P(('row', 'col'), 'dp')
The draws below stay inside these ranges and needn't reach their ends.
Inputs may be any that keep to these rules, and one draw needn't show every extreme that they name: `owner_map`: each row names every block once. `stat_left`: symmetric. `stat_right`: symmetric.
All inputs are finite; a program needn't handle non-finite values.
Results may differ from the reference program's by a relative error of at most 0.00074.
Values may be sent and summed in bfloat16 or wider, within the bound.
No kernel may reach another device: no remote copies, remote signals or barrier semaphores. Data moves between devices by JAX's collectives and lax.ppermute only.
A program may use at most 384 MiB of HBM per device.

```python
import math
import jax
import jax.numpy as jnp
from jax import lax

D = 768
HEADS = 12
HD = 64
FF = 3072
PATCH = 768
L = 197
LAYERS = 2
MICRO = 2
CLASSES = 1000
BLK = 96
TOK_MB = 6304
TOKENS = 12608
IMAGES_MB = 32
VROWS = 227
PARAMS = 15509760
GRID = 8
NBLK = 192
N_DP = 4
N_ROW = 2
N_COL = 4


def noise_draw(key, shape):
    return jax.random.truncated_normal(key, -3.0, 3.0, shape, jnp.float32)


def stat_scale():
    return 0.0625 * BLK / (TOKENS * PARAMS)


def diagonal_mask():
    return jnp.arange(BLK)[:, None] == jnp.arange(BLK)[None, :]


def stat_draw(key):
    shape = (GRID, NBLK, BLK, BLK)
    key_diag, key_off = jax.random.split(key)
    diag_vals = jnp.exp(jax.random.uniform(key_diag, (GRID, NBLK, BLK), jnp.float32, 0.0, math.log(4.0)))
    off_vals = noise_draw(key_off, shape) * 0.05
    off_vals = 0.5 * (off_vals + jnp.swapaxes(off_vals, 2, 3))
    return stat_scale() * (jnp.where(diagonal_mask(), diag_vals[..., None], 0.0) + off_vals)


def root_draw(key):
    shape = (GRID, NBLK, BLK, BLK)
    key_diag, key_off = jax.random.split(key)
    diag_vals = jnp.exp(jax.random.uniform(key_diag, (GRID, NBLK, BLK), jnp.float32, math.log(0.5), math.log(2.0)))
    off_vals = noise_draw(key_off, shape) * 0.03
    return stat_scale() ** (-0.25) * (jnp.where(diagonal_mask(), diag_vals[..., None], 0.0) + off_vals)


def draw_patch_mask(key, part):
    token_ids = jnp.arange(TOK_MB, dtype=jnp.int32)
    threshold = 200 + 600 * token_ids // (TOK_MB - 1)
    picks = jax.random.randint(jax.random.fold_in(key, 21), (MICRO, TOK_MB), 0, 1000, jnp.int32)
    return (picks < threshold[None, :]).astype(jnp.int32)


def draw_stat_left(key, part):
    return stat_draw(jax.random.fold_in(key, 11))


def draw_stat_right(key, part):
    return stat_draw(jax.random.fold_in(key, 12))


def draw_root_left(key, part):
    return root_draw(jax.random.fold_in(key, 13))


def draw_root_right(key, part):
    return root_draw(jax.random.fold_in(key, 14))


def draw_vectors(key, part):
    noise_vals = noise_draw(jax.random.fold_in(key, 15), (VROWS, D))
    row_ids = jnp.arange(VROWS)[:, None]
    gain_rows = row_ids == L + 3
    for layer_idx in range(LAYERS):
        gain_rows = gain_rows | (row_ids == L + 6 + 12 * layer_idx) | (row_ids == L + 11 + 12 * layer_idx)
    row_scale = jnp.where(row_ids < L, 0.5, jnp.where((row_ids == L) | (row_ids == L + 1), 1.0, 0.3))
    return jnp.where(gain_rows, 1.0 + 0.15 * noise_vals, row_scale * noise_vals)


def set_ends(entries, key, least, largest):
    shape = entries.shape
    index_at = [jax.random.randint(jax.random.fold_in(key, axis), (), 0, shape[axis]) for axis in range(len(shape))]
    entries = entries.at[tuple(index_at)].set(least)
    longest = shape.index(max(shape))
    index_at[longest] = (index_at[longest] + 1) % shape[longest]
    return entries.at[tuple(index_at)].set(largest)


def block_scale(own_key, dims, cuts, smallest, top_value):
    def one(dim, shards_of):
        draws = jax.random.uniform(jax.random.fold_in(jax.random.fold_in(own_key, 6), dim), (shards_of,), jnp.float32, smallest / len(cuts), top_value / len(cuts))
        return jnp.repeat(jnp.exp(draws), dims[dim] // shards_of).reshape((-1,) + (1,) * (len(dims) - dim - 1))

    level = one(*cuts[0])
    for cut in cuts[1:]:
        level = level * one(*cut)
    return level


def bell_draw(stream_key, shape, width, bound, cuts=(), kind=jnp.bfloat16):
    drawn = jax.random.normal(stream_key, shape, jnp.float32) * width
    if len(cuts) > 0:
        drawn = block_scale(stream_key, shape, cuts, -0.22, 0.18) * drawn
    return jnp.clip(drawn, min=-bound, max=bound).astype(kind)


def setup_inputs(seed: int = 0) -> dict:
    splits = jax.random.split(jax.random.key(seed), 21)
    return {
        "pixels": bell_draw(splits[0], (MICRO, TOK_MB, PATCH), 1.0, 6.0, ((1, 16), (2, 2))),
        "patch_mask": draw_patch_mask(jax.random.fold_in(splits[20], 71), 0),
        "class_ids": set_ends(jax.random.randint(splits[2], (MICRO, IMAGES_MB), 0, CLASSES), jax.random.fold_in(splits[2], 1), 0, CLASSES - 1).astype(jnp.int32),
        "class_counts": set_ends(jax.random.randint(splits[3], (CLASSES,), 16, 65), jax.random.fold_in(splits[3], 1), 16, 64).astype(jnp.int32),
        "step_count": jax.random.randint(splits[4], (), 1, 21).astype(jnp.int32),
        "weight_qkv": bell_draw(splits[5], (LAYERS, D, 3 * D), D ** -0.5, 0.21875, ((1, 4), (2, 2))),
        "weight_out": bell_draw(splits[6], (LAYERS, D, D), 32 ** -0.5, 1.0, ((1, 2), (2, 4))),
        "weight_up": bell_draw(splits[7], (LAYERS, D, FF), D ** -0.5, 0.21875, ((1, 4), (2, 2))),
        "weight_down": bell_draw(splits[8], (LAYERS, FF, D), FF ** -0.5, 0.109375, ((1, 2), (2, 4))),
        "weight_ends": bell_draw(splits[9], (2, PATCH, D), D ** -0.5, 0.21875, ((1, 2), (2, 4))),
        "vectors": draw_vectors(jax.random.fold_in(splits[20], 71), 0),
        "vector_moment": bell_draw(splits[11], (VROWS, D), (0.33 * 0.25 * (TOKENS * PARAMS) ** -0.5), 2.86102294921875e-06, (), jnp.float32),
        "vector_second": jnp.clip(jnp.exp(jax.random.uniform(splits[12], (VROWS, D), jnp.float32, math.log(2.876545488215759e-15), math.log(1.1506181952863036e-14))), 2.876545488215759e-15, 1.1506181952863036e-14),
        "ends_moment": bell_draw(splits[13], (2, PATCH, D), (0.11 * 0.25 * (TOKENS * PARAMS) ** -0.5), 9.5367431640625e-07, ((1, 2), (2, 4)), jnp.float32),
        "ends_second": jnp.clip(jnp.exp(math.log(1.2784646261361867e-15) - 1.3862944 * jax.random.uniform(splits[14], (2, PATCH, D), jnp.float32) ** block_scale(splits[14], (2, PATCH, D), ((1, 2), (2, 4)), -0.2, 0.2)), 3.196161565340467e-16, 1.2784646261361867e-15),
        "stat_left": draw_stat_left(jax.random.fold_in(splits[20], 71), 0),
        "stat_right": draw_stat_right(jax.random.fold_in(splits[20], 71), 0),
        "root_left": draw_root_left(jax.random.fold_in(splits[20], 71), 0),
        "root_right": draw_root_right(jax.random.fold_in(splits[20], 71), 0),
        "owner_map": jax.vmap(lambda own: jax.random.permutation(own, NBLK))(jax.random.split(splits[19], GRID)).reshape((GRID, NBLK)).astype(jnp.int32),
    }


norm_eps = 1e-06
beta_first = 0.9
beta_second = 0.999
adam_eps = 1e-08
decay_stat = 0.5
rate_matrix = 0.02
rate_vector = 0.2
rate_blocks = 0.1
weight_decay = 0.05
clip_scale = 0.25
highest = lax.Precision.HIGHEST

@jax.custom_vjp
def low(v):
    return lax.optimization_barrier(v.astype(jnp.bfloat16)).astype(jnp.float32)

@jax.custom_vjp
def low_back(v):
    return v

def low_keep(v):
    return (low(v), None)

def low_pass(kept, grad):
    return (grad,)

def back_keep(v):
    return (v, None)

def back_low(kept, grad):
    return (low(grad),)
low.defvjp(low_keep, low_pass)
low_back.defvjp(back_keep, back_low)

def product(lhs_mat, rhs_mat):
    return jnp.dot(lhs_mat, rhs_mat, precision=highest)

def layer_norm(residual, gain, shift):
    center = residual - lax.optimization_barrier(jnp.mean(residual, axis=-1, keepdims=True))
    var_rows = lax.optimization_barrier(jnp.mean(center * center, axis=-1, keepdims=True))
    return center * lax.rsqrt(var_rows + norm_eps) * gain + shift

def block_loss(params, pix_rows, mask_rows, keep_rows, count_all):
    weight_qkv, weight_out, weight_up, weight_down, weight_ends, vectors = params
    tokens = pix_rows.shape[0]
    images = tokens // L
    position = jnp.arange(tokens) % L
    first_rows = (position == 0)[:, None]
    hidden_rows = (mask_rows > 0)[:, None]
    embedded = low_back(product(pix_rows, weight_ends[0]) + vectors[L + 2])
    residual = jnp.where(first_rows, vectors[L], jnp.where(hidden_rows, vectors[L + 1], embedded))
    residual = residual + jnp.tile(vectors[:L], (images, 1))
    for layer_idx in range(LAYERS):
        row_base = L + 6 + 12 * layer_idx
        normed = low(layer_norm(residual, vectors[row_base], vectors[row_base + 1]))
        mixed_qkv = product(normed, weight_qkv[layer_idx]).reshape(tokens, HEADS, 3, HD)
        bias_qkv = jnp.stack([vectors[row_base + 2], jnp.zeros((D,), jnp.float32), vectors[row_base + 3]], 0)
        bias_qkv = bias_qkv.reshape(3, HEADS, HD).transpose(1, 0, 2)
        mixed_qkv = low_back(mixed_qkv + bias_qkv)
        queries = low(mixed_qkv[:, :, 0] * 0.125).reshape(images, L, HEADS, HD)
        key_rows = low(mixed_qkv[:, :, 1]).reshape(images, L, HEADS, HD)
        values = low(mixed_qkv[:, :, 2]).reshape(images, L, HEADS, HD)
        scores = low_back(jnp.einsum('bqhd,bkhd->bhqk', queries, key_rows, precision=highest))
        attend = low(jax.nn.softmax(scores, axis=-1))
        context = low_back(jnp.einsum('bhqk,bkhd->bqhd', attend, values, precision=highest))
        context = low(context).reshape(tokens, D)
        residual = residual + low_back(product(context, weight_out[layer_idx]) + vectors[row_base + 4])
        normed = low(layer_norm(residual, vectors[row_base + 5], vectors[row_base + 6]))
        hidden_pre = low_back(product(normed, weight_up[layer_idx]) + vectors[row_base + 7:row_base + 11].reshape(FF))
        active = low(jax.nn.gelu(hidden_pre, approximate=False))
        residual = residual + low_back(product(active, weight_down[layer_idx]) + vectors[row_base + 11])
    final = low(layer_norm(residual, vectors[L + 3], vectors[L + 4]))
    predict = low_back(jnp.dot(final, weight_ends[1].T, precision=highest) + vectors[L + 5])
    pred_error = predict - pix_rows
    return jnp.sum(keep_rows * lax.optimization_barrier(jnp.sum(pred_error * pred_error, axis=-1))) / (PATCH * count_all)

def tile_blocks(matrix, rows_parts, rows_idx, cols_parts, cols_idx):
    rows_tile = matrix.shape[0] // rows_parts
    cols_tile = matrix.shape[1] // cols_parts
    tile_mat = matrix[rows_idx * rows_tile:(rows_idx + 1) * rows_tile, cols_idx * cols_tile:(cols_idx + 1) * cols_tile]
    tile_mat = tile_mat.reshape(rows_tile // BLK, BLK, cols_tile // BLK, BLK).transpose(0, 2, 1, 3)
    return tile_mat.reshape(-1, BLK, BLK)

def grid_blocks(matrices, row_idx, col_idx):
    pieces = []
    for layer_idx in range(LAYERS):
        pieces.append(tile_blocks(matrices[0][layer_idx], N_COL, col_idx, N_ROW, row_idx))
        pieces.append(tile_blocks(matrices[1][layer_idx], N_ROW, row_idx, N_COL, col_idx))
        pieces.append(tile_blocks(matrices[2][layer_idx], N_COL, col_idx, N_ROW, row_idx))
        pieces.append(tile_blocks(matrices[3][layer_idx], N_ROW, row_idx, N_COL, col_idx))
    return jnp.concatenate(pieces, axis=0)

def adam_update(weight, gradient, moment, second, rate, decay, factor, step_value):
    clipped = gradient * factor
    moment_new = beta_first * moment + (1.0 - beta_first) * clipped
    second_new = beta_second * second + (1.0 - beta_second) * clipped * clipped
    corr_first = 1.0 - jnp.power(beta_first, step_value)
    corr_second = 1.0 - jnp.power(beta_second, step_value)
    stride = moment_new / corr_first / (jnp.sqrt(second_new / corr_second) + adam_eps)
    return (weight - rate * (stride + decay * weight), moment_new, second_new)

def reference(pixels, patch_mask, class_ids, class_counts, step_count, weight_qkv, weight_out, weight_up, weight_down, weight_ends, vectors, vector_moment, vector_second, ends_moment, ends_second, stat_left, stat_right, root_left, root_right, owner_map):
    groups = MICRO * N_DP
    group_tok = TOK_MB // N_DP
    pix_groups = pixels.astype(jnp.float32).reshape(groups, group_tok, PATCH)
    mask_groups = patch_mask.reshape(groups, group_tok)
    position = jnp.arange(group_tok) % L
    live_groups = ((mask_groups > 0) & (position != 0)[None, :]).astype(jnp.float32)
    count_all = jnp.sum(live_groups)
    image_weight = 32.0 / class_counts.astype(jnp.float32)[class_ids]
    weight_rows = jnp.repeat(image_weight.reshape(groups, -1), L, axis=1)
    keep_groups = weight_rows * live_groups
    params = (weight_qkv.astype(jnp.float32), weight_out.astype(jnp.float32), weight_up.astype(jnp.float32), weight_down.astype(jnp.float32), weight_ends.astype(jnp.float32), vectors)

    def total_loss(params_in):

        def step_fn(running, block_in):
            return (running + jax.checkpoint(block_loss)(params_in, block_in[0], block_in[1], block_in[2], count_all), None)
        total_value, unused = lax.scan(step_fn, jnp.float32(0.0), (pix_groups, mask_groups, keep_groups))
        return total_value
    loss_total, pullback = jax.vjp(total_loss, params)
    grads = pullback(jnp.ones((), loss_total.dtype))[0]
    grad_norm = jnp.sqrt(sum((jnp.sum(grad_item * grad_item) for grad_item in grads)))
    factor = jnp.minimum(1.0, clip_scale / math.sqrt(TOKENS) / grad_norm)
    step_value = step_count.astype(jnp.float32)
    vector_next, moment_vector, second_vector = adam_update(vectors, grads[5], vector_moment, vector_second, rate_vector, 0.0, factor, step_value)
    ends_next, moment_ends, second_ends = adam_update(params[4], grads[4], ends_moment, ends_second, rate_matrix, weight_decay, factor, step_value)
    grad_list, left_list, right_list, weight_list = ([], [], [], [])
    for grid_idx in range(N_ROW * N_COL):
        row_idx = grid_idx // N_COL
        col_idx = grid_idx % N_COL
        slot_order = owner_map[grid_idx]
        block_g = jnp.take(grid_blocks(grads[:4], row_idx, col_idx), slot_order, axis=0) * factor
        block_w = jnp.take(grid_blocks(params[:4], row_idx, col_idx), slot_order, axis=0)
        left_list.append(decay_stat * stat_left[grid_idx] + (1.0 - decay_stat) * jnp.einsum('sij,skj->sik', block_g, block_g, precision=highest))
        right_list.append(decay_stat * stat_right[grid_idx] + (1.0 - decay_stat) * jnp.einsum('sji,sjk->sik', block_g, block_g, precision=highest))
        inner_prod = jnp.einsum('sij,sjk->sik', block_g, root_right[grid_idx], precision=highest)
        precond = jnp.einsum('sij,sjk->sik', root_left[grid_idx], inner_prod, precision=highest)
        weight_list.append(block_w - rate_blocks * (precond + weight_decay * block_w))
        grad_list.append(block_g)
    return (loss_total, grad_norm, vector_next, moment_vector, second_vector, ends_next, moment_ends, second_ends, jnp.stack(grad_list), jnp.stack(left_list), jnp.stack(right_list), jnp.stack(weight_list))
```

```python
import math

import jax
import jax.numpy as jnp
from jax import lax
from jax.experimental import pallas as pl
from jax.experimental.pallas import tpu as pltpu
from jax.sharding import PartitionSpec as P

HD = 64
PATCH = 768
L = 197
LP = 208
BLK = 96

norm_eps = 1e-06
beta_first = 0.9
beta_second = 0.999
adam_eps = 1e-08
decay_stat = 0.5
rate_matrix = 0.02
rate_vector = 0.2
rate_blocks = 0.1
weight_decay = 0.05
clip_scale = 0.25
highest = lax.Precision.HIGHEST
bf16 = jnp.bfloat16
f16 = jnp.float16
f32 = jnp.float32


COST = 16
VMEM = pl.BlockSpec(memory_space=pltpu.VMEM)
SMEM = pl.BlockSpec(memory_space=pltpu.SMEM)


def whole_call(body, outs, name, flops, scratch=()):
    return pl.pallas_call(
        body,
        out_shape=[jax.ShapeDtypeStruct(shape, dtype) for shape, dtype in outs],
        scratch_shapes=list(scratch),
        compiler_params=pltpu.CompilerParams(vmem_limit_bytes=52 * 2**20),
        cost_estimate=pl.CostEstimate(flops=flops // COST, bytes_accessed=2**16, transcendentals=0),
        name=name,
    )


def dot(lhs_mat, rhs_mat, lhs_dim, rhs_dim):
    return lax.dot_general(
        lhs_mat, rhs_mat, (((lhs_dim,), (rhs_dim,)), ((), ())), preferred_element_type=f32
    )


def exact(lhs_mat, rhs_mat, lhs_dim, rhs_dim):
    return lax.dot_general(
        lhs_mat,
        rhs_mat,
        (((lhs_dim,), (rhs_dim,)), ((), ())),
        precision=highest,
        preferred_element_type=f32,
    )


def swap(value, axis, mask):
    size = lax.axis_size(axis)
    return lax.ppermute(value, axis, [(i, i ^ mask) for i in range(size)])


def bits_of(axis):
    return [1 << b for b in range(lax.axis_size(axis).bit_length() - 1)]


def butterfly(value, axes, op=jnp.add):
    for axis in axes:
        for mask in bits_of(axis):
            value = op(value, swap(value, axis, mask))
    return value


def softmax_scores(queries, key_rows):
    scores = dot(queries, key_rows, 1, 1)
    spot = lax.broadcasted_iota(jnp.int32, scores.shape, 1)
    scores = jnp.where(spot < L, scores, -1e30)
    top = jnp.max(scores, axis=1, keepdims=True)
    exponent = jnp.exp(scores - top)
    return exponent / jnp.sum(exponent, axis=1, keepdims=True)


def attend_forward(qkv_ref, ctx_ref):
    rows, wide = qkv_ref.shape
    for image in range(rows // LP):
        span = slice(image * LP, (image + 1) * LP)
        for pair in range(wide // (6 * HD)):
            made = []
            for head in (2 * pair, 2 * pair + 1):
                base = head * 3 * HD
                queries = qkv_ref[span, base : base + HD]
                key_rows = qkv_ref[span, base + HD : base + 2 * HD]
                values = qkv_ref[span, base + 2 * HD : base + 3 * HD]
                attend = softmax_scores(queries, key_rows).astype(bf16)
                made.append(dot(attend, values, 1, 0).astype(bf16))
            ctx_ref[span, pair * 2 * HD : (pair + 1) * 2 * HD] = jnp.concatenate(made, axis=1)


def attend_backward(qkv_ref, grad_ref, out_ref):
    rows, wide = qkv_ref.shape
    for image in range(rows // LP):
        span = slice(image * LP, (image + 1) * LP)
        for pair in range(wide // (6 * HD)):
            made = []
            for head in (2 * pair, 2 * pair + 1):
                base = head * 3 * HD
                queries = qkv_ref[span, base : base + HD]
                key_rows = qkv_ref[span, base + HD : base + 2 * HD]
                values = qkv_ref[span, base + 2 * HD : base + 3 * HD]
                grad = grad_ref[span, head * HD : (head + 1) * HD].astype(bf16)
                attend = softmax_scores(queries, key_rows)
                grad_values = dot(attend.astype(bf16), grad, 0, 0)
                grad_attend = dot(grad, values, 1, 1)
                inner = jnp.sum(grad_attend * attend, axis=1, keepdims=True)
                grad_scores = (attend * (grad_attend - inner)).astype(bf16)
                made.append((dot(grad_scores, key_rows, 1, 0) * 0.125).astype(bf16))
                made.append(dot(grad_scores, queries, 0, 0).astype(bf16))
                made.append(grad_values.astype(bf16))
            out_ref[span, pair * 6 * HD : (pair + 1) * 6 * HD] = jnp.concatenate(made, axis=1)


def normed_of(residual):
    center = residual - jnp.mean(residual, axis=1, keepdims=True)
    inverse = lax.rsqrt(jnp.mean(center * center, axis=1, keepdims=True) + norm_eps)
    return center * inverse, inverse


def norm_backward(grad_normed, residual, gain):
    normed, inverse = normed_of(residual)
    scaled = grad_normed * gain
    mean_one = jnp.mean(scaled, axis=1, keepdims=True)
    mean_two = jnp.mean(scaled * normed, axis=1, keepdims=True)
    grad_in = inverse * (scaled - mean_one - normed * mean_two)
    gain_sum = jnp.sum(grad_normed * normed, axis=0, keepdims=True)
    return grad_in, gain_sum, jnp.sum(grad_normed, axis=0, keepdims=True)


def rows_sum(value):
    return jnp.sum(value.astype(f32), axis=0, keepdims=True)


def put_rows(ref, rows):
    ref[...] = jnp.zeros(ref.shape, f32)
    for i, row in enumerate(rows):
        ref[i : i + 1, :] = row


def own_first(row, core):
    half = row.shape[1] // 2
    return jnp.where(core == 1, jnp.concatenate([row[:, half:], row[:, :half]], axis=1), row)


def qkv_part(base, places, vec, vectors, residual, weights, low_one, qkv, context):
    normed, _ = normed_of(residual)
    low_one[...] = (normed * vec[base : base + 1, :] + vec[base + 1 : base + 2, :]).astype(bf16)
    query_bias = own_first(vectors[base + 2 : base + 3, :], places[1])
    value_bias = own_first(vectors[base + 3 : base + 4, :], places[1])
    for half in range(2):
        heads = qkv[half].shape[1] // (3 * HD)
        parts = []
        for head in range(heads):
            at = (half * heads + head) * HD
            parts += [query_bias[:, at : at + HD], jnp.zeros((1, HD), f32), value_bias[:, at : at + HD]]
        bias = jnp.concatenate(parts, axis=1)
        kind = (lax.broadcasted_iota(jnp.int32, bias.shape, 1) // HD) % 3
        factor = jnp.where(kind == 0, 0.125, 1.0)
        step = 6 * HD
        for at in range(0, heads * 3 * HD, step):
            span = slice(at, at + step)
            mixed = dot(low_one[...], weights[half][:, span], 1, 0)
            qkv[half][:, span] = ((mixed + bias[:, span]) * factor[:, span]).astype(bf16)
        attend_forward(qkv[half], context[half])


def embed_qkv_body(
    places, vec, vectors, pix_a, pix_b, flags, ends_a, ends_b, qkv_a, qkv_b,
    residual, low_one, out_a, out_b, ctx_a, ctx_b,
):
    embedded = dot(pix_a[...], ends_a[...], 1, 1) + dot(pix_b[...], ends_b[...], 1, 1)
    embedded = embedded + vec[L + 2 : L + 3, :]
    spots = vec[0:LP, :]
    spots = jnp.concatenate([spots] * (embedded.shape[0] // LP), axis=0)
    picked = jnp.where(flags[:, 1:2] > 0, vec[L + 1 : L + 2, :], embedded)
    picked = jnp.where(flags[:, 0:1] > 0, vec[L : L + 1, :], picked)
    residual[...] = jnp.where(flags[:, 2:3] > 0, picked + spots, 0.0)
    qkv_part(
        L + 6, places, vec, vectors, residual[...], (qkv_a, qkv_b), low_one, (out_a, out_b), (ctx_a, ctx_b)
    )


def up_body(
    base, places, vec, vectors, residual, ctx_a, ctx_b, out_a, out_b, up_a, up_b,
    mid, low_two, act_a, act_b, slope_a, slope_b,
):
    branch = dot(ctx_a[...], out_a[...], 1, 1) + dot(ctx_b[...], out_b[...], 1, 1)
    mid[...] = residual[...] + (branch + vec[base + 4 : base + 5, :])
    normed, _ = normed_of(mid[...])
    low_two[...] = (normed * vec[base + 5 : base + 6, :] + vec[base + 6 : base + 7, :]).astype(bf16)
    wide = vec.shape[1]
    for half, (weight, active, slope) in enumerate(((up_a, act_a, slope_a), (up_b, act_b, slope_b))):
        for k in range(weight.shape[1] // wide):
            row = base + 7 + (weight.shape[1] // wide) * jnp.bitwise_xor(places[1], half) + k
            span = slice(k * wide, (k + 1) * wide)
            pre = dot(low_two[...], weight[:, span], 1, 0) + vectors[pl.ds(row, 1), :]
            phi = 0.5 * (1.0 + lax.erf(pre * math.sqrt(0.5)))
            active[:, span] = (pre * phi).astype(bf16)
            slope[:, span] = phi + pre * (jnp.exp(-0.5 * pre * pre) * (1.0 / math.sqrt(2.0 * math.pi)))


def down_qkv_body(
    base, places, vec, vectors, mid, act_a, act_b, down_a, down_b, qkv_a, qkv_b,
    residual, low_one, out_a, out_b, ctx_a, ctx_b,
):
    branch = dot(act_a[...], down_a[...], 1, 1) + dot(act_b[...], down_b[...], 1, 1)
    residual[...] = mid[...] + (branch + vec[base - 1 : base, :])
    qkv_part(
        base, places, vec, vectors, residual[...], (qkv_a, qkv_b), low_one, (out_a, out_b), (ctx_a, ctx_b)
    )


def down_head_body(
    base, places, vec, vectors, scale, mid, act_a, act_b, down_a, down_b, ends_a, ends_b, pix_a, pix_b, flags,
    low_fin, pred_a, pred_b, grad_res, grad_low, wide, flat, loss,
):
    branch = dot(act_a[...], down_a[...], 1, 1) + dot(act_b[...], down_b[...], 1, 1)
    residual = mid[...] + (branch + vec[base + 11 : base + 12, :])
    normed, _ = normed_of(residual)
    low_fin[...] = (normed * vec[L + 3 : L + 4, :] + vec[L + 4 : L + 5, :]).astype(bf16)
    bias = own_first(vectors[L + 5 : L + 6, :], places[1])
    keep = flags[:, 3:4]
    total = jnp.zeros((1, 1), f32)
    sums = []
    for half, (ends, pix, pred) in enumerate(((ends_a, pix_a, pred_a), (ends_b, pix_b, pred_b))):
        span = ends.shape[1]
        error = dot(low_fin[...], ends[...], 1, 0) + bias[:, half * span : (half + 1) * span]
        error = error - pix[...].astype(f32)
        total = total + jnp.sum(jnp.sum(keep * error * error, axis=1, keepdims=True), axis=0, keepdims=True)
        pred[...] = (2.0 * scale[0] * keep * error).astype(bf16)
        sums.append(rows_sum(pred[...]))
    loss[...] = jnp.broadcast_to(total * scale[0], loss.shape)
    grad_fin = dot(pred_a[...], ends_a[...], 1, 1) + dot(pred_b[...], ends_b[...], 1, 1)
    grad, gain_sum, shift_sum = norm_backward(grad_fin, residual, vec[L + 3 : L + 4, :])
    grad_res[...] = grad
    grad_low[...] = grad.astype(bf16)
    put_rows(wide, [gain_sum, shift_sum])
    put_rows(flat, [jnp.concatenate(sums, axis=1)])


def back_mlp_body(
    base, vec, grad_res, grad_low, down_a, down_b, slope_a, slope_b, up_a, up_b, mid,
    grad_mid, mid_low, hid_a, hid_b, wide, flat,
):
    span = vec.shape[1]
    sums = []
    total = None
    for down, slope, up, hid in ((down_a, slope_a, up_a, hid_a), (down_b, slope_b, up_b, hid_b)):
        for at in range(0, down.shape[1], span):
            cols = slice(at, at + span)
            hid[:, cols] = (dot(grad_low[...], down[:, cols], 1, 0) * slope[:, cols]).astype(bf16)
            sums.append(rows_sum(hid[:, cols]))
        part = dot(hid[...], up[...], 1, 1)
        total = part if total is None else total + part
    grad, gain_sum, shift_sum = norm_backward(total, mid[...], vec[base + 5 : base + 6, :])
    grad = grad_res[...] + grad
    grad_mid[...] = grad
    mid_low[...] = grad.astype(bf16)
    put_rows(wide, [rows_sum(grad_low[...]), gain_sum, shift_sum])
    put_rows(flat, sums)


def back_attend_body(
    base, vec, grad_mid, mid_low, out_a, out_b, qkv_a, qkv_b, wqkv_a, wqkv_b, residual,
    grad_res, grad_low, mix_a, mix_b, wide, flat, ctx,
):
    total = None
    query_sums, value_sums = [], []
    for out, qkv, wqkv, mix in ((out_a, qkv_a, wqkv_a, mix_a), (out_b, qkv_b, wqkv_b, mix_b)):
        ctx[...] = dot(mid_low[...], out[...], 1, 0)
        attend_backward(qkv, ctx, mix)
        part = dot(mix[...], wqkv[...], 1, 1)
        total = part if total is None else total + part
        sums = rows_sum(mix[...])
        for head in range(mix.shape[1] // (3 * HD)):
            at = head * 3 * HD
            query_sums.append(sums[:, at : at + HD])
            value_sums.append(sums[:, at + 2 * HD : at + 3 * HD])
    grad, gain_sum, shift_sum = norm_backward(total, residual[...], vec[base : base + 1, :])
    grad = grad_mid[...] + grad
    grad_res[...] = grad
    grad_low[...] = grad.astype(bf16)
    put_rows(wide, [rows_sum(mid_low[...]), gain_sum, shift_sum])
    put_rows(flat, [jnp.concatenate(query_sums, axis=1), jnp.concatenate(value_sums, axis=1)])


def back_embed_body(grad_res, flags, grad_low, place, wide):
    grad = grad_res[...]
    low = jnp.where(flags[:, 4:5] > 0, grad, 0.0).astype(bf16)
    grad_low[...] = low
    total = grad[0:LP]
    for image in range(1, grad.shape[0] // LP):
        total = total + grad[image * LP : (image + 1) * LP]
    place[...] = total
    class_sum = rows_sum(jnp.where(flags[:, 0:1] > 0, grad, 0.0))
    mask_sum = rows_sum(jnp.where(flags[:, 1:2] > 0, grad, 0.0))
    put_rows(wide, [class_sum, mask_sum, rows_sum(low)])


def tie(*trees):
    leaves, shape = jax.tree.flatten(trees)
    return jax.tree.unflatten(shape, lax.optimization_barrier(leaves))


def prepare_body(plan, cuts, places, qkv, out, up, down, ends, *rest):
    outs, turned = rest[:-1], rest[-1]
    whole, owns, firsts = outs[0], outs[1::2], outs[2::2]
    sub_at = places[0]
    part = whole.shape[1]
    refs = {"qkv": qkv, "out": out, "up": up, "down": down, "ends": ends}
    for chunk in range(len(cuts) - 1):
        begin = plan[cuts[chunk]][2]
        for name, layer, start, width in plan[cuts[chunk] : cuts[chunk + 1]]:
            ref = refs[name]
            plain = name in ("qkv", "up")
            if not plain:
                turned[:, :width] = ref[layer].T.astype(f32)
            for k in range(4):
                rows = pl.ds(pl.multiple_of(jnp.bitwise_xor(sub_at, k) * part, 16), part)
                piece = ref[layer, rows, :] if plain else turned[rows, :width].astype(bf16)
                whole[k, :, start : start + width] = piece
                owns[chunk][k, :, start - begin : start - begin + width] = piece
                if k == 0:
                    firsts[chunk][:, start - begin : start - begin + width] = piece


def prepare_tiles(plan, cuts, places, qkv, out, up, down, ends):
    height = qkv.shape[1]
    part = height // 4
    outs = [((4, part, plan[-1][2] + plan[-1][3]), bf16)]
    for j, k in zip(cuts[:-1], cuts[1:]):
        width = plan[k - 1][2] + plan[k - 1][3] - plan[j][2]
        outs += [((4, part, width), bf16), ((part, width), bf16)]
    widest = max(entry[3] for entry in plan)
    got = whole_call_smem(
        lambda *refs: prepare_body(plan, cuts, *refs), 1, 5, outs, "prepare_tiles", 10**8,
        [pltpu.VMEM((height, widest), f32)],
    )(places, qkv, out, up, down, ends)
    return got[0], got[1::2], got[2::2]


def whole_call_smem(body, scalars, arrays, outs, name, flops, scratch=()):
    return pl.pallas_call(
        body,
        in_specs=[SMEM] * scalars + [VMEM] * arrays,
        out_specs=[VMEM] * len(outs),
        out_shape=[jax.ShapeDtypeStruct(shape, dtype) for shape, dtype in outs],
        scratch_shapes=list(scratch),
        compiler_params=pltpu.CompilerParams(vmem_limit_bytes=52 * 2**20),
        cost_estimate=pl.CostEstimate(flops=flops // COST, bytes_accessed=2**16, transcendentals=0),
        name=name,
    )


def assemble_body(widths, own, stack, from_x, from_y, left, right, *outs):
    part = own.shape[1]
    half = left.shape[1]
    start = 0
    for out, width in zip(outs, widths):
        stop = start + width
        for k in range(4):
            out[4 * k * part : (4 * k + 1) * part, :] = own[k, :, start:stop]
            rows = slice((4 * k + 1) * part, 4 * (k + 1) * part)
            if k < 3:
                out[rows, :] = (stack, from_x, from_y)[k][:, start:stop]
                continue
            middle = min(max(half, start), stop)
            if middle > start:
                out[rows, : middle - start] = left[:, start:middle]
            if stop > middle:
                out[rows, middle - start :] = right[:, middle - half : stop - half]
        start = stop


class Gather:
    def __init__(self, own, first, widths):
        self.own, self.first, self.widths = own, first, widths
        self.state = []

    def along(self):
        self.state = [jnp.concatenate([swap(self.first, "col", k) for k in (1, 2, 3)], axis=0)]

    def across(self):
        stack = self.state[0]
        self.state = [stack, swap(stack, "dp", 1), swap(stack, "dp", 2)]

    def diagonal(self):
        stack, from_x, from_y = self.state
        half = stack.shape[1] // 256 * 128
        left = swap(from_x[:, :half], "dp", 2)
        right = swap(from_y[:, half:], "dp", 1)
        self.state = [stack, from_x, from_y, left, right]

    def weights(self):
        height = 16 * self.own.shape[1]
        mine = whole_call(
            lambda *refs: assemble_body(self.widths, *refs),
            [((height, w), bf16) for w in self.widths],
            "assemble",
            10**8,
        )(self.own, *self.state)
        return [(w, swap(w, "row", 1)) for w in mine]


DIMS = ("y", "x", "c1", "c0")
WHERE = {"c1": ("col", 2), "c0": ("col", 1), "y": ("dp", 2), "x": ("dp", 1)}


def row_runs(name, part):
    block = part << (3 - DIMS.index(name))
    count = 16 * part // block
    return [(i * block, block) for i in range(0, count, 2)], [(i * block, block) for i in range(1, count, 2)]


def product_body(runs, left, left_got, right, right_got, keep, send, power, total):
    total[...] = dot(left[...], right[...], 0, 0) + dot(left_got[...], right_got[...], 0, 0)
    top = jnp.max(jnp.abs(total[...]), axis=0, keepdims=True)
    exponent = jnp.clip(jnp.ceil(jnp.log2(top)) + 1.0, -100.0, 120.0)
    scale = jnp.exp2(14.0 - exponent)
    power[...] = exponent
    for out, spans, factor in ((keep, runs[0], None), (send, runs[1], scale)):
        at = 0
        for start, size in spans:
            piece = total[start : start + size, :]
            out[at : at + size, :] = piece if factor is None else piece * factor
            at += size
    send[at:, :] = jnp.broadcast_to(exponent, (16, exponent.shape[1]))


def product_sum(name, left, left_got, right, right_got, block, blocks):
    rows, height = left.shape
    width = block * len(blocks)
    first = blocks[0]
    runs = row_runs(name, height // 16)
    whole = pl.BlockSpec((rows, height), lambda i: (0, 0))
    part = pl.BlockSpec((rows, block), lambda i: (0, i + first))
    half = pl.BlockSpec((height // 2, block), lambda i: (0, i))
    return pl.pallas_call(
        lambda *refs: product_body(runs, *refs),
        grid=(len(blocks),),
        in_specs=[whole, whole, part, part],
        out_specs=[
            half,
            pl.BlockSpec((height // 2 + 16, block), lambda i: (0, i)),
            pl.BlockSpec((1, block), lambda i: (0, i)),
        ],
        out_shape=[
            jax.ShapeDtypeStruct((height // 2, width), f32),
            jax.ShapeDtypeStruct((height // 2 + 16, width), f32),
            jax.ShapeDtypeStruct((1, width), f32),
        ],
        scratch_shapes=[pltpu.VMEM((height, block), f32)],
        compiler_params=pltpu.CompilerParams(vmem_limit_bytes=32 * 2**20),
        cost_estimate=pl.CostEstimate(
            flops=4 * rows * height * width // COST, bytes_accessed=2**16, transcendentals=0
        ),
        name="product_sum",
    )(left, left_got, right, right_got)


def lowered(rows, exponent):
    tail = jnp.broadcast_to(exponent, (16, exponent.shape[1]))
    return jnp.concatenate([rows * jnp.exp2(14.0 - exponent), tail], axis=0).astype(f16)


def tail_of(payload):
    return jnp.max(payload[-16:].astype(f32), axis=0, keepdims=True)


def decoded(rows, exponent):
    return rows.astype(f32) * jnp.exp2(exponent - 14.0)


def halves(rows, block):
    shaped = rows.reshape(-1, 2, block, rows.shape[1])
    return shaped[:, 0].reshape(-1, rows.shape[1]), shaped[:, 1].reshape(-1, rows.shape[1])


class Reduce:
    def __init__(self, first_x, first_y):
        self.parts = []
        for products in (first_x, first_y):
            keep, send, exponent = (jnp.concatenate(list(p), axis=1) for p in zip(*products))
            self.parts.append([keep, send.astype(f16), exponent])
        self.stage = 0

    def send(self):
        ways = ((("dp", 1), ("dp", 2)), (("dp", 2), ("dp", 1)), (("col", 1),), (("col", 2),))[self.stage]
        self.got = [swap(part[1], axis, mask) for part, (axis, mask) in zip(self.parts, ways)]

    def absorb(self):
        part = self.parts[0][0].shape[0] * 2 // (16 >> self.stage)
        if self.stage == 0:
            blocks = (8 * part // 2, 4 * part)
        elif self.stage == 1:
            blocks = (part, part)
        elif self.stage == 2:
            blocks = (part,)
        made = []
        for i, ((keep, _, exponent), got) in enumerate(zip(self.parts, self.got)):
            theirs = tail_of(got)
            after = jnp.maximum(exponent, theirs) + 1.0
            if self.stage == 3:
                made.append([keep + decoded(got[:-16], theirs), None, after])
                continue
            stay, leave = halves(keep, blocks[i])
            got_stay, got_leave = halves(got[:-16], blocks[i])
            stay = stay + decoded(got_stay, theirs)
            leave = leave + decoded(got_leave, theirs)
            made.append([stay, leave, after])
        if self.stage == 1:
            made = [[jnp.concatenate(list(p), axis=1) for p in zip(*made)]]
        self.stage += 1
        if self.stage < 4:
            self.parts = [[stay, lowered(leave, after), after] for stay, leave, after in made]
            return
        keep, _, after = made[0]
        for mask in bits_of("dp")[2:]:
            keep = keep + swap(keep, "dp", mask)
            after = after + 1.0
        self.parts = []
        self.keep, self.exponent = keep, after


def shampoo_body(
    group, layout, info, weight, *rest
):
    pieces, (rl, rr, grad_out, left, right, precond, weight_out), grads = rest[:-8], rest[-8:-1], rest[-1]
    step = pl.program_id(0)

    @pl.when(step == 0)
    def _():
        for ref, (sub, spans) in zip(pieces, layout):
            for source, target, size in spans:
                grads[sub, :, target : target + size] = ref[:, source : source + size]

    window = 2 * 128

    def block_of(ref, slot):
        start = pl.multiple_of(info[2, slot] * 128, 128)
        tops = [ref[info[k, slot], :, pl.ds(start, window)].astype(f32) for k in range(2)]
        both = jnp.concatenate(tops, axis=0)
        both = pltpu.roll(both, info[3, slot], 1)[:, :BLK]
        return jnp.where(info[4, slot] == 1, both.T, both)

    for j in range(group):
        slot = step * group + j
        g = block_of(grads, slot)
        grad_out[j] = g
        weight_out[j] = block_of(weight, slot)
        left[j] = exact(g, g, 1, 1)
        right[j] = exact(g, g, 0, 0)
        precond[j] = exact(rl[j], exact(g, rr[j], 1, 0), 1, 0)


def shampoo(info, weight, pieces, layout, root_left, root_right):
    count = root_left.shape[0]
    group = next(g for g in (8, 6, 4, 3, 2, 1) if count % g == 0)
    plain = pl.BlockSpec((group, BLK, BLK), lambda i: (i, 0, 0))
    return pl.pallas_call(
        lambda *refs: shampoo_body(group, layout, *refs),
        grid=(count // group,),
        in_specs=[SMEM] + [VMEM] * (1 + len(pieces)) + [plain] * 2,
        out_specs=[plain] * 5,
        out_shape=[jax.ShapeDtypeStruct((count, BLK, BLK), f32)] * 5,
        scratch_shapes=[pltpu.VMEM(weight.shape, f32)],
        compiler_params=pltpu.CompilerParams(vmem_limit_bytes=52 * 2**20),
        cost_estimate=pl.CostEstimate(
            flops=count * 48 * BLK**3 // COST, bytes_accessed=2**16, transcendentals=0
        ),
        name="shampoo",
    )(info, weight, *pieces, root_left, root_right)


def ends_body(places, *refs):
    out = refs[-1]
    part = refs[0].shape[0]
    for end in range(2):
        for k in range(4):
            sub = jnp.bitwise_xor(places[0], k)
            out[end, pl.ds(pl.multiple_of(sub * part, 8), part), :] = refs[4 * end + k][...]


def adam_update(weight, gradient, moment, second, rate, decay, factor, step_value):
    clipped = gradient * factor
    moment_new = beta_first * moment + (1.0 - beta_first) * clipped
    second_new = beta_second * second + (1.0 - beta_second) * clipped * clipped
    corr_first = 1.0 - jnp.power(beta_first, step_value)
    corr_second = 1.0 - jnp.power(beta_second, step_value)
    stride = moment_new / corr_first / (jnp.sqrt(second_new / corr_second) + adam_eps)
    return (weight - rate * (stride + decay * weight), moment_new, second_new)


def shards(
    pixels,
    patch_mask,
    class_ids,
    class_counts,
    step_count,
    weight_qkv,
    weight_out,
    weight_up,
    weight_down,
    weight_ends,
    vectors,
    vector_moment,
    vector_second,
    ends_moment,
    ends_second,
    stat_left,
    stat_right,
    root_left,
    root_right,
    owner_map,
):
    data_count = lax.axis_size("dp")
    row_index = lax.axis_index("row")
    col_index = lax.axis_index("col")
    data_index = lax.axis_index("dp")
    sub_index = data_index & 3
    layer_count = weight_qkv.shape[0]
    width = vectors.shape[1]
    images = pixels.shape[1] // L
    total_tokens = pixels.shape[0] * pixels.shape[1] * lax.axis_size("col") * data_count
    places = jnp.stack([sub_index, row_index]).astype(jnp.int32)
    swapped = row_index == 1

    names = [("ends", 0)]
    for i in range(layer_count):
        names += [("qkv", i), ("out", i), ("up", i), ("down", i)]
    names.append(("ends", 1))
    sizes = {
        "qkv": weight_qkv.shape[2],
        "out": weight_out.shape[1],
        "up": weight_up.shape[2],
        "down": weight_down.shape[1],
        "ends": weight_ends.shape[1],
    }
    plan, at = [], 0
    for name, i in names:
        plan.append((name, i, at, sizes[name]))
        at += sizes[name]
    start_of = {entry[:2]: entry[2] for entry in plan}
    cuts = [0]
    for i in range(layer_count):
        cuts += [2 + 4 * i, 4 + 4 * i]
    cuts.append(len(plan))
    tiles_own, owns, firsts = prepare_tiles(
        plan, cuts, places, weight_qkv, weight_out, weight_up, weight_down, weight_ends
    )
    chunks = [
        Gather(own, first, [entry[3] for entry in plan[j:k]])
        for own, first, j, k in zip(owns, firsts, cuts[:-1], cuts[1:])
    ]

    part = weight_qkv.shape[1] // 4
    column = jnp.arange(width)
    piece, inner = column // part, column % part
    source = ((piece & 3) ^ col_index) * (4 * part) + ((piece >> 2) ^ sub_index) * part + inner
    turn = (column[:, None] == source[None, :]).astype(f32)
    vec = exact(vectors, turn, 1, 0)

    def pad_rows(value):
        shaped = value.reshape(images, L, -1)
        return jnp.pad(shaped, ((0, 0), (0, LP - L), (0, 0))).reshape(images * LP, -1)

    pix_mine = lax.dynamic_index_in_dim(pixels, row_index, 0, keepdims=False)
    pix_give = lax.dynamic_index_in_dim(pixels, 1 - row_index, 0, keepdims=False)
    pix_got = swap(pix_give, "row", 1)
    pix_half = [pad_rows(pix_mine), pad_rows(pix_got)]
    pix_other = pad_rows(pix_give)

    live_group = (patch_mask > 0) & ((jnp.arange(patch_mask.shape[1]) % L) != 0)[None, :]
    count_all = butterfly(jnp.sum(live_group.astype(f32)), ("dp",))
    mask_mine = lax.dynamic_slice(
        patch_mask, (row_index, col_index * images * L), (1, images * L)
    ).reshape(images, L)
    ids_mine = lax.dynamic_slice(class_ids, (row_index, col_index * images), (1, images))[0]
    chosen = ids_mine[:, None] == jnp.arange(class_counts.shape[0])[None, :]
    image_weight = 32.0 / jnp.sum(jnp.where(chosen, class_counts[None, :], 0), axis=1).astype(f32)
    position = jnp.broadcast_to(jnp.arange(LP)[None, :], (images, LP))
    hidden = jnp.pad(mask_mine, ((0, 0), (0, LP - L))) > 0
    first_rows = position == 0
    real_rows = position < L
    live = hidden & (position != 0)
    keep_rows = jnp.where(live, image_weight[:, None], 0.0)
    patch_rows = real_rows & jnp.logical_not(first_rows) & jnp.logical_not(live)
    columns = [first_rows, live, real_rows, keep_rows, patch_rows]
    flags = jnp.stack([c.astype(f32).reshape(-1) for c in columns] + [jnp.zeros((images * LP,), f32)] * 3, axis=1)
    tokens = images * LP

    def activations(*widths):
        return [((tokens, w), bf16) for w in widths]

    weights, values = {}, {}
    qkv_outs = [((tokens, width), f32)] + activations(width, *[sizes["qkv"]] * 2, *[sizes["out"]] * 2)
    full = 2 * tokens * width
    loss_scale = 1.0 / (PATCH * count_all)

    def across_core(value):
        return swap(value, "row", 1)

    def keep_qkv(i, got):
        values["residual", i], values["low_one", i] = got[0], got[1]
        values["qkv", i], values["context", i] = got[2:4], got[4:6]
        values["got_one", i], values["got_context", i] = across_core(got[1]), across_core(got[5])

    def forward_stage(index, pairs):
        layer, odd = divmod(index, 2)
        for entry, pair in zip(plan[cuts[index] : cuts[index + 1]], pairs):
            weights[entry[:2]] = pair
        base = L + 6 + 12 * layer
        if index == 0:
            got = whole_call_smem(
                embed_qkv_body, 1, 9, qkv_outs, "embed_qkv", full * (width + 3 * width)
            )(places, vec, vectors, *pix_half, flags, *weights["ends", 0], *weights["qkv", 0])
            keep_qkv(0, got)
        elif odd:
            outs = [((tokens, width), f32)] + activations(width, *[sizes["up"]] * 2)
            outs += [((tokens, sizes["up"]), f32)] * 2
            got = whole_call_smem(
                lambda *refs: up_body(base, *refs), 1, 9, outs, "out_up", full * 5 * width
            )(
                places, vec, vectors, values["residual", layer], *values["context", layer],
                *weights["out", layer], *weights["up", layer],
            )
            values["mid", layer], values["low_two", layer] = got[0], got[1]
            values["active", layer], values["slope", layer] = got[2:4], got[4:6]
            values["got_two", layer], values["got_active", layer] = across_core(got[1]), across_core(got[3])
        elif layer < layer_count:
            got = whole_call_smem(
                lambda *refs: down_qkv_body(base, *refs), 1, 9, qkv_outs, "down_qkv", full * 7 * width
            )(
                places, vec, vectors, values["mid", layer - 1], *values["active", layer - 1],
                *weights["down", layer - 1], *weights["qkv", layer],
            )
            keep_qkv(layer, got)
        else:
            outs = activations(width, *[sizes["ends"]] * 2) + [((tokens, width), f32)] + activations(width)
            outs += [((8, width), f32), ((8, width), f32), ((8, 128), f32)]
            got = whole_call_smem(
                lambda *refs: down_head_body(base - 12, refs[0], refs[2], refs[3], refs[1], *refs[4:]),
                2, 12, outs, "down_head", full * 6 * width,
            )(
                places, loss_scale.reshape(1), vec, vectors, values["mid", layer - 1],
                *values["active", layer - 1], *weights["down", layer - 1], *weights["ends", 1],
                *pix_half, flags,
            )
            values["low_fin"], values["pred"] = got[0], got[1:3]
            values["grad_res"], values["grad_low"] = got[3], got[4]
            values["wide", "head"], values["flat", "head"], values["loss"] = got[5:]
            values["got_fin"], values["got_pred"] = across_core(got[0]), across_core(got[2])
            values["got_low"] = across_core(got[4])

    count = len(chunks)
    for step in range(count + 3):
        begun = list(values)
        if step < count:
            chunks[step].along()
        if 0 <= step - 1 < count:
            chunks[step - 1].across()
        if 0 <= step - 2 < count:
            chunks[step - 2].diagonal()
        if 0 <= step - 3 < count:
            forward_stage(step - 3, chunks[step - 3].weights())
        if step == count + 2:
            break
        moving = chunks[max(0, step - 2) : step + 1]
        later = chunks[step + 1 :]
        keys = [k for k in values if k in begun or not (isinstance(k, tuple) and k[0][:3] == "got")]
        states, waiting, kept = tie(
            [c.state for c in moving], [c.first for c in later], [values[k] for k in keys]
        )
        values.update(zip(keys, kept))
        for c, s in zip(moving, states):
            c.state = s
        for c, w in zip(later, waiting):
            c.first = w

    flying, done = [], []

    def step_on(value, fresh):
        value, landed, ready = tie(value, [r.got for r in flying], [r.parts for r in fresh])
        for r, got in zip(flying, landed):
            r.got = got
            r.absorb()
        for r, parts in zip(fresh, ready):
            r.parts = parts
        done.extend(r for r in flying if r.stage == 4)
        flying[:] = [r for r in flying if r.stage < 4] + list(fresh)
        for r in flying:
            r.send()
        return value

    wides = {"head": values["wide", "head"]}
    flats = {"head": values["flat", "head"]}
    grad_res, grad_low, got_low = values["grad_res"], values["grad_low"], values["got_low"]
    small = sizes["out"]
    blocks_of = {name: range(sizes[name] // small) for name in sizes}
    big = 2 * small
    groups = []

    def product(way, left, left_got, right, right_got, name, part=None):
        blocks = list(part if part is not None else blocks_of[name])
        block = small
        if len(blocks) % 2 == 0 and blocks[0] % 2 == 0:
            block, blocks = big, list(range(blocks[0] // 2, blocks[0] // 2 + len(blocks) // 2))
        return product_sum(way, left, left_got, right, right_got, block, blocks)

    for i in reversed(range(layer_count)):
        base = L + 6 + 12 * i
        outs = [((tokens, width), f32)] + activations(width, *[sizes["up"]] * 2) + [((8, width), f32)] * 2
        grad_mid, mid_low, hid_a, hid_b, wides["mlp", i], flats["mlp", i] = whole_call(
            lambda *refs: back_mlp_body(base, *refs), outs, "back_mlp", full * 8 * width
        )(
            vec, grad_res, grad_low, *weights["down", i], *values["slope", i], *weights["up", i],
            values["mid", i],
        )
        got_mid, got_hid = across_core(mid_low), across_core(hid_b)
        active = values["active", i]
        first_x = [product("x", grad_low, got_low, active[0], values["got_active", i], "down")]
        names_x = [("down", i)]
        if i == layer_count - 1:
            first_x.append(
                product("x", values["low_fin"], values["got_fin"], values["pred"][0], values["got_pred"], "ends")
            )
            names_x.append(("ends", 1))
        first_y = [product("y", values["low_two", i], values["got_two", i], hid_a, got_hid, "up")]
        group = Reduce(first_x, first_y)
        groups.append((group, names_x + [("up", i)]))
        grad_mid, mid_low, got_mid = step_on((grad_mid, mid_low, got_mid), [group])
        outs = [((tokens, width), f32)] + activations(width, *[sizes["qkv"]] * 2) + [((8, width), f32)] * 2
        grad_res, grad_low, mix_a, mix_b, wides["mix", i], flats["mix", i] = whole_call(
            lambda *refs: back_attend_body(base, *refs), outs, "back_attend", full * 8 * width,
            [pltpu.VMEM((tokens, sizes["out"]), f32)],
        )(
            vec, grad_mid, mid_low, *weights["out", i], *values["qkv", i], *weights["qkv", i],
            values["residual", i],
        )
        got_mix = across_core(mix_b)
        if i > 0:
            got_low = across_core(grad_low)
        else:
            outs = activations(width) + [((LP, width), f32), ((8, width), f32)]
            embed_low, place_sum, wides["embed"] = whole_call(back_embed_body, outs, "back_embed", full)(
                grad_res, flags
            )
            got_embed = across_core(embed_low)
        low_one, got_one = values["low_one", i], values["got_one", i]
        out_args = (mid_low, got_mid, values["context", i][0], values["got_context", i], "out")
        if i > 0:
            first_x = [product("x", low_one, got_one, mix_a, got_mix, "qkv", range(0, 2))]
            first_y = [product("y", low_one, got_one, mix_a, got_mix, "qkv", range(2, 3)), product("y", *out_args)]
            group_names = [("qkv", i), ("out", i)]
        else:
            first_x = [product("x", low_one, got_one, mix_a, got_mix, "qkv")]
            first_y = [
                product("y", *out_args),
                product("y", embed_low, got_embed, pix_half[0], pix_other, "ends"),
            ]
            group_names = [("qkv", i), ("out", i), ("ends", 0)]
        group = Reduce(first_x, first_y)
        groups.append((group, group_names))
        grad_res, grad_low, got_low = step_on((grad_res, grad_low, got_low), [group])

    raw_wide = [place_sum, wides["embed"], wides["head"]]
    raw_flat = [flats["head"]]
    source_wide = list(range(L)) + [LP, LP + 1, LP + 2, LP + 8, LP + 9, -1]
    source_flat = [-1] * (L + 5) + [0]
    rolled = [1] * 8
    for i in range(layer_count):
        at, low = LP + 16 * (i + 1), 8 + 16 * i
        raw_wide += [wides["mlp", i], wides["mix", i]]
        raw_flat += [flats["mlp", i], flats["mix", i]]
        source_wide += [at + 9, at + 10, -1, -1, at + 8, at + 1, at + 2, -1, -1, -1, -1, at]
        source_flat += [-1, -1, low + 8, low + 9, -1, -1, -1, low, low + 1, low + 2, low + 3, -1]
        rolled += [0] * 8 + [1] * 8
    rows_all = -(-vectors.shape[0] // 256) * 256
    spare = [-1] * (rows_all - vectors.shape[0])
    source_wide, source_flat = jnp.array(source_wide + spare), jnp.array(source_flat + spare)
    raw_wide = jnp.concatenate(raw_wide, axis=0)
    raw_flat = jnp.concatenate(raw_flat, axis=0)
    other = jnp.concatenate([raw_flat[:, width // 2 :], raw_flat[:, : width // 2]], axis=1)
    raw_flat = jnp.where(swapped & (jnp.array(rolled)[:, None] == 1), other, raw_flat)
    is_up = (source_flat >= 0) & (source_flat % 16 >= 8) & (source_flat % 16 < 12)
    turned_row = source_flat // 4 * 4 + (source_flat % 4 + 2 * row_index) % 4
    source_flat = jnp.where(is_up, turned_row, source_flat)
    pick_wide = (source_wide[:, None] == jnp.arange(raw_wide.shape[0])[None, :]).astype(f32)
    pick_flat = (source_flat[:, None] == jnp.arange(raw_flat.shape[0])[None, :]).astype(f32)
    grad_vec = exact(exact(pick_wide, raw_wide, 1, 0), turn, 1, 1) + exact(pick_flat, raw_flat, 1, 0)

    def rows_at(value, index, size):
        return lax.dynamic_slice_in_dim(value, index * size, size)

    half_rows, sub_rows, end_rows = rows_all // 2, rows_all // 8, rows_all // 32
    value = rows_at(grad_vec, row_index, half_rows) + across_core(rows_at(grad_vec, 1 - row_index, half_rows))
    value = rows_at(value, sub_index, sub_rows) + sum(
        swap(rows_at(value, sub_index ^ k, sub_rows), "dp", k) for k in (1, 2, 3)
    )
    value = rows_at(value, col_index, end_rows) + sum(
        swap(rows_at(value, col_index ^ k, end_rows), "col", k) for k in (1, 2, 3)
    )
    for mask in bits_of("dp")[2:]:
        value = value + swap(value, "dp", mask)
    vec_square = jnp.sum(value * value)
    value = jnp.concatenate([value] + [swap(value, "col", k) for k in (1, 2, 3)], axis=0)
    value = jnp.concatenate([value] + [swap(value, "dp", k) for k in (1, 2, 3)], axis=0)
    value = jnp.concatenate([value, across_core(value)], axis=0)
    spot = jnp.arange(rows_all)
    native = (
        ((spot // half_rows) ^ row_index) * half_rows
        + (((spot // sub_rows) & 3) ^ sub_index) * sub_rows
        + (((spot // end_rows) & 3) ^ col_index) * end_rows
        + spot % end_rows
    )
    pick = (jnp.arange(vectors.shape[0])[:, None] == native[None, :]).astype(f32)
    vec_sum = exact(pick, value, 1, 0)

    def spread(members):
        value = jnp.concatenate([g.keep for g in members], axis=1)
        exponent = jnp.concatenate([g.exponent for g in members], axis=1)
        payload = lowered(value, exponent)
        return [payload] + [swap(payload, "dp", k) for k in (1, 2, 3)]

    spreads = []
    ready = 0

    def spread_ready(size):
        nonlocal ready
        spreads.append((spread([g for g, _ in groups[ready : ready + size]]), groups[ready : ready + size]))
        ready += size

    marker = grad_res
    while flying:
        marker = step_on(marker, [])
        finished = sum(1 for g, _ in groups if g.stage == 4)
        if ready == 0 and finished >= 2:
            spread_ready(2)
    spread_ready(len(groups) - ready)
    axes = ("row", "dp", "col")
    copies = max(1, data_count // 4)
    square = sum(jnp.sum(g.keep * g.keep) for g, _ in groups) + vec_square
    pair = butterfly(jnp.stack([square / copies, values["loss"][0, 0]]), axes)
    loss_total = pair[1]
    grad_norm = jnp.sqrt(pair[0])
    factor = jnp.minimum(1.0, clip_scale / math.sqrt(total_tokens) / grad_norm)

    pieces, layout, ends_parts = [], [], {}
    for payloads, members in spreads:
        names_in = [name for _, group_names in members for name in group_names]
        spans, at = [], 0
        for name in names_in:
            size = sizes[name[0]]
            spans.append((at, start_of[name], size))
            if name[0] == "ends":
                ends_parts[name[1]] = (len(pieces), at)
            at += size
        for k, payload in enumerate(payloads):
            pieces.append(decoded(payload[:-16], tail_of(payload)))
            layout.append((k, spans))
    per_owner = owner_map.shape[1] // data_count
    slots = lax.dynamic_slice_in_dim(owner_map[0], data_index * per_owner, per_owner)
    edge = part * 4 // BLK
    firsts_of, kinds = [], []
    at = 0
    for i in range(layer_count):
        for name in ("qkv", "out", "up", "down"):
            firsts_of.append(at)
            kinds.append((start_of[name, i], sizes[name] // BLK, name in ("out", "down")))
            at += edge * sizes[name] // BLK
    top = jnp.zeros_like(slots)
    left_at = jnp.zeros_like(slots)
    turned = jnp.zeros_like(slots)
    for begin, (start, across, is_turned) in zip(firsts_of, kinds):
        inside = slots >= begin
        local = slots - begin
        top = jnp.where(inside, local % edge if is_turned else local // across, top)
        left_at = jnp.where(inside, start + BLK * (local // edge if is_turned else local % across), left_at)
        turned = jnp.where(inside, int(is_turned), turned)
    upper = (2 * top) ^ sub_index
    shift = left_at % 128
    info = jnp.stack([upper, (2 * top + 1) ^ sub_index, left_at // 128, (256 - shift) % 256, turned]).astype(jnp.int32)
    raw_grad, raw_left, raw_right, raw_precond, own_weight = shampoo(
        info, tiles_own, pieces, layout, root_left[0], root_right[0]
    )
    block_grad = raw_grad * factor
    square_factor = (1.0 - decay_stat) * factor * factor
    left_next = decay_stat * stat_left[0] + square_factor * raw_left
    right_next = decay_stat * stat_right[0] + square_factor * raw_right
    block_next = own_weight - rate_blocks * (factor * raw_precond + weight_decay * own_weight)

    ends_refs = []
    for end in range(2):
        index, at = ends_parts[end]
        ends_refs += [pieces[index + k][:, at : at + sizes["ends"]] for k in range(4)]
    ends_flat = whole_call_smem(
        ends_body, 1, 8, [((2, 4 * part, sizes["ends"]), f32)], "ends_order", 10**7
    )(places, *ends_refs)[0]
    ends_grad = ends_flat.transpose(0, 2, 1)
    step_value = step_count.astype(f32)
    vector_next, moment_vector, second_vector = adam_update(
        vectors, vec_sum, vector_moment, vector_second, rate_vector, 0.0, factor, step_value
    )
    ends_next, moment_ends, second_ends = adam_update(
        weight_ends.astype(f32),
        ends_grad,
        ends_moment,
        ends_second,
        rate_matrix,
        weight_decay,
        factor,
        step_value,
    )
    return (
        loss_total,
        grad_norm,
        vector_next,
        moment_vector,
        second_vector,
        ends_next,
        moment_ends,
        second_ends,
        block_grad[None],
        left_next[None],
        right_next[None],
        block_next[None],
    )


def solution(mesh):
    grid = P(None, "row", "col")
    slots = P(("row", "col"), "dp", None, None)
    return jax.shard_map(
        shards,
        mesh=mesh,
        in_specs=(
            P(None, ("dp", "col"), "row"),
            P(None, "dp"),
            P(None, "dp"),
            P(),
            P(),
            P(None, "col", "row"),
            grid,
            P(None, "col", "row"),
            grid,
            grid,
            P(),
            P(),
            P(),
            grid,
            grid,
            slots,
            slots,
            slots,
            slots,
            P(("row", "col"), None),
        ),
        out_specs=(P(), P(), P(), P(), P(), grid, grid, grid, slots, slots, slots, slots),
        check_vma=False,
    )
```

```python
import math

import jax
import jax.numpy as jnp
from jax import lax
from jax.experimental import pallas as pl
from jax.experimental.pallas import tpu as pltpu
from jax.sharding import PartitionSpec as P

HD = 64
PATCH = 768
L = 197
LP = 208
BLK = 96

norm_eps = 1e-06
beta_first = 0.9
beta_second = 0.999
adam_eps = 1e-08
decay_stat = 0.5
rate_matrix = 0.02
rate_vector = 0.2
rate_blocks = 0.1
weight_decay = 0.05
clip_scale = 0.25
highest = lax.Precision.HIGHEST
bf16 = jnp.bfloat16
f16 = jnp.float16
f32 = jnp.float32


COST = 16
VMEM = pl.BlockSpec(memory_space=pltpu.VMEM)
SMEM = pl.BlockSpec(memory_space=pltpu.SMEM)


def whole_call(body, outs, name, flops, scratch=()):
    return pl.pallas_call(
        body,
        out_shape=[jax.ShapeDtypeStruct(shape, dtype) for shape, dtype in outs],
        scratch_shapes=list(scratch),
        compiler_params=pltpu.CompilerParams(vmem_limit_bytes=52 * 2**20),
        cost_estimate=pl.CostEstimate(flops=flops // COST, bytes_accessed=2**16, transcendentals=0),
        name=name,
    )


def dot(lhs_mat, rhs_mat, lhs_dim, rhs_dim):
    return lax.dot_general(
        lhs_mat, rhs_mat, (((lhs_dim,), (rhs_dim,)), ((), ())), preferred_element_type=f32
    )


def exact(lhs_mat, rhs_mat, lhs_dim, rhs_dim):
    return lax.dot_general(
        lhs_mat,
        rhs_mat,
        (((lhs_dim,), (rhs_dim,)), ((), ())),
        precision=highest,
        preferred_element_type=f32,
    )


def swap(value, axis, mask):
    size = lax.axis_size(axis)
    return lax.ppermute(value, axis, [(i, i ^ mask) for i in range(size)])


def bits_of(axis):
    return [1 << b for b in range(lax.axis_size(axis).bit_length() - 1)]


def butterfly(value, axes, op=jnp.add):
    for axis in axes:
        for mask in bits_of(axis):
            value = op(value, swap(value, axis, mask))
    return value


def softmax_scores(queries, key_rows):
    scores = dot(queries, key_rows, 1, 1)
    spot = lax.broadcasted_iota(jnp.int32, scores.shape, 1)
    scores = jnp.where(spot < L, scores, -1e30)
    top = jnp.max(scores, axis=1, keepdims=True)
    exponent = jnp.exp(scores - top)
    return exponent / jnp.sum(exponent, axis=1, keepdims=True)


def attend_forward(qkv_ref, ctx_ref):
    rows, wide = qkv_ref.shape
    for image in range(rows // LP):
        span = slice(image * LP, (image + 1) * LP)
        for pair in range(wide // (6 * HD)):
            made = []
            for head in (2 * pair, 2 * pair + 1):
                base = head * 3 * HD
                queries = qkv_ref[span, base : base + HD]
                key_rows = qkv_ref[span, base + HD : base + 2 * HD]
                values = qkv_ref[span, base + 2 * HD : base + 3 * HD]
                attend = softmax_scores(queries, key_rows).astype(bf16)
                made.append(dot(attend, values, 1, 0).astype(bf16))
            ctx_ref[span, pair * 2 * HD : (pair + 1) * 2 * HD] = jnp.concatenate(made, axis=1)


def attend_backward(qkv_ref, grad_ref, out_ref):
    rows, wide = qkv_ref.shape
    for image in range(rows // LP):
        span = slice(image * LP, (image + 1) * LP)
        for pair in range(wide // (6 * HD)):
            made = []
            for head in (2 * pair, 2 * pair + 1):
                base = head * 3 * HD
                queries = qkv_ref[span, base : base + HD]
                key_rows = qkv_ref[span, base + HD : base + 2 * HD]
                values = qkv_ref[span, base + 2 * HD : base + 3 * HD]
                grad = grad_ref[span, head * HD : (head + 1) * HD].astype(bf16)
                attend = softmax_scores(queries, key_rows)
                grad_values = dot(attend.astype(bf16), grad, 0, 0)
                grad_attend = dot(grad, values, 1, 1)
                inner = jnp.sum(grad_attend * attend, axis=1, keepdims=True)
                grad_scores = (attend * (grad_attend - inner)).astype(bf16)
                made.append((dot(grad_scores, key_rows, 1, 0) * 0.125).astype(bf16))
                made.append(dot(grad_scores, queries, 0, 0).astype(bf16))
                made.append(grad_values.astype(bf16))
            out_ref[span, pair * 6 * HD : (pair + 1) * 6 * HD] = jnp.concatenate(made, axis=1)


def normed_of(residual):
    center = residual - jnp.mean(residual, axis=1, keepdims=True)
    inverse = lax.rsqrt(jnp.mean(center * center, axis=1, keepdims=True) + norm_eps)
    return center * inverse, inverse


def norm_backward(grad_normed, residual, gain):
    normed, inverse = normed_of(residual)
    scaled = grad_normed * gain
    mean_one = jnp.mean(scaled, axis=1, keepdims=True)
    mean_two = jnp.mean(scaled * normed, axis=1, keepdims=True)
    grad_in = inverse * (scaled - mean_one - normed * mean_two)
    gain_sum = jnp.sum(grad_normed * normed, axis=0, keepdims=True)
    return grad_in, gain_sum, jnp.sum(grad_normed, axis=0, keepdims=True)


def rows_sum(value):
    return jnp.sum(value.astype(f32), axis=0, keepdims=True)


def put_rows(ref, rows):
    ref[...] = jnp.zeros(ref.shape, f32)
    for i, row in enumerate(rows):
        ref[i : i + 1, :] = row


def own_first(row, core):
    half = row.shape[1] // 2
    return jnp.where(core == 1, jnp.concatenate([row[:, half:], row[:, :half]], axis=1), row)


def qkv_part(base, places, vec, vectors, residual, weights, low_one, qkv, context):
    normed, _ = normed_of(residual)
    low_one[...] = (normed * vec[base : base + 1, :] + vec[base + 1 : base + 2, :]).astype(bf16)
    query_bias = own_first(vectors[base + 2 : base + 3, :], places[1])
    value_bias = own_first(vectors[base + 3 : base + 4, :], places[1])
    for half in range(2):
        heads = qkv[half].shape[1] // (3 * HD)
        parts = []
        for head in range(heads):
            at = (half * heads + head) * HD
            parts += [query_bias[:, at : at + HD], jnp.zeros((1, HD), f32), value_bias[:, at : at + HD]]
        bias = jnp.concatenate(parts, axis=1)
        kind = (lax.broadcasted_iota(jnp.int32, bias.shape, 1) // HD) % 3
        factor = jnp.where(kind == 0, 0.125, 1.0)
        step = 6 * HD
        for at in range(0, heads * 3 * HD, step):
            span = slice(at, at + step)
            mixed = dot(low_one[...], weights[half][:, span], 1, 0)
            qkv[half][:, span] = ((mixed + bias[:, span]) * factor[:, span]).astype(bf16)
        attend_forward(qkv[half], context[half])


def give(ref, parts):
    at = 0
    for part in parts:
        ref[:, at : at + part.shape[1]] = part[...]
        at += part.shape[1]


def embed_qkv_body(
    places, vec, vectors, pix_a, pix_b, flags, ends_a, ends_b, qkv_a, qkv_b,
    residual, low_one, out_a, out_b, ctx_a, ctx_b, gift,
):
    embedded = dot(pix_a[...], ends_a[...], 1, 1) + dot(pix_b[...], ends_b[...], 1, 1)
    embedded = embedded + vec[L + 2 : L + 3, :]
    spots = vec[0:LP, :]
    spots = jnp.concatenate([spots] * (embedded.shape[0] // LP), axis=0)
    picked = jnp.where(flags[:, 1:2] > 0, vec[L + 1 : L + 2, :], embedded)
    picked = jnp.where(flags[:, 0:1] > 0, vec[L : L + 1, :], picked)
    residual[...] = jnp.where(flags[:, 2:3] > 0, picked + spots, 0.0)
    qkv_part(
        L + 6, places, vec, vectors, residual[...], (qkv_a, qkv_b), low_one, (out_a, out_b), (ctx_a, ctx_b)
    )
    give(gift, (low_one, ctx_b))


def up_body(
    base, places, vec, vectors, residual, ctx_a, ctx_b, out_a, out_b, up_a, up_b,
    mid, low_two, act_a, act_b, slope_a, slope_b, gift,
):
    branch = dot(ctx_a[...], out_a[...], 1, 1) + dot(ctx_b[...], out_b[...], 1, 1)
    mid[...] = residual[...] + (branch + vec[base + 4 : base + 5, :])
    normed, _ = normed_of(mid[...])
    low_two[...] = (normed * vec[base + 5 : base + 6, :] + vec[base + 6 : base + 7, :]).astype(bf16)
    wide = vec.shape[1]
    for half, (weight, active, slope) in enumerate(((up_a, act_a, slope_a), (up_b, act_b, slope_b))):
        for k in range(weight.shape[1] // wide):
            row = base + 7 + (weight.shape[1] // wide) * jnp.bitwise_xor(places[1], half) + k
            span = slice(k * wide, (k + 1) * wide)
            pre = dot(low_two[...], weight[:, span], 1, 0) + vectors[pl.ds(row, 1), :]
            phi = 0.5 * (1.0 + lax.erf(pre * math.sqrt(0.5)))
            active[:, span] = (pre * phi).astype(bf16)
            slope[:, span] = phi + pre * (jnp.exp(-0.5 * pre * pre) * (1.0 / math.sqrt(2.0 * math.pi)))
    give(gift, (low_two, act_b))


def down_qkv_body(
    base, places, vec, vectors, mid, act_a, act_b, down_a, down_b, qkv_a, qkv_b,
    residual, low_one, out_a, out_b, ctx_a, ctx_b, gift,
):
    branch = dot(act_a[...], down_a[...], 1, 1) + dot(act_b[...], down_b[...], 1, 1)
    residual[...] = mid[...] + (branch + vec[base - 1 : base, :])
    qkv_part(
        base, places, vec, vectors, residual[...], (qkv_a, qkv_b), low_one, (out_a, out_b), (ctx_a, ctx_b)
    )
    give(gift, (low_one, ctx_b))


def down_head_body(
    base, places, vec, vectors, scale, mid, act_a, act_b, down_a, down_b, ends_a, ends_b, pix_a, pix_b, flags,
    low_fin, pred_a, pred_b, grad_res, grad_low, wide, flat, loss, gift,
):
    branch = dot(act_a[...], down_a[...], 1, 1) + dot(act_b[...], down_b[...], 1, 1)
    residual = mid[...] + (branch + vec[base + 11 : base + 12, :])
    normed, _ = normed_of(residual)
    low_fin[...] = (normed * vec[L + 3 : L + 4, :] + vec[L + 4 : L + 5, :]).astype(bf16)
    bias = own_first(vectors[L + 5 : L + 6, :], places[1])
    keep = flags[:, 3:4]
    total = jnp.zeros((1, 1), f32)
    sums = []
    for half, (ends, pix, pred) in enumerate(((ends_a, pix_a, pred_a), (ends_b, pix_b, pred_b))):
        span = ends.shape[1]
        error = dot(low_fin[...], ends[...], 1, 0) + bias[:, half * span : (half + 1) * span]
        error = error - pix[...].astype(f32)
        total = total + jnp.sum(jnp.sum(keep * error * error, axis=1, keepdims=True), axis=0, keepdims=True)
        pred[...] = (2.0 * scale[0] * keep * error).astype(bf16)
        sums.append(rows_sum(pred[...]))
    loss[...] = jnp.broadcast_to(total * scale[0], loss.shape)
    grad_fin = dot(pred_a[...], ends_a[...], 1, 1) + dot(pred_b[...], ends_b[...], 1, 1)
    grad, gain_sum, shift_sum = norm_backward(grad_fin, residual, vec[L + 3 : L + 4, :])
    grad_res[...] = grad
    grad_low[...] = grad.astype(bf16)
    put_rows(wide, [gain_sum, shift_sum])
    put_rows(flat, [jnp.concatenate(sums, axis=1)])
    give(gift, (low_fin, grad_low, pred_b))


def back_mlp_body(
    base, vec, grad_res, grad_low, down_a, down_b, slope_a, slope_b, up_a, up_b, mid,
    grad_mid, mid_low, hid_a, hid_b, wide, flat, gift,
):
    span = vec.shape[1]
    sums = []
    total = None
    for down, slope, up, hid in ((down_a, slope_a, up_a, hid_a), (down_b, slope_b, up_b, hid_b)):
        for at in range(0, down.shape[1], span):
            cols = slice(at, at + span)
            hid[:, cols] = (dot(grad_low[...], down[:, cols], 1, 0) * slope[:, cols]).astype(bf16)
            sums.append(rows_sum(hid[:, cols]))
        part = dot(hid[...], up[...], 1, 1)
        total = part if total is None else total + part
    grad, gain_sum, shift_sum = norm_backward(total, mid[...], vec[base + 5 : base + 6, :])
    grad = grad_res[...] + grad
    grad_mid[...] = grad
    mid_low[...] = grad.astype(bf16)
    put_rows(wide, [rows_sum(grad_low[...]), gain_sum, shift_sum])
    put_rows(flat, sums)
    give(gift, (mid_low, hid_b))


def back_attend_body(
    base, vec, grad_mid, mid_low, out_a, out_b, qkv_a, qkv_b, wqkv_a, wqkv_b, residual,
    grad_res, grad_low, mix_a, mix_b, wide, flat, gift, ctx,
):
    total = None
    query_sums, value_sums = [], []
    for out, qkv, wqkv, mix in ((out_a, qkv_a, wqkv_a, mix_a), (out_b, qkv_b, wqkv_b, mix_b)):
        ctx[...] = dot(mid_low[...], out[...], 1, 0)
        attend_backward(qkv, ctx, mix)
        part = dot(mix[...], wqkv[...], 1, 1)
        total = part if total is None else total + part
        sums = rows_sum(mix[...])
        for head in range(mix.shape[1] // (3 * HD)):
            at = head * 3 * HD
            query_sums.append(sums[:, at : at + HD])
            value_sums.append(sums[:, at + 2 * HD : at + 3 * HD])
    grad, gain_sum, shift_sum = norm_backward(total, residual[...], vec[base : base + 1, :])
    grad = grad_mid[...] + grad
    grad_res[...] = grad
    grad_low[...] = grad.astype(bf16)
    put_rows(wide, [rows_sum(mid_low[...]), gain_sum, shift_sum])
    put_rows(flat, [jnp.concatenate(query_sums, axis=1), jnp.concatenate(value_sums, axis=1)])
    give(gift, (grad_low, mix_b))


def back_embed_body(grad_res, flags, grad_low, place, wide):
    grad = grad_res[...]
    low = jnp.where(flags[:, 4:5] > 0, grad, 0.0).astype(bf16)
    grad_low[...] = low
    total = grad[0:LP]
    for image in range(1, grad.shape[0] // LP):
        total = total + grad[image * LP : (image + 1) * LP]
    place[...] = total
    class_sum = rows_sum(jnp.where(flags[:, 0:1] > 0, grad, 0.0))
    mask_sum = rows_sum(jnp.where(flags[:, 1:2] > 0, grad, 0.0))
    put_rows(wide, [class_sum, mask_sum, rows_sum(low)])


def tie(*trees):
    leaves, shape = jax.tree.flatten(trees)
    return jax.tree.unflatten(shape, lax.optimization_barrier(leaves))


def prepare_body(plan, cuts, places, qkv, out, up, down, ends, *rest):
    outs, turned = rest[:-1], rest[-1]
    whole, owns, firsts = outs[0], outs[1::2], outs[2::2]
    sub_at = places[0]
    part = whole.shape[1]
    refs = {"qkv": qkv, "out": out, "up": up, "down": down, "ends": ends}
    for chunk in range(len(cuts) - 1):
        begin = plan[cuts[chunk]][2]
        for name, layer, start, width in plan[cuts[chunk] : cuts[chunk + 1]]:
            ref = refs[name]
            plain = name in ("qkv", "up")
            if not plain:
                turned[:, :width] = ref[layer].T.astype(f32)
            for k in range(4):
                rows = pl.ds(pl.multiple_of(jnp.bitwise_xor(sub_at, k) * part, 16), part)
                piece = ref[layer, rows, :] if plain else turned[rows, :width].astype(bf16)
                whole[k, :, start : start + width] = piece
                owns[chunk][k, :, start - begin : start - begin + width] = piece
                if k == 0:
                    firsts[chunk][:, start - begin : start - begin + width] = piece


def prepare_tiles(plan, cuts, places, qkv, out, up, down, ends):
    height = qkv.shape[1]
    part = height // 4
    outs = [((4, part, plan[-1][2] + plan[-1][3]), bf16)]
    for j, k in zip(cuts[:-1], cuts[1:]):
        width = plan[k - 1][2] + plan[k - 1][3] - plan[j][2]
        outs += [((4, part, width), bf16), ((part, width), bf16)]
    widest = max(entry[3] for entry in plan)
    got = whole_call_smem(
        lambda *refs: prepare_body(plan, cuts, *refs), 1, 5, outs, "prepare_tiles", 10**8,
        [pltpu.VMEM((height, widest), f32)],
    )(places, qkv, out, up, down, ends)
    return got[0], got[1::2], got[2::2]


def whole_call_smem(body, scalars, arrays, outs, name, flops, scratch=()):
    return pl.pallas_call(
        body,
        in_specs=[SMEM] * scalars + [VMEM] * arrays,
        out_specs=[VMEM] * len(outs),
        out_shape=[jax.ShapeDtypeStruct(shape, dtype) for shape, dtype in outs],
        scratch_shapes=list(scratch),
        compiler_params=pltpu.CompilerParams(vmem_limit_bytes=52 * 2**20),
        cost_estimate=pl.CostEstimate(flops=flops // COST, bytes_accessed=2**16, transcendentals=0),
        name=name,
    )


def assemble_body(widths, half, at_left, at_right, own, stack, from_x, from_y, in_y, in_x, *outs):
    part = own.shape[1]
    start = 0
    for out, width in zip(outs, widths):
        stop = start + width
        for k in range(4):
            out[4 * k * part : (4 * k + 1) * part, :] = own[k, :, start:stop]
            rows = slice((4 * k + 1) * part, 4 * (k + 1) * part)
            if k < 3:
                out[rows, :] = (stack, from_x, from_y)[k][:, start:stop]
                continue
            middle = min(max(half, start), stop)
            if middle > start:
                out[rows, : middle - start] = in_y[:, at_left + start : at_left + middle]
            if stop > middle:
                out[rows, middle - start :] = in_x[:, at_right + middle - half : at_right + stop - half]
        start = stop


class Gather:
    def __init__(self, own, first, widths):
        self.own, self.first, self.widths = own, first, widths
        self.total = sum(widths)
        self.half = self.total // 256 * 128
        self.state = []

    def along(self):
        self.state = [jnp.concatenate([swap(self.first, "col", k) for k in (1, 2, 3)], axis=0)]

    @staticmethod
    def across(new, old):
        out_x, out_y = [], []
        if new is not None:
            out_x.append(new.state[0])
            out_y.append(new.state[0])
        if old is not None:
            out_y.append(old.state[1][:, : old.half])
            out_x.append(old.state[2][:, old.half : old.total])
        got_x = swap(jnp.concatenate(out_x, axis=1) if len(out_x) > 1 else out_x[0], "dp", 1)
        got_y = swap(jnp.concatenate(out_y, axis=1) if len(out_y) > 1 else out_y[0], "dp", 2)
        if new is not None:
            new.state += [got_x, got_y]
        if old is not None:
            old.at = 0 if new is None else new.total
            old.state += [got_y, got_x]

    def weights(self):
        height = 16 * self.own.shape[1]
        mine = whole_call(
            lambda *refs: assemble_body(self.widths, self.half, self.at, self.at, *refs),
            [((height, w), bf16) for w in self.widths],
            "assemble",
            10**8,
        )(self.own, *self.state)
        return [(w, swap(w, "row", 1)) for w in mine]


def row_runs(name, part):
    runs = []
    for bit in range(2):
        rows = []
        for other in range(2):
            sub = 2 * other + bit if name == "x" else 2 * bit + other
            rows += [((4 * sub + 2 * high + low) * part, part) for low in range(2) for high in range(2)]
        runs.append(rows)
    return runs


def product_body(runs, left, left_got, right, right_got, keep, send, power, total):
    total[...] = dot(left[...], right[...], 0, 0) + dot(left_got[...], right_got[...], 0, 0)
    top = jnp.max(jnp.abs(total[...]), axis=0, keepdims=True)
    exponent = jnp.clip(jnp.ceil(jnp.log2(top)) + 1.0, -100.0, 120.0)
    scale = jnp.exp2(14.0 - exponent)
    power[...] = exponent
    for out, spans, factor in ((keep, runs[0], None), (send, runs[1], scale)):
        at = 0
        for start, size in spans:
            piece = total[start : start + size, :]
            out[at : at + size, :] = piece if factor is None else piece * factor
            at += size
    send[at:, :] = jnp.broadcast_to(exponent, (16, exponent.shape[1]))


def product_sum(name, left, left_got, left_at, right, right_got, right_at, block, blocks):
    rows, height = left.shape
    width = block * len(blocks)
    first = blocks[0]
    runs = row_runs(name, height // 16)
    whole = pl.BlockSpec((rows, height), lambda i: (0, 0))
    whole_got = pl.BlockSpec((rows, height), lambda i: (0, left_at // height))
    part = pl.BlockSpec((rows, block), lambda i: (0, i + first))
    part_got = pl.BlockSpec((rows, block), lambda i: (0, i + first + right_at // block))
    half = pl.BlockSpec((height // 2, block), lambda i: (0, i))
    return pl.pallas_call(
        lambda *refs: product_body(runs, *refs),
        grid=(len(blocks),),
        in_specs=[whole, whole_got, part, part_got],
        out_specs=[
            half,
            pl.BlockSpec((height // 2 + 16, block), lambda i: (0, i)),
            pl.BlockSpec((1, block), lambda i: (0, i)),
        ],
        out_shape=[
            jax.ShapeDtypeStruct((height // 2, width), f32),
            jax.ShapeDtypeStruct((height // 2 + 16, width), f32),
            jax.ShapeDtypeStruct((1, width), f32),
        ],
        scratch_shapes=[pltpu.VMEM((height, block), f32)],
        compiler_params=pltpu.CompilerParams(vmem_limit_bytes=32 * 2**20),
        cost_estimate=pl.CostEstimate(
            flops=4 * rows * height * width // COST, bytes_accessed=2**16, transcendentals=0
        ),
        name="product_sum",
    )(left, left_got, right, right_got)


def lowered(rows, exponent):
    tail = jnp.broadcast_to(exponent, (16, exponent.shape[1]))
    return jnp.concatenate([rows * jnp.exp2(14.0 - exponent), tail], axis=0).astype(f16)


def tail_of(payload):
    return jnp.max(payload[-16:].astype(f32), axis=0, keepdims=True)


def decoded(rows, exponent):
    return rows.astype(f32) * jnp.exp2(exponent - 14.0)


class Reduce:
    def __init__(self, first_x, first_y):
        self.parts = []
        for products in (first_x, first_y):
            keep, send, exponent = (jnp.concatenate(list(p), axis=1) for p in zip(*products))
            self.parts.append([keep, send.astype(f16), exponent])
        self.stage = 0

    def send(self):
        ways = ((("dp", 1), ("dp", 2)), (("dp", 2), ("dp", 1)), (("col", 1),), (("col", 2),))[self.stage]
        self.got = [swap(part[1], axis, mask) for part, (axis, mask) in zip(self.parts, ways)]

    def absorb(self):
        made = []
        for (keep, _, exponent), got in zip(self.parts, self.got):
            theirs = tail_of(got)
            after = jnp.maximum(exponent, theirs) + 1.0
            if self.stage == 3:
                made.append([keep + decoded(got[:-16], theirs), None, after])
                continue
            half = keep.shape[0] // 2
            stay = keep[:half] + decoded(got[:half], theirs)
            leave = keep[half:] + decoded(got[half : 2 * half], theirs)
            made.append([stay, leave, after])
        if self.stage == 1:
            made = [[jnp.concatenate(list(p), axis=1) for p in zip(*made)]]
        self.stage += 1
        if self.stage < 4:
            self.parts = [[stay, lowered(leave, after), after] for stay, leave, after in made]
            return
        keep, _, after = made[0]
        for mask in bits_of("dp")[2:]:
            keep = keep + swap(keep, "dp", mask)
            after = after + 1.0
        self.parts = []
        self.keep, self.exponent = keep, after


def split(value):
    high = value.astype(bf16)
    return high, (value - high.astype(f32)).astype(bf16)


def close(lhs, rhs, lhs_dim, rhs_dim):
    small = dot(lhs[0], rhs[1], lhs_dim, rhs_dim) + dot(lhs[1], rhs[0], lhs_dim, rhs_dim)
    return dot(lhs[0], rhs[0], lhs_dim, rhs_dim) + small


def shampoo_body(
    group, layout, info, weight, *rest
):
    pieces, (rl, rr, grad_out, left, right, precond, weight_out), grads = rest[:-8], rest[-8:-1], rest[-1]
    step = pl.program_id(0)

    @pl.when(step == 0)
    def _():
        for ref, (sub, spans) in zip(pieces, layout):
            for source, target, size in spans:
                grads[sub, :, target : target + size] = ref[:, source : source + size]

    window = 2 * 128

    def block_of(ref, slot):
        start = pl.multiple_of(info[2, slot] * 128, 128)
        tops = [ref[info[k, slot], :, pl.ds(start, window)].astype(f32) for k in range(2)]
        both = jnp.concatenate(tops, axis=0)
        both = pltpu.roll(both, info[3, slot], 1)[:, :BLK]
        return jnp.where(info[4, slot] == 1, both.T, both)

    for j in range(group):
        slot = step * group + j
        g = block_of(grads, slot)
        grad_out[j] = g
        weight_out[j] = block_of(weight, slot)
        both = split(g)
        left[j] = close(both, both, 1, 1)
        right[j] = close(both, both, 0, 0)
        inner = close(both, split(rr[j]), 1, 0)
        precond[j] = close(split(rl[j]), split(inner), 1, 0)


def shampoo(info, weight, pieces, layout, root_left, root_right):
    count = root_left.shape[0]
    group = next(g for g in (8, 6, 4, 3, 2, 1) if count % g == 0)
    plain = pl.BlockSpec((group, BLK, BLK), lambda i: (i, 0, 0))
    return pl.pallas_call(
        lambda *refs: shampoo_body(group, layout, *refs),
        grid=(count // group,),
        in_specs=[SMEM] + [VMEM] * (1 + len(pieces)) + [plain] * 2,
        out_specs=[plain] * 5,
        out_shape=[jax.ShapeDtypeStruct((count, BLK, BLK), f32)] * 5,
        scratch_shapes=[pltpu.VMEM(weight.shape, f32)],
        compiler_params=pltpu.CompilerParams(vmem_limit_bytes=52 * 2**20),
        cost_estimate=pl.CostEstimate(
            flops=count * 48 * BLK**3 // COST, bytes_accessed=2**16, transcendentals=0
        ),
        name="shampoo",
    )(info, weight, *pieces, root_left, root_right)


def ends_body(places, *refs):
    out = refs[-1]
    part = refs[0].shape[0]
    for end in range(2):
        for k in range(4):
            sub = jnp.bitwise_xor(places[0], k)
            out[end, pl.ds(pl.multiple_of(sub * part, 8), part), :] = refs[4 * end + k][...]


def adam_update(weight, gradient, moment, second, rate, decay, factor, step_value):
    clipped = gradient * factor
    moment_new = beta_first * moment + (1.0 - beta_first) * clipped
    second_new = beta_second * second + (1.0 - beta_second) * clipped * clipped
    corr_first = 1.0 - jnp.power(beta_first, step_value)
    corr_second = 1.0 - jnp.power(beta_second, step_value)
    stride = moment_new / corr_first / (jnp.sqrt(second_new / corr_second) + adam_eps)
    return (weight - rate * (stride + decay * weight), moment_new, second_new)


def shards(
    pixels,
    patch_mask,
    class_ids,
    class_counts,
    step_count,
    weight_qkv,
    weight_out,
    weight_up,
    weight_down,
    weight_ends,
    vectors,
    vector_moment,
    vector_second,
    ends_moment,
    ends_second,
    stat_left,
    stat_right,
    root_left,
    root_right,
    owner_map,
):
    data_count = lax.axis_size("dp")
    row_index = lax.axis_index("row")
    col_index = lax.axis_index("col")
    data_index = lax.axis_index("dp")
    sub_index = data_index & 3
    layer_count = weight_qkv.shape[0]
    width = vectors.shape[1]
    images = pixels.shape[1] // L
    total_tokens = pixels.shape[0] * pixels.shape[1] * lax.axis_size("col") * data_count
    places = jnp.stack([sub_index, row_index]).astype(jnp.int32)
    swapped = row_index == 1

    names = [("ends", 0)]
    for i in range(layer_count):
        names += [("qkv", i), ("out", i), ("up", i), ("down", i)]
    names.append(("ends", 1))
    sizes = {
        "qkv": weight_qkv.shape[2],
        "out": weight_out.shape[1],
        "up": weight_up.shape[2],
        "down": weight_down.shape[1],
        "ends": weight_ends.shape[1],
    }
    plan, at = [], 0
    for name, i in names:
        plan.append((name, i, at, sizes[name]))
        at += sizes[name]
    start_of = {entry[:2]: entry[2] for entry in plan}
    stage_cuts = [0]
    for i in range(layer_count):
        stage_cuts += [2 + 4 * i, 4 + 4 * i]
    stage_cuts.append(len(plan))
    last = len(stage_cuts) - 1
    stages_of = [[0, 1]] + [[k] for k in range(2, last - 2)] + [[last - 2, last - 1]]
    cuts = [stage_cuts[stages[0]] for stages in stages_of] + [len(plan)]
    tiles_own, owns, firsts = prepare_tiles(
        plan, cuts, places, weight_qkv, weight_out, weight_up, weight_down, weight_ends
    )
    chunks = [
        Gather(own, first, [entry[3] for entry in plan[j:k]])
        for own, first, j, k in zip(owns, firsts, cuts[:-1], cuts[1:])
    ]

    part = weight_qkv.shape[1] // 4
    column = jnp.arange(width)
    piece, inner = column // part, column % part
    source = ((piece & 3) ^ col_index) * (4 * part) + ((piece >> 2) ^ sub_index) * part + inner
    turn = (column[:, None] == source[None, :]).astype(f32)
    vec = exact(vectors, turn, 1, 0)

    def pad_rows(value):
        shaped = value.reshape(images, L, -1)
        return jnp.pad(shaped, ((0, 0), (0, LP - L), (0, 0))).reshape(images * LP, -1)

    pix_mine = lax.dynamic_index_in_dim(pixels, row_index, 0, keepdims=False)
    pix_give = lax.dynamic_index_in_dim(pixels, 1 - row_index, 0, keepdims=False)
    pix_got = swap(pix_give, "row", 1)
    pix_half = [pad_rows(pix_mine), pad_rows(pix_got)]
    pix_other = pad_rows(pix_give)

    live_group = (patch_mask > 0) & ((jnp.arange(patch_mask.shape[1]) % L) != 0)[None, :]
    count_all = butterfly(jnp.sum(live_group.astype(f32)), ("dp",))
    mask_mine = lax.dynamic_slice(
        patch_mask, (row_index, col_index * images * L), (1, images * L)
    ).reshape(images, L)
    ids_mine = lax.dynamic_slice(class_ids, (row_index, col_index * images), (1, images))[0]
    chosen = ids_mine[:, None] == jnp.arange(class_counts.shape[0])[None, :]
    image_weight = 32.0 / jnp.sum(jnp.where(chosen, class_counts[None, :], 0), axis=1).astype(f32)
    position = jnp.broadcast_to(jnp.arange(LP)[None, :], (images, LP))
    hidden = jnp.pad(mask_mine, ((0, 0), (0, LP - L))) > 0
    first_rows = position == 0
    real_rows = position < L
    live = hidden & (position != 0)
    keep_rows = jnp.where(live, image_weight[:, None], 0.0)
    patch_rows = real_rows & jnp.logical_not(first_rows) & jnp.logical_not(live)
    columns = [first_rows, live, real_rows, keep_rows, patch_rows]
    flags = jnp.stack([c.astype(f32).reshape(-1) for c in columns] + [jnp.zeros((images * LP,), f32)] * 3, axis=1)
    tokens = images * LP

    per_owner = owner_map.shape[1] // data_count
    slots = lax.dynamic_slice_in_dim(owner_map[0], data_index * per_owner, per_owner)
    edge = part * 4 // BLK
    firsts_of, kinds = [], []
    at = 0
    for i in range(layer_count):
        for name in ("qkv", "out", "up", "down"):
            firsts_of.append(at)
            kinds.append((start_of[name, i], sizes[name] // BLK, name in ("out", "down")))
            at += edge * sizes[name] // BLK
    top = jnp.zeros_like(slots)
    left_at = jnp.zeros_like(slots)
    turned = jnp.zeros_like(slots)
    for begin, (start, across, is_turned) in zip(firsts_of, kinds):
        inside = slots >= begin
        local = slots - begin
        top = jnp.where(inside, local % edge if is_turned else local // across, top)
        left_at = jnp.where(inside, start + BLK * (local // edge if is_turned else local % across), left_at)
        turned = jnp.where(inside, int(is_turned), turned)
    upper = (2 * top) ^ sub_index
    shift = left_at % 128
    info = jnp.stack([upper, (2 * top + 1) ^ sub_index, left_at // 128, (256 - shift) % 256, turned]).astype(jnp.int32)

    def activations(*widths):
        return [((tokens, w), bf16) for w in widths]

    weights, values = {}, {}
    qkv_outs = [((tokens, width), f32)] + activations(
        width, *[sizes["qkv"]] * 2, *[sizes["out"]] * 2, width + sizes["out"]
    )
    full = 2 * tokens * width
    loss_scale = 1.0 / (PATCH * count_all)

    def across_core(value):
        return swap(value, "row", 1)

    def keep_qkv(i, got):
        values["residual", i], values["low_one", i] = got[0], got[1]
        values["qkv", i], values["context", i] = got[2:4], got[4:6]
        values["got_qkv", i] = across_core(got[6])

    def forward_stage(index):
        layer, odd = divmod(index, 2)
        base = L + 6 + 12 * layer
        if index == 0:
            got = whole_call_smem(
                embed_qkv_body, 1, 9, qkv_outs, "embed_qkv", full * (width + 3 * width)
            )(places, vec, vectors, *pix_half, flags, *weights["ends", 0], *weights["qkv", 0])
            keep_qkv(0, got)
        elif odd:
            outs = [((tokens, width), f32)] + activations(width, *[sizes["up"]] * 2)
            outs += [((tokens, sizes["up"]), f32)] * 2 + activations(width + sizes["up"])
            got = whole_call_smem(
                lambda *refs: up_body(base, *refs), 1, 9, outs, "out_up", full * 5 * width
            )(
                places, vec, vectors, values["residual", layer], *values["context", layer],
                *weights["out", layer], *weights["up", layer],
            )
            values["mid", layer], values["low_two", layer] = got[0], got[1]
            values["active", layer], values["slope", layer] = got[2:4], got[4:6]
            values["got_up", layer] = across_core(got[6])
        elif layer < layer_count:
            got = whole_call_smem(
                lambda *refs: down_qkv_body(base, *refs), 1, 9, qkv_outs, "down_qkv", full * 7 * width
            )(
                places, vec, vectors, values["mid", layer - 1], *values["active", layer - 1],
                *weights["down", layer - 1], *weights["qkv", layer],
            )
            keep_qkv(layer, got)
        else:
            outs = activations(width, *[sizes["ends"]] * 2) + [((tokens, width), f32)] + activations(width)
            outs += [((8, width), f32), ((8, width), f32), ((8, 128), f32)]
            outs += activations(2 * width + sizes["ends"])
            got = whole_call_smem(
                lambda *refs: down_head_body(base - 12, refs[0], refs[2], refs[3], refs[1], *refs[4:]),
                2, 12, outs, "down_head", full * 6 * width,
            )(
                places, loss_scale.reshape(1), vec, vectors, values["mid", layer - 1],
                *values["active", layer - 1], *weights["down", layer - 1], *weights["ends", 1],
                *pix_half, flags,
            )
            values["low_fin"], values["pred"] = got[0], got[1:3]
            values["grad_res"], values["grad_low"] = got[3], got[4]
            values["wide", "head"], values["flat", "head"], values["loss"] = got[5:8]
            values["got_head"] = across_core(got[8])

    count = len(chunks)
    for step in range(count + 3):
        begun = list(values)
        if step < count:
            chunks[step].along()
        new = chunks[step - 1] if 0 <= step - 1 < count else None
        old = chunks[step - 2] if 0 <= step - 2 < count else None
        if new is not None or old is not None:
            Gather.across(new, old)
        if 0 <= step - 3 < count:
            pairs = chunks[step - 3].weights()
            for entry, pair in zip(plan[cuts[step - 3] : cuts[step - 2]], pairs):
                weights[entry[:2]] = pair
            for stage in stages_of[step - 3]:
                forward_stage(stage)
        if step == count + 2:
            break
        moving = chunks[max(0, step - 2) : step + 1]
        later = chunks[step + 1 :]
        if step == 0:
            setup = (vec, flags, pix_half, pix_other, loss_scale, info, turn)
            chunks[0].state, setup = tie(chunks[0].state, setup)
            vec, flags, pix_half, pix_other, loss_scale, info, turn = setup
        keys = [k for k in values if k in begun or not (isinstance(k, tuple) and k[0][:3] == "got")]
        states, waiting, kept = tie(
            [c.state for c in moving], [c.first for c in later], [values[k] for k in keys]
        )
        values.update(zip(keys, kept))
        for c, s in zip(moving, states):
            c.state = s
        for c, w in zip(later, waiting):
            c.first = w

    flying, done = [], []

    spreads, groups = [], []
    ready = 0

    def spread(members):
        value = jnp.concatenate([g.keep for g in members], axis=1)
        exponent = jnp.concatenate([g.exponent for g in members], axis=1)
        payload = lowered(value, exponent)
        return [payload] + [swap(payload, "dp", k) for k in (1, 2, 3)]

    def step_on(value, fresh):
        nonlocal ready
        value, landed, parts_in = tie(value, [r.got for r in flying], [r.parts for r in fresh])
        for r, got in zip(flying, landed):
            r.got = got
            r.absorb()
        for r, parts in zip(fresh, parts_in):
            r.parts = parts
        done.extend(r for r in flying if r.stage == 4)
        flying[:] = [r for r in flying if r.stage < 4] + list(fresh)
        for r in flying:
            r.send()
        stop = sum(1 for g, _ in groups if g.stage == 4)
        if stop > ready and len(groups) == 2 * layer_count:
            spreads.append([spread([g for g, _ in groups[ready:stop]]), groups[ready:stop]])
            ready = stop
        return value

    wides = {"head": values["wide", "head"]}
    flats = {"head": values["flat", "head"]}
    grad_res, grad_low = values["grad_res"], values["grad_low"]
    got_low, low_at = values["got_head"], width
    small = sizes["out"]
    blocks_of = {name: range(sizes[name] // small) for name in sizes}
    big = 2 * small

    def product(way, left, left_got, left_at, right, right_got, right_at, name, part=None):
        blocks = list(part if part is not None else blocks_of[name])
        block = small
        if len(blocks) % 2 == 0 and blocks[0] % 2 == 0 and right_at % big == 0:
            block, blocks = big, list(range(blocks[0] // 2, blocks[0] // 2 + len(blocks) // 2))
        return product_sum(way, left, left_got, left_at, right, right_got, right_at, block, blocks)

    for i in reversed(range(layer_count)):
        base = L + 6 + 12 * i
        outs = [((tokens, width), f32)] + activations(width, *[sizes["up"]] * 2) + [((8, width), f32)] * 2
        outs += activations(width + sizes["up"])
        got = whole_call(lambda *refs: back_mlp_body(base, *refs), outs, "back_mlp", full * 8 * width)(
            vec, grad_res, grad_low, *weights["down", i], *values["slope", i], *weights["up", i],
            values["mid", i],
        )
        got, got_low = step_on((got, got_low), [])
        grad_mid, mid_low, hid_a, hid_b, wides["mlp", i], flats["mlp", i], gift = got
        got_mid = across_core(gift)
        active = values["active", i]
        first_x = [product("x", grad_low, got_low, low_at, active[0], values["got_up", i], width, "down")]
        names_x = [("down", i)]
        if i == layer_count - 1:
            head = values["got_head"]
            first_x.append(
                product("x", values["low_fin"], head, 0, values["pred"][0], head, 2 * width, "ends")
            )
            names_x.append(("ends", 1))
        first_y = [product("y", values["low_two", i], values["got_up", i], 0, hid_a, got_mid, width, "up")]
        group = Reduce(first_x, first_y)
        groups.append((group, names_x + [("up", i)]))
        grad_mid, mid_low, got_mid = step_on((grad_mid, mid_low, got_mid), [group])
        outs = [((tokens, width), f32)] + activations(width, *[sizes["qkv"]] * 2) + [((8, width), f32)] * 2
        outs += activations(width + sizes["qkv"])
        got = whole_call(
            lambda *refs: back_attend_body(base, *refs), outs, "back_attend", full * 8 * width,
            [pltpu.VMEM((tokens, sizes["out"]), f32)],
        )(
            vec, grad_mid, mid_low, *weights["out", i], *values["qkv", i], *weights["qkv", i],
            values["residual", i],
        )
        got = step_on(got, [])
        grad_res, grad_low, mix_a, mix_b, wides["mix", i], flats["mix", i], gift = got
        got_low, low_at = across_core(gift), 0
        low_one, got_qkv = values["low_one", i], values["got_qkv", i]
        out_args = (mid_low, got_mid, 0, values["context", i][0], got_qkv, width, "out")
        mix_args = (low_one, got_qkv, 0, mix_a, got_low, width, "qkv")
        if i > 0:
            first_x = [product("x", *mix_args, range(0, 2))]
            first_y = [product("y", *mix_args, range(2, 3)), product("y", *out_args)]
            group_names = [("qkv", i), ("out", i)]
        else:
            outs = activations(width) + [((LP, width), f32), ((8, width), f32)]
            embed_low, place_sum, wides["embed"] = whole_call(back_embed_body, outs, "back_embed", full)(
                grad_res, flags
            )
            got_embed = across_core(embed_low)
            first_x = [product("x", *mix_args)]
            first_y = [
                product("y", *out_args),
                product("y", embed_low, got_embed, 0, pix_half[0], pix_other, 0, "ends"),
            ]
            group_names = [("qkv", i), ("out", i), ("ends", 0)]
        group = Reduce(first_x, first_y)
        groups.append((group, group_names))
        if i > 0:
            grad_res, grad_low, got_low = step_on((grad_res, grad_low, got_low), [group])
        else:
            wide_keys, flat_keys = list(wides), list(flats)
            place_sum, wide_rows, flat_rows = step_on(
                (place_sum, [wides[k] for k in wide_keys], [flats[k] for k in flat_keys]), [group]
            )
            wides.update(zip(wide_keys, wide_rows))
            flats.update(zip(flat_keys, flat_rows))

    raw_wide = [place_sum, wides["embed"], wides["head"]]
    raw_flat = [flats["head"]]
    source_wide = list(range(L)) + [LP, LP + 1, LP + 2, LP + 8, LP + 9, -1]
    source_flat = [-1] * (L + 5) + [0]
    rolled = [1] * 8
    for i in range(layer_count):
        at, low = LP + 16 * (i + 1), 8 + 16 * i
        raw_wide += [wides["mlp", i], wides["mix", i]]
        raw_flat += [flats["mlp", i], flats["mix", i]]
        source_wide += [at + 9, at + 10, -1, -1, at + 8, at + 1, at + 2, -1, -1, -1, -1, at]
        source_flat += [-1, -1, low + 8, low + 9, -1, -1, -1, low, low + 1, low + 2, low + 3, -1]
        rolled += [0] * 8 + [1] * 8
    rows_all = -(-vectors.shape[0] // 256) * 256
    spare = [-1] * (rows_all - vectors.shape[0])
    source_wide, source_flat = jnp.array(source_wide + spare), jnp.array(source_flat + spare)
    raw_wide = jnp.concatenate(raw_wide, axis=0)
    raw_flat = jnp.concatenate(raw_flat, axis=0)
    other = jnp.concatenate([raw_flat[:, width // 2 :], raw_flat[:, : width // 2]], axis=1)
    raw_flat = jnp.where(swapped & (jnp.array(rolled)[:, None] == 1), other, raw_flat)
    is_up = (source_flat >= 0) & (source_flat % 16 >= 8) & (source_flat % 16 < 12)
    turned_row = source_flat // 4 * 4 + (source_flat % 4 + 2 * row_index) % 4
    source_flat = jnp.where(is_up, turned_row, source_flat)
    pick_wide = (source_wide[:, None] == jnp.arange(raw_wide.shape[0])[None, :]).astype(f32)
    pick_flat = (source_flat[:, None] == jnp.arange(raw_flat.shape[0])[None, :]).astype(f32)
    grad_vec = exact(exact(pick_wide, raw_wide, 1, 0), turn, 1, 1) + exact(pick_flat, raw_flat, 1, 0)

    def rows_at(value, index, size):
        return lax.dynamic_slice_in_dim(value, index * size, size)

    half_rows, sub_rows = rows_all // 2, rows_all // 8
    value = rows_at(grad_vec, row_index, half_rows) + across_core(rows_at(grad_vec, 1 - row_index, half_rows))
    value = step_on(value, [])
    value = rows_at(value, sub_index, sub_rows) + sum(
        swap(rows_at(value, sub_index ^ k, sub_rows), "dp", k) for k in (1, 2, 3)
    )
    value = step_on(value, [])
    value = butterfly(value, ("col",))
    for mask in bits_of("dp")[2:]:
        value = value + swap(value, "dp", mask)
    while flying:
        value = step_on(value, [])
    copies = max(1, data_count // 4)
    square = sum(jnp.sum(g.keep * g.keep) for g, _ in groups)
    square = (square + jnp.sum(value * value) / lax.axis_size("col")) / copies
    pair = butterfly(jnp.stack([square, values["loss"][0, 0]]), ("row", "dp"))
    value = jnp.concatenate([value] + [swap(value, "dp", k) for k in (1, 2, 3)], axis=0)
    value = jnp.concatenate([value, across_core(value)], axis=0)
    pair, value, payloads = tie(pair, value, [payloads for payloads, _ in spreads])
    for entry, got in zip(spreads, payloads):
        entry[0] = got
    spot = jnp.arange(rows_all)
    native = (
        ((spot // half_rows) ^ row_index) * half_rows
        + (((spot // sub_rows) & 3) ^ sub_index) * sub_rows
        + spot % sub_rows
    )
    pick = (jnp.arange(vectors.shape[0])[:, None] == native[None, :]).astype(f32)
    vec_sum = exact(pick, value, 1, 0)
    pair = butterfly(pair, ("col",))
    loss_total = pair[1]
    grad_norm = jnp.sqrt(pair[0])
    factor = jnp.minimum(1.0, clip_scale / math.sqrt(total_tokens) / grad_norm)

    pieces, layout, ends_parts = [], [], {}
    for payloads, members in spreads:
        names_in = [name for _, group_names in members for name in group_names]
        spans, at = [], 0
        for name in names_in:
            size = sizes[name[0]]
            spans.append((at, start_of[name], size))
            if name[0] == "ends":
                ends_parts[name[1]] = (len(pieces), at)
            at += size
        for k, payload in enumerate(payloads):
            pieces.append(decoded(payload[:-16], tail_of(payload)))
            layout.append((k, spans))
    raw_grad, raw_left, raw_right, raw_precond, own_weight = shampoo(
        info, tiles_own, pieces, layout, root_left[0], root_right[0]
    )
    block_grad = raw_grad * factor
    square_factor = (1.0 - decay_stat) * factor * factor
    left_next = decay_stat * stat_left[0] + square_factor * raw_left
    right_next = decay_stat * stat_right[0] + square_factor * raw_right
    block_next = own_weight - rate_blocks * (factor * raw_precond + weight_decay * own_weight)

    ends_refs = []
    for end in range(2):
        index, at = ends_parts[end]
        ends_refs += [pieces[index + k][:, at : at + sizes["ends"]] for k in range(4)]
    ends_flat = whole_call_smem(
        ends_body, 1, 8, [((2, 4 * part, sizes["ends"]), f32)], "ends_order", 10**7
    )(places, *ends_refs)[0]
    ends_grad = ends_flat.transpose(0, 2, 1)
    step_value = step_count.astype(f32)
    vector_next, moment_vector, second_vector = adam_update(
        vectors, vec_sum, vector_moment, vector_second, rate_vector, 0.0, factor, step_value
    )
    ends_next, moment_ends, second_ends = adam_update(
        weight_ends.astype(f32),
        ends_grad,
        ends_moment,
        ends_second,
        rate_matrix,
        weight_decay,
        factor,
        step_value,
    )
    return (
        loss_total,
        grad_norm,
        vector_next,
        moment_vector,
        second_vector,
        ends_next,
        moment_ends,
        second_ends,
        block_grad[None],
        left_next[None],
        right_next[None],
        block_next[None],
    )


def solution(mesh):
    grid = P(None, "row", "col")
    slots = P(("row", "col"), "dp", None, None)
    return jax.shard_map(
        shards,
        mesh=mesh,
        in_specs=(
            P(None, ("dp", "col"), "row"),
            P(None, "dp"),
            P(None, "dp"),
            P(),
            P(),
            P(None, "col", "row"),
            grid,
            P(None, "col", "row"),
            grid,
            grid,
            P(),
            P(),
            P(),
            grid,
            grid,
            slots,
            slots,
            slots,
            slots,
            P(("row", "col"), None),
        ),
        out_specs=(P(), P(), P(), P(), P(), grid, grid, grid, slots, slots, slots, slots),
        check_vma=False,
    )
```

```python
import math

import jax
import jax.numpy as jnp
from jax import lax
from jax.experimental import pallas as pl
from jax.experimental.pallas import tpu as pltpu
from jax.sharding import PartitionSpec as P

HD = 64
PATCH = 768
L = 197
LP = 208
BLK = 96

norm_eps = 1e-06
beta_first = 0.9
beta_second = 0.999
adam_eps = 1e-08
decay_stat = 0.5
rate_matrix = 0.02
rate_vector = 0.2
rate_blocks = 0.1
weight_decay = 0.05
clip_scale = 0.25
highest = lax.Precision.HIGHEST
bf16 = jnp.bfloat16
f16 = jnp.float16
f32 = jnp.float32


COST = 16
VMEM = pl.BlockSpec(memory_space=pltpu.VMEM)
SMEM = pl.BlockSpec(memory_space=pltpu.SMEM)


def whole_call(body, outs, name, flops, scratch=()):
    return pl.pallas_call(
        body,
        out_shape=[jax.ShapeDtypeStruct(shape, dtype) for shape, dtype in outs],
        scratch_shapes=list(scratch),
        compiler_params=pltpu.CompilerParams(vmem_limit_bytes=52 * 2**20),
        cost_estimate=pl.CostEstimate(flops=flops // COST, bytes_accessed=2**16, transcendentals=0),
        name=name,
    )


def dot(lhs_mat, rhs_mat, lhs_dim, rhs_dim):
    return lax.dot_general(
        lhs_mat, rhs_mat, (((lhs_dim,), (rhs_dim,)), ((), ())), preferred_element_type=f32
    )


def exact(lhs_mat, rhs_mat, lhs_dim, rhs_dim):
    return lax.dot_general(
        lhs_mat,
        rhs_mat,
        (((lhs_dim,), (rhs_dim,)), ((), ())),
        precision=highest,
        preferred_element_type=f32,
    )


def swap(value, axis, mask):
    size = lax.axis_size(axis)
    return lax.ppermute(value, axis, [(i, i ^ mask) for i in range(size)])


def bits_of(axis):
    return [1 << b for b in range(lax.axis_size(axis).bit_length() - 1)]


def butterfly(value, axes, op=jnp.add):
    for axis in axes:
        for mask in bits_of(axis):
            value = op(value, swap(value, axis, mask))
    return value


def softmax_scores(queries, key_rows):
    scores = dot(queries, key_rows, 1, 1)
    spot = lax.broadcasted_iota(jnp.int32, scores.shape, 1)
    scores = jnp.where(spot < L, scores, -1e30)
    top = jnp.max(scores, axis=1, keepdims=True)
    exponent = jnp.exp(scores - top)
    return exponent / jnp.sum(exponent, axis=1, keepdims=True)


def attend_forward(qkv_ref, ctx_ref):
    rows, wide = qkv_ref.shape
    for image in range(rows // LP):
        span = slice(image * LP, (image + 1) * LP)
        for pair in range(wide // (6 * HD)):
            made = []
            for head in (2 * pair, 2 * pair + 1):
                base = head * 3 * HD
                queries = qkv_ref[span, base : base + HD]
                key_rows = qkv_ref[span, base + HD : base + 2 * HD]
                values = qkv_ref[span, base + 2 * HD : base + 3 * HD]
                attend = softmax_scores(queries, key_rows).astype(bf16)
                made.append(dot(attend, values, 1, 0).astype(bf16))
            ctx_ref[span, pair * 2 * HD : (pair + 1) * 2 * HD] = jnp.concatenate(made, axis=1)


def attend_backward(qkv_ref, grad_ref, out_ref):
    rows, wide = qkv_ref.shape
    for image in range(rows // LP):
        span = slice(image * LP, (image + 1) * LP)
        for pair in range(wide // (6 * HD)):
            made = []
            for head in (2 * pair, 2 * pair + 1):
                base = head * 3 * HD
                queries = qkv_ref[span, base : base + HD]
                key_rows = qkv_ref[span, base + HD : base + 2 * HD]
                values = qkv_ref[span, base + 2 * HD : base + 3 * HD]
                grad = grad_ref[span, head * HD : (head + 1) * HD].astype(bf16)
                attend = softmax_scores(queries, key_rows)
                grad_values = dot(attend.astype(bf16), grad, 0, 0)
                grad_attend = dot(grad, values, 1, 1)
                inner = jnp.sum(grad_attend * attend, axis=1, keepdims=True)
                grad_scores = (attend * (grad_attend - inner)).astype(bf16)
                made.append((dot(grad_scores, key_rows, 1, 0) * 0.125).astype(bf16))
                made.append(dot(grad_scores, queries, 0, 0).astype(bf16))
                made.append(grad_values.astype(bf16))
            out_ref[span, pair * 6 * HD : (pair + 1) * 6 * HD] = jnp.concatenate(made, axis=1)


def normed_of(residual):
    center = residual - jnp.mean(residual, axis=1, keepdims=True)
    inverse = lax.rsqrt(jnp.mean(center * center, axis=1, keepdims=True) + norm_eps)
    return center * inverse, inverse


def norm_backward(grad_normed, residual, gain):
    normed, inverse = normed_of(residual)
    scaled = grad_normed * gain
    mean_one = jnp.mean(scaled, axis=1, keepdims=True)
    mean_two = jnp.mean(scaled * normed, axis=1, keepdims=True)
    grad_in = inverse * (scaled - mean_one - normed * mean_two)
    gain_sum = jnp.sum(grad_normed * normed, axis=0, keepdims=True)
    return grad_in, gain_sum, jnp.sum(grad_normed, axis=0, keepdims=True)


def rows_sum(value):
    return jnp.sum(value.astype(f32), axis=0, keepdims=True)


def put_rows(ref, rows):
    ref[...] = jnp.zeros(ref.shape, f32)
    for i, row in enumerate(rows):
        ref[i : i + 1, :] = row


def own_first(row, core):
    half = row.shape[1] // 2
    return jnp.where(core == 1, jnp.concatenate([row[:, half:], row[:, :half]], axis=1), row)


def qkv_part(base, places, vec, vectors, residual, weights, low_one, qkv, context):
    normed, _ = normed_of(residual)
    low_one[...] = (normed * vec[base : base + 1, :] + vec[base + 1 : base + 2, :]).astype(bf16)
    query_bias = own_first(vectors[base + 2 : base + 3, :], places[1])
    value_bias = own_first(vectors[base + 3 : base + 4, :], places[1])
    for half in range(2):
        heads = qkv[half].shape[1] // (3 * HD)
        parts = []
        for head in range(heads):
            at = (half * heads + head) * HD
            parts += [query_bias[:, at : at + HD], jnp.zeros((1, HD), f32), value_bias[:, at : at + HD]]
        bias = jnp.concatenate(parts, axis=1)
        kind = (lax.broadcasted_iota(jnp.int32, bias.shape, 1) // HD) % 3
        factor = jnp.where(kind == 0, 0.125, 1.0)
        step = 6 * HD
        for at in range(0, heads * 3 * HD, step):
            span = slice(at, at + step)
            mixed = dot(low_one[...], weights[half][:, span], 1, 0)
            qkv[half][:, span] = ((mixed + bias[:, span]) * factor[:, span]).astype(bf16)
        attend_forward(qkv[half], context[half])


def give(ref, parts):
    at = 0
    for part in parts:
        ref[:, at : at + part.shape[1]] = part[...]
        at += part.shape[1]


def embed_qkv_body(
    places, vec, vectors, pix_a, pix_b, flags, ends_a, ends_b, qkv_a, qkv_b,
    residual, low_one, out_a, out_b, ctx_a, ctx_b, gift,
):
    embedded = dot(pix_a[...], ends_a[...], 1, 1) + dot(pix_b[...], ends_b[...], 1, 1)
    embedded = embedded + vec[L + 2 : L + 3, :]
    spots = vec[0:LP, :]
    spots = jnp.concatenate([spots] * (embedded.shape[0] // LP), axis=0)
    picked = jnp.where(flags[:, 1:2] > 0, vec[L + 1 : L + 2, :], embedded)
    picked = jnp.where(flags[:, 0:1] > 0, vec[L : L + 1, :], picked)
    residual[...] = jnp.where(flags[:, 2:3] > 0, picked + spots, 0.0)
    qkv_part(
        L + 6, places, vec, vectors, residual[...], (qkv_a, qkv_b), low_one, (out_a, out_b), (ctx_a, ctx_b)
    )
    give(gift, (low_one, ctx_b))


def up_body(
    base, places, vec, vectors, residual, ctx_a, ctx_b, out_a, out_b, up_a, up_b,
    mid, low_two, act_a, act_b, slope_a, slope_b, gift,
):
    branch = dot(ctx_a[...], out_a[...], 1, 1) + dot(ctx_b[...], out_b[...], 1, 1)
    mid[...] = residual[...] + (branch + vec[base + 4 : base + 5, :])
    normed, _ = normed_of(mid[...])
    low_two[...] = (normed * vec[base + 5 : base + 6, :] + vec[base + 6 : base + 7, :]).astype(bf16)
    wide = vec.shape[1]
    for half, (weight, active, slope) in enumerate(((up_a, act_a, slope_a), (up_b, act_b, slope_b))):
        for k in range(weight.shape[1] // wide):
            row = base + 7 + (weight.shape[1] // wide) * jnp.bitwise_xor(places[1], half) + k
            span = slice(k * wide, (k + 1) * wide)
            pre = dot(low_two[...], weight[:, span], 1, 0) + vectors[pl.ds(row, 1), :]
            phi = 0.5 * (1.0 + lax.erf(pre * math.sqrt(0.5)))
            active[:, span] = (pre * phi).astype(bf16)
            slope[:, span] = phi + pre * (jnp.exp(-0.5 * pre * pre) * (1.0 / math.sqrt(2.0 * math.pi)))
    give(gift, (low_two, act_b))


def down_qkv_body(
    base, places, vec, vectors, mid, act_a, act_b, down_a, down_b, qkv_a, qkv_b,
    residual, low_one, out_a, out_b, ctx_a, ctx_b, gift,
):
    branch = dot(act_a[...], down_a[...], 1, 1) + dot(act_b[...], down_b[...], 1, 1)
    residual[...] = mid[...] + (branch + vec[base - 1 : base, :])
    qkv_part(
        base, places, vec, vectors, residual[...], (qkv_a, qkv_b), low_one, (out_a, out_b), (ctx_a, ctx_b)
    )
    give(gift, (low_one, ctx_b))


def down_head_body(
    base, places, vec, vectors, scale, mid, act_a, act_b, down_a, down_b, ends_a, ends_b, pix_a, pix_b, flags,
    low_fin, pred_a, pred_b, grad_res, grad_low, wide, flat, loss, gift,
):
    branch = dot(act_a[...], down_a[...], 1, 1) + dot(act_b[...], down_b[...], 1, 1)
    residual = mid[...] + (branch + vec[base + 11 : base + 12, :])
    normed, _ = normed_of(residual)
    low_fin[...] = (normed * vec[L + 3 : L + 4, :] + vec[L + 4 : L + 5, :]).astype(bf16)
    bias = own_first(vectors[L + 5 : L + 6, :], places[1])
    keep = flags[:, 3:4]
    total = jnp.zeros((1, 1), f32)
    sums = []
    for half, (ends, pix, pred) in enumerate(((ends_a, pix_a, pred_a), (ends_b, pix_b, pred_b))):
        span = ends.shape[1]
        error = dot(low_fin[...], ends[...], 1, 0) + bias[:, half * span : (half + 1) * span]
        error = error - pix[...].astype(f32)
        total = total + jnp.sum(jnp.sum(keep * error * error, axis=1, keepdims=True), axis=0, keepdims=True)
        pred[...] = (2.0 * scale[0] * keep * error).astype(bf16)
        sums.append(rows_sum(pred[...]))
    loss[...] = jnp.broadcast_to(total * scale[0], loss.shape)
    grad_fin = dot(pred_a[...], ends_a[...], 1, 1) + dot(pred_b[...], ends_b[...], 1, 1)
    grad, gain_sum, shift_sum = norm_backward(grad_fin, residual, vec[L + 3 : L + 4, :])
    grad_res[...] = grad
    grad_low[...] = grad.astype(bf16)
    put_rows(wide, [gain_sum, shift_sum])
    put_rows(flat, [jnp.concatenate(sums, axis=1)])
    give(gift, (low_fin, grad_low, pred_b))


def back_mlp_body(
    base, vec, grad_res, grad_low, down_a, down_b, slope_a, slope_b, up_a, up_b, mid,
    grad_mid, mid_low, hid_a, hid_b, wide, flat, gift,
):
    span = vec.shape[1]
    sums = []
    total = None
    for down, slope, up, hid in ((down_a, slope_a, up_a, hid_a), (down_b, slope_b, up_b, hid_b)):
        for at in range(0, down.shape[1], span):
            cols = slice(at, at + span)
            hid[:, cols] = (dot(grad_low[...], down[:, cols], 1, 0) * slope[:, cols]).astype(bf16)
            sums.append(rows_sum(hid[:, cols]))
        part = dot(hid[...], up[...], 1, 1)
        total = part if total is None else total + part
    grad, gain_sum, shift_sum = norm_backward(total, mid[...], vec[base + 5 : base + 6, :])
    grad = grad_res[...] + grad
    grad_mid[...] = grad
    mid_low[...] = grad.astype(bf16)
    put_rows(wide, [rows_sum(grad_low[...]), gain_sum, shift_sum])
    put_rows(flat, sums)
    give(gift, (mid_low, hid_b))


def back_attend_body(
    base, vec, grad_mid, mid_low, out_a, out_b, qkv_a, qkv_b, wqkv_a, wqkv_b, residual,
    grad_res, grad_low, mix_a, mix_b, wide, flat, gift, ctx,
):
    total = None
    query_sums, value_sums = [], []
    for out, qkv, wqkv, mix in ((out_a, qkv_a, wqkv_a, mix_a), (out_b, qkv_b, wqkv_b, mix_b)):
        ctx[...] = dot(mid_low[...], out[...], 1, 0)
        attend_backward(qkv, ctx, mix)
        part = dot(mix[...], wqkv[...], 1, 1)
        total = part if total is None else total + part
        sums = rows_sum(mix[...])
        for head in range(mix.shape[1] // (3 * HD)):
            at = head * 3 * HD
            query_sums.append(sums[:, at : at + HD])
            value_sums.append(sums[:, at + 2 * HD : at + 3 * HD])
    grad, gain_sum, shift_sum = norm_backward(total, residual[...], vec[base : base + 1, :])
    grad = grad_mid[...] + grad
    grad_res[...] = grad
    grad_low[...] = grad.astype(bf16)
    put_rows(wide, [rows_sum(mid_low[...]), gain_sum, shift_sum])
    put_rows(flat, [jnp.concatenate(query_sums, axis=1), jnp.concatenate(value_sums, axis=1)])
    give(gift, (grad_low, mix_b))


def back_embed_body(grad_res, flags, grad_low, place, wide):
    grad = grad_res[...]
    low = jnp.where(flags[:, 4:5] > 0, grad, 0.0).astype(bf16)
    grad_low[...] = low
    total = grad[0:LP]
    for image in range(1, grad.shape[0] // LP):
        total = total + grad[image * LP : (image + 1) * LP]
    place[...] = total
    class_sum = rows_sum(jnp.where(flags[:, 0:1] > 0, grad, 0.0))
    mask_sum = rows_sum(jnp.where(flags[:, 1:2] > 0, grad, 0.0))
    put_rows(wide, [class_sum, mask_sum, rows_sum(low)])


def four(value, axis):
    got = [swap(value, axis, k) for k in (1, 2, 3)]
    return (value + got[0]) + (got[1] + got[2])


def tie(*trees):
    leaves, shape = jax.tree.flatten(trees)
    return jax.tree.unflatten(shape, lax.optimization_barrier(leaves))


def prepare_body(plan, cuts, places, qkv, out, up, down, ends, *rest):
    whole, owns, firsts = rest[0], rest[1::2], rest[2::2]
    sub_at = places[0]
    part = whole.shape[1]
    refs = {"qkv": qkv, "out": out, "up": up, "down": down, "ends": ends}
    for chunk in range(len(cuts) - 1):
        begin = plan[cuts[chunk]][2]
        for name, layer, start, width in plan[cuts[chunk] : cuts[chunk + 1]]:
            ref = refs[name]
            for k in range(4):
                rows = pl.ds(pl.multiple_of(jnp.bitwise_xor(sub_at, k) * part, 16), part)
                piece = ref[layer, rows, :]
                whole[k, :, start : start + width] = piece
                owns[chunk][k, :, start - begin : start - begin + width] = piece
                if k == 0:
                    firsts[chunk][:, start - begin : start - begin + width] = piece


def prepare_tiles(plan, cuts, places, qkv, out, up, down, ends):
    height = qkv.shape[1]
    part = height // 4
    outs = [((4, part, plan[-1][2] + plan[-1][3]), bf16)]
    for j, k in zip(cuts[:-1], cuts[1:]):
        width = plan[k - 1][2] + plan[k - 1][3] - plan[j][2]
        outs += [((4, part, width), bf16), ((part, width), bf16)]
    got = whole_call_smem(
        lambda *refs: prepare_body(plan, cuts, *refs), 1, 5, outs, "prepare_tiles", 10**8,
    )(places, qkv, out.swapaxes(1, 2), up, down.swapaxes(1, 2), ends.swapaxes(1, 2))
    return got[0], got[1::2], got[2::2]


def whole_call_smem(body, scalars, arrays, outs, name, flops, scratch=()):
    return pl.pallas_call(
        body,
        in_specs=[SMEM] * scalars + [VMEM] * arrays,
        out_specs=[VMEM] * len(outs),
        out_shape=[jax.ShapeDtypeStruct(shape, dtype) for shape, dtype in outs],
        scratch_shapes=list(scratch),
        compiler_params=pltpu.CompilerParams(vmem_limit_bytes=52 * 2**20),
        cost_estimate=pl.CostEstimate(flops=flops // COST, bytes_accessed=2**16, transcendentals=0),
        name=name,
    )


def assemble_body(widths, half, at_left, at_right, own, stack, from_x, from_y, in_y, in_x, *outs):
    part = own.shape[1]
    start = 0
    for out, width in zip(outs, widths):
        stop = start + width
        for k in range(4):
            out[4 * k * part : (4 * k + 1) * part, :] = own[k, :, start:stop]
            rows = slice((4 * k + 1) * part, 4 * (k + 1) * part)
            if k < 3:
                out[rows, :] = (stack, from_x, from_y)[k][:, start:stop]
                continue
            middle = min(max(half, start), stop)
            if middle > start:
                out[rows, : middle - start] = in_y[:, at_left + start : at_left + middle]
            if stop > middle:
                out[rows, middle - start :] = in_x[:, at_right + middle - half : at_right + stop - half]
        start = stop


class Gather:
    def __init__(self, own, first, widths):
        self.own, self.first, self.widths = own, first, widths
        self.total = sum(widths)
        self.half = self.total // 256 * 128
        self.state = []

    def along(self):
        self.state = [jnp.concatenate([swap(self.first, "col", k) for k in (1, 2, 3)], axis=0)]

    @staticmethod
    def across(new, old):
        out_x, out_y = [], []
        if new is not None:
            out_x.append(new.state[0])
            out_y.append(new.state[0])
        if old is not None:
            out_y.append(old.state[1][:, : old.half])
            out_x.append(old.state[2][:, old.half : old.total])
        got_x = swap(jnp.concatenate(out_x, axis=1) if len(out_x) > 1 else out_x[0], "dp", 1)
        got_y = swap(jnp.concatenate(out_y, axis=1) if len(out_y) > 1 else out_y[0], "dp", 2)
        if new is not None:
            new.state += [got_x, got_y]
        if old is not None:
            old.at = 0 if new is None else new.total
            old.state += [got_y, got_x]

    def weights(self):
        height = 16 * self.own.shape[1]
        mine = whole_call(
            lambda *refs: assemble_body(self.widths, self.half, self.at, self.at, *refs),
            [((height, w), bf16) for w in self.widths],
            "assemble",
            10**8,
        )(self.own, *self.state)
        return [(w, swap(w, "row", 1)) for w in mine]


def row_runs(name, part):
    runs = []
    for bit in range(2):
        rows = []
        for other in range(2):
            sub = 2 * other + bit if name == "x" else 2 * bit + other
            rows += [((4 * sub + 2 * high + low) * part, part) for low in range(2) for high in range(2)]
        runs.append(rows)
    return runs


def product_body(runs, left, left_got, right, right_got, keep, send, power, total):
    total[...] = dot(left[...], right[...], 0, 0) + dot(left_got[...], right_got[...], 0, 0)
    top = jnp.max(jnp.abs(total[...]), axis=0, keepdims=True)
    exponent = jnp.clip(jnp.ceil(jnp.log2(top)) + 1.0, -100.0, 120.0)
    scale = jnp.exp2(14.0 - exponent)
    power[...] = exponent
    for out, spans, factor in ((keep, runs[0], None), (send, runs[1], scale)):
        at = 0
        for start, size in spans:
            piece = total[start : start + size, :]
            out[at : at + size, :] = piece if factor is None else piece * factor
            at += size
    send[at:, :] = jnp.broadcast_to(exponent, (16, exponent.shape[1]))


def product_sum(name, left, left_got, left_at, right, right_got, right_at, block, blocks):
    rows, height = left.shape
    width = block * len(blocks)
    first = blocks[0]
    runs = row_runs(name, height // 16)
    whole = pl.BlockSpec((rows, height), lambda i: (0, 0))
    whole_got = pl.BlockSpec((rows, height), lambda i: (0, left_at // height))
    part = pl.BlockSpec((rows, block), lambda i: (0, i + first))
    part_got = pl.BlockSpec((rows, block), lambda i: (0, i + first + right_at // block))
    half = pl.BlockSpec((height // 2, block), lambda i: (0, i))
    return pl.pallas_call(
        lambda *refs: product_body(runs, *refs),
        grid=(len(blocks),),
        in_specs=[whole, whole_got, part, part_got],
        out_specs=[
            half,
            pl.BlockSpec((height // 2 + 16, block), lambda i: (0, i)),
            pl.BlockSpec((1, block), lambda i: (0, i)),
        ],
        out_shape=[
            jax.ShapeDtypeStruct((height // 2, width), f32),
            jax.ShapeDtypeStruct((height // 2 + 16, width), f32),
            jax.ShapeDtypeStruct((1, width), f32),
        ],
        scratch_shapes=[pltpu.VMEM((height, block), f32)],
        compiler_params=pltpu.CompilerParams(vmem_limit_bytes=32 * 2**20),
        cost_estimate=pl.CostEstimate(
            flops=4 * rows * height * width // COST, bytes_accessed=2**16, transcendentals=0
        ),
        name="product_sum",
    )(left, left_got, right, right_got)


def lowered(rows, exponent):
    tail = jnp.broadcast_to(exponent, (16, exponent.shape[1]))
    return jnp.concatenate([rows * jnp.exp2(14.0 - exponent), tail], axis=0).astype(f16)


def tail_of(payload):
    return jnp.max(payload[-16:].astype(f32), axis=0, keepdims=True)


def decoded(rows, exponent):
    return rows.astype(f32) * jnp.exp2(exponent - 14.0)


class Reduce:
    def __init__(self, first_x, first_y):
        self.parts = []
        for products in (first_x, first_y):
            keep, send, exponent = (jnp.concatenate(list(p), axis=1) for p in zip(*products))
            self.parts.append([keep, send.astype(f16), exponent])
        self.stage = 0

    def send(self):
        ways = ((("dp", 1), ("dp", 2)), (("dp", 2), ("dp", 1)), (("col", 1),), (("col", 2),))[self.stage]
        self.got = [swap(part[1], axis, mask) for part, (axis, mask) in zip(self.parts, ways)]

    def absorb(self):
        made = []
        for (keep, _, exponent), got in zip(self.parts, self.got):
            theirs = tail_of(got)
            after = jnp.maximum(exponent, theirs) + 1.0
            if self.stage == 3:
                made.append([keep + decoded(got[:-16], theirs), None, after])
                continue
            half = keep.shape[0] // 2
            stay = keep[:half] + decoded(got[:half], theirs)
            leave = keep[half:] + decoded(got[half : 2 * half], theirs)
            made.append([stay, leave, after])
        if self.stage == 1:
            made = [[jnp.concatenate(list(p), axis=1) for p in zip(*made)]]
        self.stage += 1
        if self.stage < 4:
            self.parts = [[stay, lowered(leave, after), after] for stay, leave, after in made]
            return
        keep, _, after = made[0]
        for mask in bits_of("dp")[2:]:
            keep = keep + swap(keep, "dp", mask)
            after = after + 1.0
        self.parts = []
        self.keep, self.exponent = keep, after


def split(value):
    high = value.astype(bf16)
    return high, (value - high.astype(f32)).astype(bf16)


def close(lhs, rhs, lhs_dim, rhs_dim):
    small = dot(lhs[0], rhs[1], lhs_dim, rhs_dim) + dot(lhs[1], rhs[0], lhs_dim, rhs_dim)
    return dot(lhs[0], rhs[0], lhs_dim, rhs_dim) + small


def shampoo_body(
    group, layout, info, weight, *rest
):
    pieces, (rl, rr, grad_out, left, right, precond, weight_out), grads = rest[:-8], rest[-8:-1], rest[-1]
    step = pl.program_id(0)

    @pl.when(step == 0)
    def _():
        for ref, (sub, spans) in zip(pieces, layout):
            part = grads.shape[1]
            for source, target, size in spans:
                grads[sub, :, target : target + size] = scaled(ref[:, source : source + size], part)

    window = 2 * 128

    def block_of(ref, slot):
        start = pl.multiple_of(info[2, slot] * 128, 128)
        tops = [ref[info[k, slot], :, pl.ds(start, window)].astype(f32) for k in range(2)]
        both = jnp.concatenate(tops, axis=0)
        both = pltpu.roll(both, info[3, slot], 1)[:, :BLK]
        return jnp.where(info[4, slot] == 1, both.T, both)

    for j in range(group):
        slot = step * group + j
        g = block_of(grads, slot)
        grad_out[j] = g
        weight_out[j] = block_of(weight, slot)
        both = split(g)
        left[j] = close(both, both, 1, 1)
        right[j] = close(both, both, 0, 0)
        inner = close(both, split(rr[j]), 1, 0)
        precond[j] = close(split(rl[j]), split(inner), 1, 0)


def shampoo(info, weight, pieces, layout, root_left, root_right):
    count = root_left.shape[0]
    group = next(g for g in (8, 6, 4, 3, 2, 1) if count % g == 0)
    plain = pl.BlockSpec((group, BLK, BLK), lambda i: (i, 0, 0))
    return pl.pallas_call(
        lambda *refs: shampoo_body(group, layout, *refs),
        grid=(count // group,),
        in_specs=[SMEM] + [VMEM] * (1 + len(pieces)) + [plain] * 2,
        out_specs=[plain] * 5,
        out_shape=[jax.ShapeDtypeStruct((count, BLK, BLK), f32)] * 5,
        scratch_shapes=[pltpu.VMEM(weight.shape, f32)],
        compiler_params=pltpu.CompilerParams(vmem_limit_bytes=52 * 2**20),
        cost_estimate=pl.CostEstimate(
            flops=count * 48 * BLK**3 // COST, bytes_accessed=2**16, transcendentals=0
        ),
        name="shampoo",
    )(info, weight, *pieces, root_left, root_right)


def scaled(rows, part):
    return rows[:part] * jnp.exp2(rows[part : part + 1] - 14.0)


def ends_body(places, *refs):
    out = refs[-1]
    part = out.shape[1] // 4
    for end in range(2):
        for k in range(4):
            sub = jnp.bitwise_xor(places[0], k)
            out[end, pl.ds(pl.multiple_of(sub * part, 8), part), :] = scaled(refs[4 * end + k][...], part)


def adam_update(weight, gradient, moment, second, rate, decay, factor, step_value):
    clipped = gradient * factor
    moment_new = beta_first * moment + (1.0 - beta_first) * clipped
    second_new = beta_second * second + (1.0 - beta_second) * clipped * clipped
    corr_first = 1.0 - jnp.power(beta_first, step_value)
    corr_second = 1.0 - jnp.power(beta_second, step_value)
    stride = moment_new / corr_first / (jnp.sqrt(second_new / corr_second) + adam_eps)
    return (weight - rate * (stride + decay * weight), moment_new, second_new)


def shards(
    pixels,
    patch_mask,
    class_ids,
    class_counts,
    step_count,
    weight_qkv,
    weight_out,
    weight_up,
    weight_down,
    weight_ends,
    vectors,
    vector_moment,
    vector_second,
    ends_moment,
    ends_second,
    stat_left,
    stat_right,
    root_left,
    root_right,
    owner_map,
):
    data_count = lax.axis_size("dp")
    row_index = lax.axis_index("row")
    col_index = lax.axis_index("col")
    data_index = lax.axis_index("dp")
    sub_index = data_index & 3
    layer_count = weight_qkv.shape[0]
    width = vectors.shape[1]
    images = pixels.shape[1] // L
    total_tokens = pixels.shape[0] * pixels.shape[1] * lax.axis_size("col") * data_count
    places = jnp.stack([sub_index, row_index]).astype(jnp.int32)
    swapped = row_index == 1

    names = [("ends", 0)]
    for i in range(layer_count):
        names += [("qkv", i), ("out", i), ("up", i), ("down", i)]
    names.append(("ends", 1))
    sizes = {
        "qkv": weight_qkv.shape[2],
        "out": weight_out.shape[1],
        "up": weight_up.shape[2],
        "down": weight_down.shape[1],
        "ends": weight_ends.shape[1],
    }
    plan, at = [], 0
    for name, i in names:
        plan.append((name, i, at, sizes[name]))
        at += sizes[name]
    start_of = {entry[:2]: entry[2] for entry in plan}
    stage_cuts = [0]
    for i in range(layer_count):
        stage_cuts += [2 + 4 * i, 4 + 4 * i]
    stage_cuts.append(len(plan))
    last = len(stage_cuts) - 1
    stages_of = [[0, 1]] + [[k] for k in range(2, last - 2)] + [[last - 2, last - 1]]
    cuts = [stage_cuts[stages[0]] for stages in stages_of] + [len(plan)]
    tiles_own, owns, firsts = prepare_tiles(
        plan, cuts, places, weight_qkv, weight_out, weight_up, weight_down, weight_ends
    )
    chunks = [
        Gather(own, first, [entry[3] for entry in plan[j:k]])
        for own, first, j, k in zip(owns, firsts, cuts[:-1], cuts[1:])
    ]

    part = weight_qkv.shape[1] // 4
    column = jnp.arange(width)
    piece, inner = column // part, column % part
    source = ((piece & 3) ^ col_index) * (4 * part) + ((piece >> 2) ^ sub_index) * part + inner
    turn = (column[:, None] == source[None, :]).astype(f32)
    vec = exact(vectors, turn, 1, 0)

    def pad_rows(value):
        shaped = value.reshape(images, L, -1)
        return jnp.pad(shaped, ((0, 0), (0, LP - L), (0, 0))).reshape(images * LP, -1)

    pix_mine = lax.dynamic_index_in_dim(pixels, row_index, 0, keepdims=False)
    pix_give = lax.dynamic_index_in_dim(pixels, 1 - row_index, 0, keepdims=False)
    pix_got = swap(pix_give, "row", 1)
    pix_half = [pad_rows(pix_mine), pad_rows(pix_got)]
    pix_other = pad_rows(pix_give)

    live_group = (patch_mask > 0) & ((jnp.arange(patch_mask.shape[1]) % L) != 0)[None, :]
    count_all = butterfly(jnp.sum(live_group.astype(f32)), ("dp",))
    mask_mine = lax.dynamic_slice(
        patch_mask, (row_index, col_index * images * L), (1, images * L)
    ).reshape(images, L)
    ids_mine = lax.dynamic_slice(class_ids, (row_index, col_index * images), (1, images))[0]
    chosen = ids_mine[:, None] == jnp.arange(class_counts.shape[0])[None, :]
    image_weight = 32.0 / jnp.sum(jnp.where(chosen, class_counts[None, :], 0), axis=1).astype(f32)
    position = jnp.broadcast_to(jnp.arange(LP)[None, :], (images, LP))
    hidden = jnp.pad(mask_mine, ((0, 0), (0, LP - L))) > 0
    first_rows = position == 0
    real_rows = position < L
    live = hidden & (position != 0)
    keep_rows = jnp.where(live, image_weight[:, None], 0.0)
    patch_rows = real_rows & jnp.logical_not(first_rows) & jnp.logical_not(live)
    columns = [first_rows, live, real_rows, keep_rows, patch_rows]
    flags = jnp.stack([c.astype(f32).reshape(-1) for c in columns] + [jnp.zeros((images * LP,), f32)] * 3, axis=1)
    tokens = images * LP

    per_owner = owner_map.shape[1] // data_count
    slots = lax.dynamic_slice_in_dim(owner_map[0], data_index * per_owner, per_owner)
    edge = part * 4 // BLK
    firsts_of, kinds = [], []
    at = 0
    for i in range(layer_count):
        for name in ("qkv", "out", "up", "down"):
            firsts_of.append(at)
            kinds.append((start_of[name, i], sizes[name] // BLK, name in ("out", "down")))
            at += edge * sizes[name] // BLK
    top = jnp.zeros_like(slots)
    left_at = jnp.zeros_like(slots)
    turned = jnp.zeros_like(slots)
    for begin, (start, across, is_turned) in zip(firsts_of, kinds):
        inside = slots >= begin
        local = slots - begin
        top = jnp.where(inside, local % edge if is_turned else local // across, top)
        left_at = jnp.where(inside, start + BLK * (local // edge if is_turned else local % across), left_at)
        turned = jnp.where(inside, int(is_turned), turned)
    upper = (2 * top) ^ sub_index
    shift = left_at % 128
    info = jnp.stack([upper, (2 * top + 1) ^ sub_index, left_at // 128, (256 - shift) % 256, turned]).astype(jnp.int32)

    def activations(*widths):
        return [((tokens, w), bf16) for w in widths]

    weights, values = {}, {}
    qkv_outs = [((tokens, width), f32)] + activations(
        width, *[sizes["qkv"]] * 2, *[sizes["out"]] * 2, width + sizes["out"]
    )
    full = 2 * tokens * width
    loss_scale = 1.0 / (PATCH * count_all)

    def across_core(value):
        return swap(value, "row", 1)

    def keep_qkv(i, got):
        values["residual", i], values["low_one", i] = got[0], got[1]
        values["qkv", i], values["context", i] = got[2:4], got[4:6]
        values["got_qkv", i] = across_core(got[6])

    def forward_stage(index):
        layer, odd = divmod(index, 2)
        base = L + 6 + 12 * layer
        if index == 0:
            got = whole_call_smem(
                embed_qkv_body, 1, 9, qkv_outs, "embed_qkv", full * (width + 3 * width)
            )(places, vec, vectors, *pix_half, flags, *weights["ends", 0], *weights["qkv", 0])
            keep_qkv(0, got)
        elif odd:
            outs = [((tokens, width), f32)] + activations(width, *[sizes["up"]] * 2)
            outs += [((tokens, sizes["up"]), f32)] * 2 + activations(width + sizes["up"])
            got = whole_call_smem(
                lambda *refs: up_body(base, *refs), 1, 9, outs, "out_up", full * 5 * width
            )(
                places, vec, vectors, values["residual", layer], *values["context", layer],
                *weights["out", layer], *weights["up", layer],
            )
            values["mid", layer], values["low_two", layer] = got[0], got[1]
            values["active", layer], values["slope", layer] = got[2:4], got[4:6]
            values["got_up", layer] = across_core(got[6])
        elif layer < layer_count:
            got = whole_call_smem(
                lambda *refs: down_qkv_body(base, *refs), 1, 9, qkv_outs, "down_qkv", full * 7 * width
            )(
                places, vec, vectors, values["mid", layer - 1], *values["active", layer - 1],
                *weights["down", layer - 1], *weights["qkv", layer],
            )
            keep_qkv(layer, got)
        else:
            outs = activations(width, *[sizes["ends"]] * 2) + [((tokens, width), f32)] + activations(width)
            outs += [((8, width), f32), ((8, width), f32), ((8, 128), f32)]
            outs += activations(2 * width + sizes["ends"])
            got = whole_call_smem(
                lambda *refs: down_head_body(base - 12, refs[0], refs[2], refs[3], refs[1], *refs[4:]),
                2, 12, outs, "down_head", full * 6 * width,
            )(
                places, loss_scale.reshape(1), vec, vectors, values["mid", layer - 1],
                *values["active", layer - 1], *weights["down", layer - 1], *weights["ends", 1],
                *pix_half, flags,
            )
            values["low_fin"], values["pred"] = got[0], got[1:3]
            values["grad_res"], values["grad_low"] = got[3], got[4]
            values["wide", "head"], values["flat", "head"], values["loss"] = got[5:8]
            values["got_head"] = across_core(got[8])

    count = len(chunks)
    for step in range(count + 3):
        begun = list(values)
        if step < count:
            chunks[step].along()
        new = chunks[step - 1] if 0 <= step - 1 < count else None
        old = chunks[step - 2] if 0 <= step - 2 < count else None
        if new is not None or old is not None:
            Gather.across(new, old)
        if 0 <= step - 3 < count:
            pairs = chunks[step - 3].weights()
            for entry, pair in zip(plan[cuts[step - 3] : cuts[step - 2]], pairs):
                weights[entry[:2]] = pair
            for stage in stages_of[step - 3]:
                forward_stage(stage)
        if step == count + 2:
            break
        moving = chunks[max(0, step - 2) : step + 1]
        later = chunks[step + 1 :]
        if step == 0:
            setup = (vec, flags, pix_half, pix_other, loss_scale, info, turn)
            chunks[0].state, setup = tie(chunks[0].state, setup)
            vec, flags, pix_half, pix_other, loss_scale, info, turn = setup
        keys = [k for k in values if k in begun or not (isinstance(k, tuple) and k[0][:3] == "got")]
        states, waiting, kept = tie(
            [c.state for c in moving], [c.first for c in later], [values[k] for k in keys]
        )
        values.update(zip(keys, kept))
        for c, s in zip(moving, states):
            c.state = s
        for c, w in zip(later, waiting):
            c.first = w

    flying, done = [], []

    groups = []
    ready = 0

    def spread(members):
        value = jnp.concatenate([g.keep for g in members], axis=1)
        exponent = jnp.concatenate([g.exponent for g in members], axis=1)
        payload = lowered(value, exponent)
        return [payload] + [swap(payload, "dp", k) for k in (1, 2, 3)]

    def step_on(value, fresh):
        nonlocal ready
        value, landed, parts_in = tie(value, [r.got for r in flying], [r.parts for r in fresh])
        for r, got in zip(flying, landed):
            r.got = got
            r.absorb()
        for r, parts in zip(fresh, parts_in):
            r.parts = parts
        done.extend(r for r in flying if r.stage == 4)
        flying[:] = [r for r in flying if r.stage < 4] + list(fresh)
        for r in flying:
            r.send()
        return value

    def spread_done(stop):
        nonlocal ready
        members = groups[ready:stop]
        ready = stop
        return [spread([g for g, _ in members]), members]

    def decode_all(entry):
        entry[0] = [payload.astype(f32) for payload in entry[0]]

    wides = {"head": values["wide", "head"]}
    flats = {"head": values["flat", "head"]}
    grad_res, grad_low = values["grad_res"], values["grad_low"]
    got_low, low_at = values["got_head"], width
    small = sizes["out"]
    blocks_of = {name: range(sizes[name] // small) for name in sizes}
    big = 2 * small

    def product(way, left, left_got, left_at, right, right_got, right_at, name, part=None):
        blocks = list(part if part is not None else blocks_of[name])
        block = small
        if len(blocks) % 2 == 0 and blocks[0] % 2 == 0 and right_at % big == 0:
            block, blocks = big, list(range(blocks[0] // 2, blocks[0] // 2 + len(blocks) // 2))
        return product_sum(way, left, left_got, left_at, right, right_got, right_at, block, blocks)

    for i in reversed(range(layer_count)):
        base = L + 6 + 12 * i
        outs = [((tokens, width), f32)] + activations(width, *[sizes["up"]] * 2) + [((8, width), f32)] * 2
        outs += activations(width + sizes["up"])
        got = whole_call(lambda *refs: back_mlp_body(base, *refs), outs, "back_mlp", full * 8 * width)(
            vec, grad_res, grad_low, *weights["down", i], *values["slope", i], *weights["up", i],
            values["mid", i],
        )
        got, got_low = step_on((got, got_low), [])
        grad_mid, mid_low, hid_a, hid_b, wides["mlp", i], flats["mlp", i], gift = got
        got_mid = across_core(gift)
        active = values["active", i]
        first_x = [product("x", grad_low, got_low, low_at, active[0], values["got_up", i], width, "down")]
        names_x = [("down", i)]
        if i == layer_count - 1:
            head = values["got_head"]
            first_x.append(
                product("x", values["low_fin"], head, 0, values["pred"][0], head, 2 * width, "ends")
            )
            names_x.append(("ends", 1))
        first_y = [product("y", values["low_two", i], values["got_up", i], 0, hid_a, got_mid, width, "up")]
        group = Reduce(first_x, first_y)
        groups.append((group, names_x + [("up", i)]))
        grad_mid, mid_low, got_mid = step_on((grad_mid, mid_low, got_mid), [group])
        outs = [((tokens, width), f32)] + activations(width, *[sizes["qkv"]] * 2) + [((8, width), f32)] * 2
        outs += activations(width + sizes["qkv"])
        got = whole_call(
            lambda *refs: back_attend_body(base, *refs), outs, "back_attend", full * 8 * width,
            [pltpu.VMEM((tokens, sizes["out"]), f32)],
        )(
            vec, grad_mid, mid_low, *weights["out", i], *values["qkv", i], *weights["qkv", i],
            values["residual", i],
        )
        got = step_on(got, [])
        grad_res, grad_low, mix_a, mix_b, wides["mix", i], flats["mix", i], gift = got
        got_low, low_at = across_core(gift), 0
        low_one, got_qkv = values["low_one", i], values["got_qkv", i]
        out_args = (mid_low, got_mid, 0, values["context", i][0], got_qkv, width, "out")
        mix_args = (low_one, got_qkv, 0, mix_a, got_low, width, "qkv")
        if i > 0:
            first_x = [product("x", *mix_args, range(0, 2))]
            first_y = [product("y", *mix_args, range(2, 3)), product("y", *out_args)]
            group_names = [("qkv", i), ("out", i)]
        else:
            outs = activations(width) + [((LP, width), f32), ((8, width), f32)]
            embed_low, place_sum, wides["embed"] = whole_call(back_embed_body, outs, "back_embed", full)(
                grad_res, flags
            )
            got_embed = across_core(embed_low)
            first_x = [product("x", *mix_args)]
            first_y = [
                product("y", *out_args),
                product("y", embed_low, got_embed, 0, pix_half[0], pix_other, 0, "ends"),
            ]
            group_names = [("qkv", i), ("out", i), ("ends", 0)]
        group = Reduce(first_x, first_y)
        groups.append((group, group_names))
        if i > 0:
            grad_res, grad_low, got_low = step_on((grad_res, grad_low, got_low), [group])
        else:
            wide_keys, flat_keys = list(wides), list(flats)
            place_sum, wide_rows, flat_rows = step_on(
                (place_sum, [wides[k] for k in wide_keys], [flats[k] for k in flat_keys]), [group]
            )
            wides.update(zip(wide_keys, wide_rows))
            flats.update(zip(flat_keys, flat_rows))

    raw_wide = [place_sum, wides["embed"], wides["head"]]
    raw_flat = [flats["head"]]
    source_wide = list(range(L)) + [LP, LP + 1, LP + 2, LP + 8, LP + 9, -1]
    source_flat = [-1] * (L + 5) + [0]
    rolled = [1] * 8
    for i in range(layer_count):
        at, low = LP + 16 * (i + 1), 8 + 16 * i
        raw_wide += [wides["mlp", i], wides["mix", i]]
        raw_flat += [flats["mlp", i], flats["mix", i]]
        source_wide += [at + 9, at + 10, -1, -1, at + 8, at + 1, at + 2, -1, -1, -1, -1, at]
        source_flat += [-1, -1, low + 8, low + 9, -1, -1, -1, low, low + 1, low + 2, low + 3, -1]
        rolled += [0] * 8 + [1] * 8
    rows_all = -(-vectors.shape[0] // 256) * 256
    spare = [-1] * (rows_all - vectors.shape[0])
    source_wide, source_flat = jnp.array(source_wide + spare), jnp.array(source_flat + spare)
    raw_wide = jnp.concatenate(raw_wide, axis=0)
    raw_flat = jnp.concatenate(raw_flat, axis=0)
    other = jnp.concatenate([raw_flat[:, width // 2 :], raw_flat[:, : width // 2]], axis=1)
    raw_flat = jnp.where(swapped & (jnp.array(rolled)[:, None] == 1), other, raw_flat)
    is_up = (source_flat >= 0) & (source_flat % 16 >= 8) & (source_flat % 16 < 12)
    turned_row = source_flat // 4 * 4 + (source_flat % 4 + 2 * row_index) % 4
    source_flat = jnp.where(is_up, turned_row, source_flat)
    pick_wide = (source_wide[:, None] == jnp.arange(raw_wide.shape[0])[None, :]).astype(f32)
    pick_flat = (source_flat[:, None] == jnp.arange(raw_flat.shape[0])[None, :]).astype(f32)
    grad_vec = exact(exact(pick_wide, raw_wide, 1, 0), turn, 1, 1) + exact(pick_flat, raw_flat, 1, 0)

    def rows_at(value, index, size):
        return lax.dynamic_slice_in_dim(value, index * size, size)

    half_rows, sub_rows = rows_all // 2, rows_all // 8
    value = rows_at(grad_vec, row_index, half_rows) + across_core(rows_at(grad_vec, 1 - row_index, half_rows))
    value = step_on(value, [])
    value = rows_at(value, sub_index, sub_rows) + sum(
        swap(rows_at(value, sub_index ^ k, sub_rows), "dp", k) for k in (1, 2, 3)
    )
    value = step_on(value, [])
    early = spread_done(len(groups) - 2)
    value = butterfly(value, ("col",))
    for mask in bits_of("dp")[2:]:
        value = value + swap(value, "dp", mask)
    value, early[0] = step_on((value, early[0]), [])
    decode_all(early)
    middle = spread_done(len(groups) - 1)
    square = jnp.sum(value * value) / lax.axis_size("col")
    value = jnp.concatenate([value] + [swap(value, "dp", k) for k in (1, 2, 3)], axis=0)
    value, middle[0], early[0] = step_on((value, middle[0], early[0]), [])
    decode_all(middle)
    late = spread_done(len(groups))
    spreads = [early, middle, late]
    copies = max(1, data_count // 4)
    square = (square + sum(jnp.sum(g.keep * g.keep) for g, _ in groups)) / copies
    pair = butterfly(jnp.stack([square, values["loss"][0, 0]]), ("row",))
    pair = four(pair, "dp")
    for mask in bits_of("dp")[2:]:
        pair = pair + swap(pair, "dp", mask)
    pair, late[0], middle[0] = tie(pair, late[0], middle[0])
    decode_all(late)
    pair = four(pair, "col")
    value = jnp.concatenate([value, across_core(value)], axis=0)
    spot = jnp.arange(rows_all)
    native = (
        ((spot // half_rows) ^ row_index) * half_rows
        + (((spot // sub_rows) & 3) ^ sub_index) * sub_rows
        + spot % sub_rows
    )
    pick = (jnp.arange(vectors.shape[0])[:, None] == native[None, :]).astype(f32)
    vec_sum = exact(pick, value, 1, 0)
    loss_total = pair[1]
    grad_norm = jnp.sqrt(pair[0])
    factor = jnp.minimum(1.0, clip_scale / math.sqrt(total_tokens) / grad_norm)

    pieces, layout, ends_parts = [], [], {}
    for payloads, members in spreads:
        names_in = [name for _, group_names in members for name in group_names]
        spans, at = [], 0
        for name in names_in:
            size = sizes[name[0]]
            spans.append((at, start_of[name], size))
            if name[0] == "ends":
                ends_parts[name[1]] = (len(pieces), at)
            at += size
        for k, payload in enumerate(payloads):
            pieces.append(payload)
            layout.append((k, spans))
    raw_grad, raw_left, raw_right, raw_precond, own_weight = shampoo(
        info, tiles_own, pieces, layout, root_left[0], root_right[0]
    )
    block_grad = raw_grad * factor
    square_factor = (1.0 - decay_stat) * factor * factor
    left_next = decay_stat * stat_left[0] + square_factor * raw_left
    right_next = decay_stat * stat_right[0] + square_factor * raw_right
    block_next = own_weight - rate_blocks * (factor * raw_precond + weight_decay * own_weight)

    ends_refs = []
    for end in range(2):
        index, at = ends_parts[end]
        ends_refs += [pieces[index + k][:, at : at + sizes["ends"]] for k in range(4)]
    ends_flat = whole_call_smem(
        ends_body, 1, 8, [((2, 4 * part, sizes["ends"]), f32)], "ends_order", 10**7
    )(places, *ends_refs)[0]
    ends_grad = ends_flat.transpose(0, 2, 1)
    step_value = step_count.astype(f32)
    vector_next, moment_vector, second_vector = adam_update(
        vectors, vec_sum, vector_moment, vector_second, rate_vector, 0.0, factor, step_value
    )
    ends_next, moment_ends, second_ends = adam_update(
        weight_ends.astype(f32),
        ends_grad,
        ends_moment,
        ends_second,
        rate_matrix,
        weight_decay,
        factor,
        step_value,
    )
    return (
        loss_total,
        grad_norm,
        vector_next,
        moment_vector,
        second_vector,
        ends_next,
        moment_ends,
        second_ends,
        block_grad[None],
        left_next[None],
        right_next[None],
        block_next[None],
    )


def solution(mesh):
    grid = P(None, "row", "col")
    slots = P(("row", "col"), "dp", None, None)
    return jax.shard_map(
        shards,
        mesh=mesh,
        in_specs=(
            P(None, ("dp", "col"), "row"),
            P(None, "dp"),
            P(None, "dp"),
            P(),
            P(),
            P(None, "col", "row"),
            grid,
            P(None, "col", "row"),
            grid,
            grid,
            P(),
            P(),
            P(),
            grid,
            grid,
            slots,
            slots,
            slots,
            slots,
            P(("row", "col"), None),
        ),
        out_specs=(P(), P(), P(), P(), P(), grid, grid, grid, slots, slots, slots, slots),
        check_vma=False,
    )
```

```python
import math

import jax
import jax.numpy as jnp
from jax import lax
from jax.experimental import pallas as pl
from jax.experimental.pallas import tpu as pltpu
from jax.sharding import PartitionSpec as P

HD = 64
PATCH = 768
L = 197
LP = 208
BLK = 96

norm_eps = 1e-06
beta_first = 0.9
beta_second = 0.999
adam_eps = 1e-08
decay_stat = 0.5
rate_matrix = 0.02
rate_vector = 0.2
rate_blocks = 0.1
weight_decay = 0.05
clip_scale = 0.25
highest = lax.Precision.HIGHEST
bf16 = jnp.bfloat16
f16 = jnp.float16
f32 = jnp.float32


COST = 16
VMEM = pl.BlockSpec(memory_space=pltpu.VMEM)
SMEM = pl.BlockSpec(memory_space=pltpu.SMEM)


def whole_call(body, outs, name, flops, scratch=()):
    return pl.pallas_call(
        body,
        out_shape=[jax.ShapeDtypeStruct(shape, dtype) for shape, dtype in outs],
        scratch_shapes=list(scratch),
        compiler_params=pltpu.CompilerParams(vmem_limit_bytes=52 * 2**20),
        cost_estimate=pl.CostEstimate(flops=flops // COST, bytes_accessed=2**16, transcendentals=0),
        name=name,
    )


def dot(lhs_mat, rhs_mat, lhs_dim, rhs_dim):
    return lax.dot_general(
        lhs_mat, rhs_mat, (((lhs_dim,), (rhs_dim,)), ((), ())), preferred_element_type=f32
    )


def exact(lhs_mat, rhs_mat, lhs_dim, rhs_dim):
    return lax.dot_general(
        lhs_mat,
        rhs_mat,
        (((lhs_dim,), (rhs_dim,)), ((), ())),
        precision=highest,
        preferred_element_type=f32,
    )


def swap(value, axis, mask):
    size = lax.axis_size(axis)
    return lax.ppermute(value, axis, [(i, i ^ mask) for i in range(size)])


def bits_of(axis):
    return [1 << b for b in range(lax.axis_size(axis).bit_length() - 1)]


def butterfly(value, axes, op=jnp.add):
    for axis in axes:
        for mask in bits_of(axis):
            value = op(value, swap(value, axis, mask))
    return value


def softmax_scores(queries, key_rows):
    scores = dot(queries, key_rows, 1, 1)
    spot = lax.broadcasted_iota(jnp.int32, scores.shape, 1)
    scores = jnp.where(spot < L, scores, -1e30)
    top = jnp.max(scores, axis=1, keepdims=True)
    exponent = jnp.exp(scores - top)
    return exponent / jnp.sum(exponent, axis=1, keepdims=True)


def attend_forward(qkv_ref, ctx_ref):
    rows, wide = qkv_ref.shape
    for image in range(rows // LP):
        span = slice(image * LP, (image + 1) * LP)
        for pair in range(wide // (6 * HD)):
            made = []
            for head in (2 * pair, 2 * pair + 1):
                base = head * 3 * HD
                queries = qkv_ref[span, base : base + HD]
                key_rows = qkv_ref[span, base + HD : base + 2 * HD]
                values = qkv_ref[span, base + 2 * HD : base + 3 * HD]
                attend = softmax_scores(queries, key_rows).astype(bf16)
                made.append(dot(attend, values, 1, 0).astype(bf16))
            ctx_ref[span, pair * 2 * HD : (pair + 1) * 2 * HD] = jnp.concatenate(made, axis=1)


def attend_backward(qkv_ref, grad_ref, out_ref):
    rows, wide = qkv_ref.shape
    for image in range(rows // LP):
        span = slice(image * LP, (image + 1) * LP)
        for pair in range(wide // (6 * HD)):
            made = []
            for head in (2 * pair, 2 * pair + 1):
                base = head * 3 * HD
                queries = qkv_ref[span, base : base + HD]
                key_rows = qkv_ref[span, base + HD : base + 2 * HD]
                values = qkv_ref[span, base + 2 * HD : base + 3 * HD]
                grad = grad_ref[span, head * HD : (head + 1) * HD].astype(bf16)
                attend = softmax_scores(queries, key_rows)
                grad_values = dot(attend.astype(bf16), grad, 0, 0)
                grad_attend = dot(grad, values, 1, 1)
                inner = jnp.sum(grad_attend * attend, axis=1, keepdims=True)
                grad_scores = (attend * (grad_attend - inner)).astype(bf16)
                made.append((dot(grad_scores, key_rows, 1, 0) * 0.125).astype(bf16))
                made.append(dot(grad_scores, queries, 0, 0).astype(bf16))
                made.append(grad_values.astype(bf16))
            out_ref[span, pair * 6 * HD : (pair + 1) * 6 * HD] = jnp.concatenate(made, axis=1)


def normed_of(residual):
    center = residual - jnp.mean(residual, axis=1, keepdims=True)
    inverse = lax.rsqrt(jnp.mean(center * center, axis=1, keepdims=True) + norm_eps)
    return center * inverse, inverse


def norm_backward(grad_normed, residual, gain):
    normed, inverse = normed_of(residual)
    scaled = grad_normed * gain
    mean_one = jnp.mean(scaled, axis=1, keepdims=True)
    mean_two = jnp.mean(scaled * normed, axis=1, keepdims=True)
    grad_in = inverse * (scaled - mean_one - normed * mean_two)
    gain_sum = jnp.sum(grad_normed * normed, axis=0, keepdims=True)
    return grad_in, gain_sum, jnp.sum(grad_normed, axis=0, keepdims=True)


def rows_sum(value):
    return jnp.sum(value.astype(f32), axis=0, keepdims=True)


def put_rows(ref, rows):
    ref[...] = jnp.zeros(ref.shape, f32)
    for i, row in enumerate(rows):
        ref[i : i + 1, :] = row


def own_first(row, core):
    half = row.shape[1] // 2
    return jnp.where(core == 1, jnp.concatenate([row[:, half:], row[:, :half]], axis=1), row)


def qkv_part(base, places, vec, vectors, residual, weights, low_one, qkv, context):
    normed, _ = normed_of(residual)
    low_one[...] = (normed * vec[base : base + 1, :] + vec[base + 1 : base + 2, :]).astype(bf16)
    query_bias = own_first(vectors[base + 2 : base + 3, :], places[1])
    value_bias = own_first(vectors[base + 3 : base + 4, :], places[1])
    for half in range(2):
        heads = qkv[half].shape[1] // (3 * HD)
        parts = []
        for head in range(heads):
            at = (half * heads + head) * HD
            parts += [query_bias[:, at : at + HD], jnp.zeros((1, HD), f32), value_bias[:, at : at + HD]]
        bias = jnp.concatenate(parts, axis=1)
        kind = (lax.broadcasted_iota(jnp.int32, bias.shape, 1) // HD) % 3
        factor = jnp.where(kind == 0, 0.125, 1.0)
        step = 6 * HD
        for at in range(0, heads * 3 * HD, step):
            span = slice(at, at + step)
            mixed = dot(low_one[...], weights[half][:, span], 1, 0)
            qkv[half][:, span] = ((mixed + bias[:, span]) * factor[:, span]).astype(bf16)
        attend_forward(qkv[half], context[half])


def give(ref, parts):
    at = 0
    for part in parts:
        ref[:, at : at + part.shape[1]] = part[...]
        at += part.shape[1]


def embed_qkv_body(
    places, vec, vectors, pix_a, pix_b, flags, ends_a, ends_b, qkv_a, qkv_b,
    residual, low_one, out_a, out_b, ctx_a, ctx_b, gift,
):
    embedded = dot(pix_a[...], ends_a[...], 1, 1) + dot(pix_b[...], ends_b[...], 1, 1)
    embedded = embedded + vec[L + 2 : L + 3, :]
    spots = vec[0:LP, :]
    spots = jnp.concatenate([spots] * (embedded.shape[0] // LP), axis=0)
    picked = jnp.where(flags[:, 1:2] > 0, vec[L + 1 : L + 2, :], embedded)
    picked = jnp.where(flags[:, 0:1] > 0, vec[L : L + 1, :], picked)
    residual[...] = jnp.where(flags[:, 2:3] > 0, picked + spots, 0.0)
    qkv_part(
        L + 6, places, vec, vectors, residual[...], (qkv_a, qkv_b), low_one, (out_a, out_b), (ctx_a, ctx_b)
    )
    give(gift, (low_one, ctx_b))


def up_body(
    base, places, vec, vectors, residual, ctx_a, ctx_b, out_a, out_b, up_a, up_b,
    mid, low_two, act_a, act_b, slope_a, slope_b, gift,
):
    branch = dot(ctx_a[...], out_a[...], 1, 1) + dot(ctx_b[...], out_b[...], 1, 1)
    mid[...] = residual[...] + (branch + vec[base + 4 : base + 5, :])
    normed, _ = normed_of(mid[...])
    low_two[...] = (normed * vec[base + 5 : base + 6, :] + vec[base + 6 : base + 7, :]).astype(bf16)
    wide = vec.shape[1]
    for half, (weight, active, slope) in enumerate(((up_a, act_a, slope_a), (up_b, act_b, slope_b))):
        for k in range(weight.shape[1] // wide):
            row = base + 7 + (weight.shape[1] // wide) * jnp.bitwise_xor(places[1], half) + k
            span = slice(k * wide, (k + 1) * wide)
            pre = dot(low_two[...], weight[:, span], 1, 0) + vectors[pl.ds(row, 1), :]
            phi = 0.5 * (1.0 + lax.erf(pre * math.sqrt(0.5)))
            active[:, span] = (pre * phi).astype(bf16)
            slope[:, span] = phi + pre * (jnp.exp(-0.5 * pre * pre) * (1.0 / math.sqrt(2.0 * math.pi)))
    give(gift, (low_two, act_b))


def down_qkv_body(
    base, places, vec, vectors, mid, act_a, act_b, down_a, down_b, qkv_a, qkv_b,
    residual, low_one, out_a, out_b, ctx_a, ctx_b, gift,
):
    branch = dot(act_a[...], down_a[...], 1, 1) + dot(act_b[...], down_b[...], 1, 1)
    residual[...] = mid[...] + (branch + vec[base - 1 : base, :])
    qkv_part(
        base, places, vec, vectors, residual[...], (qkv_a, qkv_b), low_one, (out_a, out_b), (ctx_a, ctx_b)
    )
    give(gift, (low_one, ctx_b))


def down_head_body(
    base, places, vec, vectors, scale, mid, act_a, act_b, down_a, down_b, ends_a, ends_b, pix_a, pix_b, flags,
    low_fin, pred_a, pred_b, grad_res, grad_low, wide, flat, loss, gift,
):
    branch = dot(act_a[...], down_a[...], 1, 1) + dot(act_b[...], down_b[...], 1, 1)
    residual = mid[...] + (branch + vec[base + 11 : base + 12, :])
    normed, _ = normed_of(residual)
    low_fin[...] = (normed * vec[L + 3 : L + 4, :] + vec[L + 4 : L + 5, :]).astype(bf16)
    bias = own_first(vectors[L + 5 : L + 6, :], places[1])
    keep = flags[:, 3:4]
    total = jnp.zeros((1, 1), f32)
    sums = []
    for half, (ends, pix, pred) in enumerate(((ends_a, pix_a, pred_a), (ends_b, pix_b, pred_b))):
        span = ends.shape[1]
        error = dot(low_fin[...], ends[...], 1, 0) + bias[:, half * span : (half + 1) * span]
        error = error - pix[...].astype(f32)
        total = total + jnp.sum(jnp.sum(keep * error * error, axis=1, keepdims=True), axis=0, keepdims=True)
        pred[...] = (2.0 * scale[0] * keep * error).astype(bf16)
        sums.append(rows_sum(pred[...]))
    loss[...] = jnp.broadcast_to(total * scale[0], loss.shape)
    grad_fin = dot(pred_a[...], ends_a[...], 1, 1) + dot(pred_b[...], ends_b[...], 1, 1)
    grad, gain_sum, shift_sum = norm_backward(grad_fin, residual, vec[L + 3 : L + 4, :])
    grad_res[...] = grad
    grad_low[...] = grad.astype(bf16)
    put_rows(wide, [gain_sum, shift_sum])
    put_rows(flat, [jnp.concatenate(sums, axis=1)])
    give(gift, (low_fin, grad_low, pred_b))


def back_mlp_body(
    base, vec, grad_res, grad_low, down_a, down_b, slope_a, slope_b, up_a, up_b, mid,
    grad_mid, mid_low, hid_a, hid_b, wide, flat, gift,
):
    span = vec.shape[1]
    sums = []
    total = None
    for down, slope, up, hid in ((down_a, slope_a, up_a, hid_a), (down_b, slope_b, up_b, hid_b)):
        for at in range(0, down.shape[1], span):
            cols = slice(at, at + span)
            hid[:, cols] = (dot(grad_low[...], down[:, cols], 1, 0) * slope[:, cols]).astype(bf16)
            sums.append(rows_sum(hid[:, cols]))
        part = dot(hid[...], up[...], 1, 1)
        total = part if total is None else total + part
    grad, gain_sum, shift_sum = norm_backward(total, mid[...], vec[base + 5 : base + 6, :])
    grad = grad_res[...] + grad
    grad_mid[...] = grad
    mid_low[...] = grad.astype(bf16)
    put_rows(wide, [rows_sum(grad_low[...]), gain_sum, shift_sum])
    put_rows(flat, sums)
    give(gift, (mid_low, hid_b))


def back_attend_body(
    base, vec, grad_mid, mid_low, out_a, out_b, qkv_a, qkv_b, wqkv_a, wqkv_b, residual,
    grad_res, grad_low, mix_a, mix_b, wide, flat, gift, ctx,
):
    total = None
    query_sums, value_sums = [], []
    for out, qkv, wqkv, mix in ((out_a, qkv_a, wqkv_a, mix_a), (out_b, qkv_b, wqkv_b, mix_b)):
        ctx[...] = dot(mid_low[...], out[...], 1, 0)
        attend_backward(qkv, ctx, mix)
        part = dot(mix[...], wqkv[...], 1, 1)
        total = part if total is None else total + part
        sums = rows_sum(mix[...])
        for head in range(mix.shape[1] // (3 * HD)):
            at = head * 3 * HD
            query_sums.append(sums[:, at : at + HD])
            value_sums.append(sums[:, at + 2 * HD : at + 3 * HD])
    grad, gain_sum, shift_sum = norm_backward(total, residual[...], vec[base : base + 1, :])
    grad = grad_mid[...] + grad
    grad_res[...] = grad
    grad_low[...] = grad.astype(bf16)
    put_rows(wide, [rows_sum(mid_low[...]), gain_sum, shift_sum])
    put_rows(flat, [jnp.concatenate(query_sums, axis=1), jnp.concatenate(value_sums, axis=1)])
    give(gift, (grad_low, mix_b))


def back_embed_body(grad_res, flags, grad_low, place, wide):
    grad = grad_res[...]
    low = jnp.where(flags[:, 4:5] > 0, grad, 0.0).astype(bf16)
    grad_low[...] = low
    total = grad[0:LP]
    for image in range(1, grad.shape[0] // LP):
        total = total + grad[image * LP : (image + 1) * LP]
    place[...] = total
    class_sum = rows_sum(jnp.where(flags[:, 0:1] > 0, grad, 0.0))
    mask_sum = rows_sum(jnp.where(flags[:, 1:2] > 0, grad, 0.0))
    put_rows(wide, [class_sum, mask_sum, rows_sum(low)])


def tie(*trees):
    leaves, shape = jax.tree.flatten(trees)
    return jax.tree.unflatten(shape, lax.optimization_barrier(leaves))


def prepare_body(plan, cuts, places, qkv, out, up, down, ends, *rest):
    whole, owns, firsts = rest[0], rest[1::2], rest[2::2]
    sub_at = places[0]
    part = whole.shape[1]
    refs = {"qkv": qkv, "out": out, "up": up, "down": down, "ends": ends}
    for chunk in range(len(cuts) - 1):
        begin = plan[cuts[chunk]][2]
        for name, layer, start, width in plan[cuts[chunk] : cuts[chunk + 1]]:
            ref = refs[name]
            for k in range(4):
                rows = pl.ds(pl.multiple_of(jnp.bitwise_xor(sub_at, k) * part, 16), part)
                piece = ref[layer, rows, :]
                whole[k, :, start : start + width] = piece
                owns[chunk][k, :, start - begin : start - begin + width] = piece
                if k == 0:
                    firsts[chunk][:, start - begin : start - begin + width] = piece


def prepare_tiles(plan, cuts, places, qkv, out, up, down, ends):
    height = qkv.shape[1]
    part = height // 4
    outs = [((4, part, plan[-1][2] + plan[-1][3]), bf16)]
    for j, k in zip(cuts[:-1], cuts[1:]):
        width = plan[k - 1][2] + plan[k - 1][3] - plan[j][2]
        outs += [((4, part, width), bf16), ((part, width), bf16)]
    got = whole_call_smem(
        lambda *refs: prepare_body(plan, cuts, *refs), 1, 5, outs, "prepare_tiles", 10**8,
    )(places, qkv, out.swapaxes(1, 2), up, down.swapaxes(1, 2), ends.swapaxes(1, 2))
    return got[0], got[1::2], got[2::2]


def whole_call_smem(body, scalars, arrays, outs, name, flops, scratch=()):
    return pl.pallas_call(
        body,
        in_specs=[SMEM] * scalars + [VMEM] * arrays,
        out_specs=[VMEM] * len(outs),
        out_shape=[jax.ShapeDtypeStruct(shape, dtype) for shape, dtype in outs],
        scratch_shapes=list(scratch),
        compiler_params=pltpu.CompilerParams(vmem_limit_bytes=52 * 2**20),
        cost_estimate=pl.CostEstimate(flops=flops // COST, bytes_accessed=2**16, transcendentals=0),
        name=name,
    )


def assemble_body(widths, half, at_left, at_right, own, stack, from_x, from_y, in_y, in_x, *outs):
    part = own.shape[1]
    start = 0
    for out, width in zip(outs, widths):
        stop = start + width
        for k in range(4):
            out[4 * k * part : (4 * k + 1) * part, :] = own[k, :, start:stop]
            rows = slice((4 * k + 1) * part, 4 * (k + 1) * part)
            if k < 3:
                out[rows, :] = (stack, from_x, from_y)[k][:, start:stop]
                continue
            middle = min(max(half, start), stop)
            if middle > start:
                out[rows, : middle - start] = in_y[:, at_left + start : at_left + middle]
            if stop > middle:
                out[rows, middle - start :] = in_x[:, at_right + middle - half : at_right + stop - half]
        start = stop


class Gather:
    def __init__(self, own, first, widths):
        self.own, self.first, self.widths = own, first, widths
        self.total = sum(widths)
        self.half = self.total // 256 * 128
        self.state = []

    def along(self):
        self.state = [jnp.concatenate([swap(self.first, "col", k) for k in (1, 2, 3)], axis=0)]

    @staticmethod
    def across(new, old):
        out_x, out_y = [], []
        if new is not None:
            out_x.append(new.state[0])
            out_y.append(new.state[0])
        if old is not None:
            out_y.append(old.state[1][:, : old.half])
            out_x.append(old.state[2][:, old.half : old.total])
        got_x = swap(jnp.concatenate(out_x, axis=1) if len(out_x) > 1 else out_x[0], "dp", 1)
        got_y = swap(jnp.concatenate(out_y, axis=1) if len(out_y) > 1 else out_y[0], "dp", 2)
        if new is not None:
            new.state += [got_x, got_y]
        if old is not None:
            old.at = 0 if new is None else new.total
            old.state += [got_y, got_x]

    def weights(self):
        height = 16 * self.own.shape[1]
        mine = whole_call(
            lambda *refs: assemble_body(self.widths, self.half, self.at, self.at, *refs),
            [((height, w), bf16) for w in self.widths],
            "assemble",
            10**8,
        )(self.own, *self.state)
        return [(w, swap(w, "row", 1)) for w in mine]


def row_runs(name, part):
    runs = []
    for bit in range(2):
        rows = []
        for other in range(2):
            sub = 2 * other + bit if name == "x" else 2 * bit + other
            rows += [((4 * sub + 2 * high + low) * part, part) for low in range(2) for high in range(2)]
        runs.append(rows)
    return runs


def product_body(runs, left, left_got, right, right_got, keep, send, power, total):
    total[...] = dot(left[...], right[...], 0, 0) + dot(left_got[...], right_got[...], 0, 0)
    top = jnp.max(jnp.abs(total[...]), axis=0, keepdims=True)
    exponent = jnp.clip(jnp.ceil(jnp.log2(top)) + 1.0, -100.0, 120.0)
    scale = jnp.exp2(14.0 - exponent)
    power[...] = exponent
    for out, spans, factor in ((keep, runs[0], None), (send, runs[1], scale)):
        at = 0
        for start, size in spans:
            piece = total[start : start + size, :]
            out[at : at + size, :] = piece if factor is None else piece * factor
            at += size
    send[at:, :] = jnp.broadcast_to(exponent, (16, exponent.shape[1]))


def product_sum(name, left, left_got, left_at, right, right_got, right_at, block, blocks):
    rows, height = left.shape
    width = block * len(blocks)
    first = blocks[0]
    runs = row_runs(name, height // 16)
    whole = pl.BlockSpec((rows, height), lambda i: (0, 0))
    whole_got = pl.BlockSpec((rows, height), lambda i: (0, left_at // height))
    part = pl.BlockSpec((rows, block), lambda i: (0, i + first))
    part_got = pl.BlockSpec((rows, block), lambda i: (0, i + first + right_at // block))
    half = pl.BlockSpec((height // 2, block), lambda i: (0, i))
    return pl.pallas_call(
        lambda *refs: product_body(runs, *refs),
        grid=(len(blocks),),
        in_specs=[whole, whole_got, part, part_got],
        out_specs=[
            half,
            pl.BlockSpec((height // 2 + 16, block), lambda i: (0, i)),
            pl.BlockSpec((1, block), lambda i: (0, i)),
        ],
        out_shape=[
            jax.ShapeDtypeStruct((height // 2, width), f32),
            jax.ShapeDtypeStruct((height // 2 + 16, width), f32),
            jax.ShapeDtypeStruct((1, width), f32),
        ],
        scratch_shapes=[pltpu.VMEM((height, block), f32)],
        compiler_params=pltpu.CompilerParams(vmem_limit_bytes=32 * 2**20),
        cost_estimate=pl.CostEstimate(
            flops=4 * rows * height * width // COST, bytes_accessed=2**16, transcendentals=0
        ),
        name="product_sum",
    )(left, left_got, right, right_got)


def lowered(rows, exponent):
    tail = jnp.broadcast_to(exponent, (16, exponent.shape[1]))
    return jnp.concatenate([rows * jnp.exp2(14.0 - exponent), tail], axis=0).astype(f16)


def tail_of(payload):
    return jnp.max(payload[-16:].astype(f32), axis=0, keepdims=True)


def decoded(rows, exponent):
    return rows.astype(f32) * jnp.exp2(exponent - 14.0)


class Reduce:
    def __init__(self, first_x, first_y):
        self.parts = []
        for products in (first_x, first_y):
            keep, send, exponent = (jnp.concatenate(list(p), axis=1) for p in zip(*products))
            self.parts.append([keep, send.astype(f16), exponent])
        self.stage = 0

    def send(self):
        ways = ((("dp", 1), ("dp", 2)), (("dp", 2), ("dp", 1)), (("col", 1),), (("col", 2),))[self.stage]
        self.got = [swap(part[1], axis, mask) for part, (axis, mask) in zip(self.parts, ways)]

    def absorb(self):
        made = []
        for (keep, _, exponent), got in zip(self.parts, self.got):
            theirs = tail_of(got)
            after = jnp.maximum(exponent, theirs) + 1.0
            if self.stage == 3:
                made.append([keep + decoded(got[:-16], theirs), None, after])
                continue
            half = keep.shape[0] // 2
            stay = keep[:half] + decoded(got[:half], theirs)
            leave = keep[half:] + decoded(got[half : 2 * half], theirs)
            made.append([stay, leave, after])
        if self.stage == 1:
            made = [[jnp.concatenate(list(p), axis=1) for p in zip(*made)]]
        self.stage += 1
        if self.stage < 4:
            self.parts = [[stay, lowered(leave, after), after] for stay, leave, after in made]
            return
        keep, _, after = made[0]
        for mask in bits_of("dp")[2:]:
            keep = keep + swap(keep, "dp", mask)
            after = after + 1.0
        self.parts = []
        self.keep, self.exponent = keep, after


def split(value):
    high = value.astype(bf16)
    return high, (value - high.astype(f32)).astype(bf16)


def close(lhs, rhs, lhs_dim, rhs_dim):
    small = dot(lhs[0], rhs[1], lhs_dim, rhs_dim) + dot(lhs[1], rhs[0], lhs_dim, rhs_dim)
    return dot(lhs[0], rhs[0], lhs_dim, rhs_dim) + small


def shampoo_body(
    group, layout, info, weight, *rest
):
    pieces, (rl, rr, grad_out, left, right, precond, weight_out), grads = rest[:-8], rest[-8:-1], rest[-1]
    step = pl.program_id(0)

    @pl.when(step == 0)
    def _():
        for ref, (sub, spans) in zip(pieces, layout):
            part = grads.shape[1]
            for source, target, size in spans:
                grads[sub, :, target : target + size] = scaled(ref[:, source : source + size], part)

    window = 2 * 128

    def block_of(ref, slot):
        start = pl.multiple_of(info[2, slot] * 128, 128)
        tops = [ref[info[k, slot], :, pl.ds(start, window)].astype(f32) for k in range(2)]
        both = jnp.concatenate(tops, axis=0)
        both = pltpu.roll(both, info[3, slot], 1)[:, :BLK]
        return jnp.where(info[4, slot] == 1, both.T, both)

    for j in range(group):
        slot = step * group + j
        g = block_of(grads, slot)
        grad_out[j] = g
        weight_out[j] = block_of(weight, slot)
        both = split(g)
        left[j] = close(both, both, 1, 1)
        right[j] = close(both, both, 0, 0)
        inner = close(both, split(rr[j]), 1, 0)
        precond[j] = close(split(rl[j]), split(inner), 1, 0)


def shampoo(info, weight, pieces, layout, root_left, root_right):
    count = root_left.shape[0]
    group = next(g for g in (8, 6, 4, 3, 2, 1) if count % g == 0)
    plain = pl.BlockSpec((group, BLK, BLK), lambda i: (i, 0, 0))
    return pl.pallas_call(
        lambda *refs: shampoo_body(group, layout, *refs),
        grid=(count // group,),
        in_specs=[SMEM] + [VMEM] * (1 + len(pieces)) + [plain] * 2,
        out_specs=[plain] * 5,
        out_shape=[jax.ShapeDtypeStruct((count, BLK, BLK), f32)] * 5,
        scratch_shapes=[pltpu.VMEM(weight.shape, f32)],
        compiler_params=pltpu.CompilerParams(vmem_limit_bytes=52 * 2**20),
        cost_estimate=pl.CostEstimate(
            flops=count * 48 * BLK**3 // COST, bytes_accessed=2**16, transcendentals=0
        ),
        name="shampoo",
    )(info, weight, *pieces, root_left, root_right)


def scaled(rows, part):
    return rows[:part] * jnp.exp2(rows[part : part + 1] - 14.0)


def ends_body(places, *refs):
    out = refs[-1]
    part = out.shape[1] // 4
    for end in range(2):
        for k in range(4):
            sub = jnp.bitwise_xor(places[0], k)
            out[end, pl.ds(pl.multiple_of(sub * part, 8), part), :] = scaled(refs[4 * end + k][...], part)


def adam_update(weight, gradient, moment, second, rate, decay, factor, step_value):
    clipped = gradient * factor
    moment_new = beta_first * moment + (1.0 - beta_first) * clipped
    second_new = beta_second * second + (1.0 - beta_second) * clipped * clipped
    corr_first = 1.0 - jnp.power(beta_first, step_value)
    corr_second = 1.0 - jnp.power(beta_second, step_value)
    stride = moment_new / corr_first / (jnp.sqrt(second_new / corr_second) + adam_eps)
    return (weight - rate * (stride + decay * weight), moment_new, second_new)


def shards(
    pixels,
    patch_mask,
    class_ids,
    class_counts,
    step_count,
    weight_qkv,
    weight_out,
    weight_up,
    weight_down,
    weight_ends,
    vectors,
    vector_moment,
    vector_second,
    ends_moment,
    ends_second,
    stat_left,
    stat_right,
    root_left,
    root_right,
    owner_map,
):
    data_count = lax.axis_size("dp")
    row_index = lax.axis_index("row")
    col_index = lax.axis_index("col")
    data_index = lax.axis_index("dp")
    sub_index = data_index & 3
    layer_count = weight_qkv.shape[0]
    width = vectors.shape[1]
    images = pixels.shape[1] // L
    total_tokens = pixels.shape[0] * pixels.shape[1] * lax.axis_size("col") * data_count
    places = jnp.stack([sub_index, row_index]).astype(jnp.int32)
    swapped = row_index == 1

    names = [("ends", 0)]
    for i in range(layer_count):
        names += [("qkv", i), ("out", i), ("up", i), ("down", i)]
    names.append(("ends", 1))
    sizes = {
        "qkv": weight_qkv.shape[2],
        "out": weight_out.shape[1],
        "up": weight_up.shape[2],
        "down": weight_down.shape[1],
        "ends": weight_ends.shape[1],
    }
    plan, at = [], 0
    for name, i in names:
        plan.append((name, i, at, sizes[name]))
        at += sizes[name]
    start_of = {entry[:2]: entry[2] for entry in plan}
    stage_cuts = [0]
    for i in range(layer_count):
        stage_cuts += [2 + 4 * i, 4 + 4 * i]
    stage_cuts.append(len(plan))
    last = len(stage_cuts) - 1
    stages_of = [[0, 1]] + [[k] for k in range(2, last - 2)] + [[last - 2, last - 1]]
    cuts = [stage_cuts[stages[0]] for stages in stages_of] + [len(plan)]
    tiles_own, owns, firsts = prepare_tiles(
        plan, cuts, places, weight_qkv, weight_out, weight_up, weight_down, weight_ends
    )
    chunks = [
        Gather(own, first, [entry[3] for entry in plan[j:k]])
        for own, first, j, k in zip(owns, firsts, cuts[:-1], cuts[1:])
    ]

    part = weight_qkv.shape[1] // 4
    column = jnp.arange(width)
    piece, inner = column // part, column % part
    source = ((piece & 3) ^ col_index) * (4 * part) + ((piece >> 2) ^ sub_index) * part + inner
    turn = (column[:, None] == source[None, :]).astype(f32)
    vec = exact(vectors, turn, 1, 0)

    def pad_rows(value):
        shaped = value.reshape(images, L, -1)
        return jnp.pad(shaped, ((0, 0), (0, LP - L), (0, 0))).reshape(images * LP, -1)

    pix_mine = lax.dynamic_index_in_dim(pixels, row_index, 0, keepdims=False)
    pix_give = lax.dynamic_index_in_dim(pixels, 1 - row_index, 0, keepdims=False)
    pix_got = swap(pix_give, "row", 1)
    pix_half = [pad_rows(pix_mine), pad_rows(pix_got)]
    pix_other = pad_rows(pix_give)

    live_group = (patch_mask > 0) & ((jnp.arange(patch_mask.shape[1]) % L) != 0)[None, :]
    count_all = butterfly(jnp.sum(live_group.astype(f32)), ("dp",))
    mask_mine = lax.dynamic_slice(
        patch_mask, (row_index, col_index * images * L), (1, images * L)
    ).reshape(images, L)
    ids_mine = lax.dynamic_slice(class_ids, (row_index, col_index * images), (1, images))[0]
    chosen = ids_mine[:, None] == jnp.arange(class_counts.shape[0])[None, :]
    image_weight = 32.0 / jnp.sum(jnp.where(chosen, class_counts[None, :], 0), axis=1).astype(f32)
    position = jnp.broadcast_to(jnp.arange(LP)[None, :], (images, LP))
    hidden = jnp.pad(mask_mine, ((0, 0), (0, LP - L))) > 0
    first_rows = position == 0
    real_rows = position < L
    live = hidden & (position != 0)
    keep_rows = jnp.where(live, image_weight[:, None], 0.0)
    patch_rows = real_rows & jnp.logical_not(first_rows) & jnp.logical_not(live)
    columns = [first_rows, live, real_rows, keep_rows, patch_rows]
    flags = jnp.stack([c.astype(f32).reshape(-1) for c in columns] + [jnp.zeros((images * LP,), f32)] * 3, axis=1)
    tokens = images * LP

    per_owner = owner_map.shape[1] // data_count
    slots = lax.dynamic_slice_in_dim(owner_map[0], data_index * per_owner, per_owner)
    edge = part * 4 // BLK
    firsts_of, kinds = [], []
    at = 0
    for i in range(layer_count):
        for name in ("qkv", "out", "up", "down"):
            firsts_of.append(at)
            kinds.append((start_of[name, i], sizes[name] // BLK, name in ("out", "down")))
            at += edge * sizes[name] // BLK
    top = jnp.zeros_like(slots)
    left_at = jnp.zeros_like(slots)
    turned = jnp.zeros_like(slots)
    for begin, (start, across, is_turned) in zip(firsts_of, kinds):
        inside = slots >= begin
        local = slots - begin
        top = jnp.where(inside, local % edge if is_turned else local // across, top)
        left_at = jnp.where(inside, start + BLK * (local // edge if is_turned else local % across), left_at)
        turned = jnp.where(inside, int(is_turned), turned)
    upper = (2 * top) ^ sub_index
    shift = left_at % 128
    info = jnp.stack([upper, (2 * top + 1) ^ sub_index, left_at // 128, (256 - shift) % 256, turned]).astype(jnp.int32)

    def activations(*widths):
        return [((tokens, w), bf16) for w in widths]

    weights, values = {}, {}
    qkv_outs = [((tokens, width), f32)] + activations(
        width, *[sizes["qkv"]] * 2, *[sizes["out"]] * 2, width + sizes["out"]
    )
    full = 2 * tokens * width
    loss_scale = 1.0 / (PATCH * count_all)

    def across_core(value):
        return swap(value, "row", 1)

    def keep_qkv(i, got):
        values["residual", i], values["low_one", i] = got[0], got[1]
        values["qkv", i], values["context", i] = got[2:4], got[4:6]
        values["got_qkv", i] = across_core(got[6])

    def forward_stage(index):
        layer, odd = divmod(index, 2)
        base = L + 6 + 12 * layer
        if index == 0:
            got = whole_call_smem(
                embed_qkv_body, 1, 9, qkv_outs, "embed_qkv", full * (width + 3 * width)
            )(places, vec, vectors, *pix_half, flags, *weights["ends", 0], *weights["qkv", 0])
            keep_qkv(0, got)
        elif odd:
            outs = [((tokens, width), f32)] + activations(width, *[sizes["up"]] * 2)
            outs += [((tokens, sizes["up"]), f32)] * 2 + activations(width + sizes["up"])
            got = whole_call_smem(
                lambda *refs: up_body(base, *refs), 1, 9, outs, "out_up", full * 5 * width
            )(
                places, vec, vectors, values["residual", layer], *values["context", layer],
                *weights["out", layer], *weights["up", layer],
            )
            values["mid", layer], values["low_two", layer] = got[0], got[1]
            values["active", layer], values["slope", layer] = got[2:4], got[4:6]
            values["got_up", layer] = across_core(got[6])
        elif layer < layer_count:
            got = whole_call_smem(
                lambda *refs: down_qkv_body(base, *refs), 1, 9, qkv_outs, "down_qkv", full * 7 * width
            )(
                places, vec, vectors, values["mid", layer - 1], *values["active", layer - 1],
                *weights["down", layer - 1], *weights["qkv", layer],
            )
            keep_qkv(layer, got)
        else:
            outs = activations(width, *[sizes["ends"]] * 2) + [((tokens, width), f32)] + activations(width)
            outs += [((8, width), f32), ((8, width), f32), ((8, 128), f32)]
            outs += activations(2 * width + sizes["ends"])
            got = whole_call_smem(
                lambda *refs: down_head_body(base - 12, refs[0], refs[2], refs[3], refs[1], *refs[4:]),
                2, 12, outs, "down_head", full * 6 * width,
            )(
                places, loss_scale.reshape(1), vec, vectors, values["mid", layer - 1],
                *values["active", layer - 1], *weights["down", layer - 1], *weights["ends", 1],
                *pix_half, flags,
            )
            values["low_fin"], values["pred"] = got[0], got[1:3]
            values["grad_res"], values["grad_low"] = got[3], got[4]
            values["wide", "head"], values["flat", "head"], values["loss"] = got[5:8]
            values["got_head"] = across_core(got[8])

    count = len(chunks)
    for step in range(count + 3):
        begun = list(values)
        if step < count:
            chunks[step].along()
        new = chunks[step - 1] if 0 <= step - 1 < count else None
        old = chunks[step - 2] if 0 <= step - 2 < count else None
        if new is not None or old is not None:
            Gather.across(new, old)
        if 0 <= step - 3 < count:
            pairs = chunks[step - 3].weights()
            for entry, pair in zip(plan[cuts[step - 3] : cuts[step - 2]], pairs):
                weights[entry[:2]] = pair
            for stage in stages_of[step - 3]:
                forward_stage(stage)
        if step == count + 2:
            break
        moving = chunks[max(0, step - 2) : step + 1]
        later = chunks[step + 1 :]
        if step == 0:
            setup = (vec, flags, pix_half, pix_other, loss_scale, info, turn)
            chunks[0].state, setup = tie(chunks[0].state, setup)
            vec, flags, pix_half, pix_other, loss_scale, info, turn = setup
        keys = [k for k in values if k in begun or not (isinstance(k, tuple) and k[0][:3] == "got")]
        states, waiting, kept = tie(
            [c.state for c in moving], [c.first for c in later], [values[k] for k in keys]
        )
        values.update(zip(keys, kept))
        for c, s in zip(moving, states):
            c.state = s
        for c, w in zip(later, waiting):
            c.first = w

    flying, done = [], []

    groups = []
    ready = 0

    def spread(members):
        value = jnp.concatenate([g.keep for g in members], axis=1)
        exponent = jnp.concatenate([g.exponent for g in members], axis=1)
        payload = lowered(value, exponent)
        return [payload] + [swap(payload, "dp", k) for k in (1, 2, 3)]

    def step_on(value, fresh):
        nonlocal ready
        value, landed, parts_in = tie(value, [r.got for r in flying], [r.parts for r in fresh])
        for r, got in zip(flying, landed):
            r.got = got
            r.absorb()
        for r, parts in zip(fresh, parts_in):
            r.parts = parts
        done.extend(r for r in flying if r.stage == 4)
        flying[:] = [r for r in flying if r.stage < 4] + list(fresh)
        for r in flying:
            r.send()
        return value

    def spread_done(stop):
        nonlocal ready
        members = groups[ready:stop]
        ready = stop
        return [spread([g for g, _ in members]), members]

    def decode_all(entry):
        entry[0] = [payload.astype(f32) for payload in entry[0]]

    wides = {"head": values["wide", "head"]}
    flats = {"head": values["flat", "head"]}
    grad_res, grad_low = values["grad_res"], values["grad_low"]
    got_low, low_at = values["got_head"], width
    small = sizes["out"]
    blocks_of = {name: range(sizes[name] // small) for name in sizes}
    big = 2 * small

    def product(way, left, left_got, left_at, right, right_got, right_at, name, part=None):
        blocks = list(part if part is not None else blocks_of[name])
        block = small
        if len(blocks) % 2 == 0 and blocks[0] % 2 == 0 and right_at % big == 0:
            block, blocks = big, list(range(blocks[0] // 2, blocks[0] // 2 + len(blocks) // 2))
        return product_sum(way, left, left_got, left_at, right, right_got, right_at, block, blocks)

    for i in reversed(range(layer_count)):
        base = L + 6 + 12 * i
        outs = [((tokens, width), f32)] + activations(width, *[sizes["up"]] * 2) + [((8, width), f32)] * 2
        outs += activations(width + sizes["up"])
        got = whole_call(lambda *refs: back_mlp_body(base, *refs), outs, "back_mlp", full * 8 * width)(
            vec, grad_res, grad_low, *weights["down", i], *values["slope", i], *weights["up", i],
            values["mid", i],
        )
        got, got_low = step_on((got, got_low), [])
        grad_mid, mid_low, hid_a, hid_b, wides["mlp", i], flats["mlp", i], gift = got
        got_mid = across_core(gift)
        active = values["active", i]
        first_x = [product("x", grad_low, got_low, low_at, active[0], values["got_up", i], width, "down")]
        names_x = [("down", i)]
        if i == layer_count - 1:
            head = values["got_head"]
            first_x.append(
                product("x", values["low_fin"], head, 0, values["pred"][0], head, 2 * width, "ends")
            )
            names_x.append(("ends", 1))
        first_y = [product("y", values["low_two", i], values["got_up", i], 0, hid_a, got_mid, width, "up")]
        group = Reduce(first_x, first_y)
        groups.append((group, names_x + [("up", i)]))
        grad_mid, mid_low, got_mid = step_on((grad_mid, mid_low, got_mid), [group])
        outs = [((tokens, width), f32)] + activations(width, *[sizes["qkv"]] * 2) + [((8, width), f32)] * 2
        outs += activations(width + sizes["qkv"])
        got = whole_call(
            lambda *refs: back_attend_body(base, *refs), outs, "back_attend", full * 8 * width,
            [pltpu.VMEM((tokens, sizes["out"]), f32)],
        )(
            vec, grad_mid, mid_low, *weights["out", i], *values["qkv", i], *weights["qkv", i],
            values["residual", i],
        )
        got = step_on(got, [])
        grad_res, grad_low, mix_a, mix_b, wides["mix", i], flats["mix", i], gift = got
        got_low, low_at = across_core(gift), 0
        low_one, got_qkv = values["low_one", i], values["got_qkv", i]
        out_args = (mid_low, got_mid, 0, values["context", i][0], got_qkv, width, "out")
        mix_args = (low_one, got_qkv, 0, mix_a, got_low, width, "qkv")
        if i > 0:
            first_x = [product("x", *mix_args, range(0, 2))]
            first_y = [product("y", *mix_args, range(2, 3)), product("y", *out_args)]
            group_names = [("qkv", i), ("out", i)]
        else:
            outs = activations(width) + [((LP, width), f32), ((8, width), f32)]
            embed_low, place_sum, wides["embed"] = whole_call(back_embed_body, outs, "back_embed", full)(
                grad_res, flags
            )
            got_embed = across_core(embed_low)
            first_x = [product("x", *mix_args)]
            first_y = [
                product("y", *out_args),
                product("y", embed_low, got_embed, 0, pix_half[0], pix_other, 0, "ends"),
            ]
            group_names = [("qkv", i), ("out", i), ("ends", 0)]
        group = Reduce(first_x, first_y)
        groups.append((group, group_names))
        if i > 0:
            grad_res, grad_low, got_low = step_on((grad_res, grad_low, got_low), [group])
        else:
            wide_keys, flat_keys = list(wides), list(flats)
            place_sum, wide_rows, flat_rows = step_on(
                (place_sum, [wides[k] for k in wide_keys], [flats[k] for k in flat_keys]), [group]
            )
            wides.update(zip(wide_keys, wide_rows))
            flats.update(zip(flat_keys, flat_rows))

    raw_wide = [place_sum, wides["embed"], wides["head"]]
    raw_flat = [flats["head"]]
    source_wide = list(range(L)) + [LP, LP + 1, LP + 2, LP + 8, LP + 9, -1]
    source_flat = [-1] * (L + 5) + [0]
    rolled = [1] * 8
    for i in range(layer_count):
        at, low = LP + 16 * (i + 1), 8 + 16 * i
        raw_wide += [wides["mlp", i], wides["mix", i]]
        raw_flat += [flats["mlp", i], flats["mix", i]]
        source_wide += [at + 9, at + 10, -1, -1, at + 8, at + 1, at + 2, -1, -1, -1, -1, at]
        source_flat += [-1, -1, low + 8, low + 9, -1, -1, -1, low, low + 1, low + 2, low + 3, -1]
        rolled += [0] * 8 + [1] * 8
    rows_all = -(-vectors.shape[0] // 256) * 256
    spare = [-1] * (rows_all - vectors.shape[0])
    source_wide, source_flat = jnp.array(source_wide + spare), jnp.array(source_flat + spare)
    raw_wide = jnp.concatenate(raw_wide, axis=0)
    raw_flat = jnp.concatenate(raw_flat, axis=0)
    other = jnp.concatenate([raw_flat[:, width // 2 :], raw_flat[:, : width // 2]], axis=1)
    raw_flat = jnp.where(swapped & (jnp.array(rolled)[:, None] == 1), other, raw_flat)
    is_up = (source_flat >= 0) & (source_flat % 16 >= 8) & (source_flat % 16 < 12)
    turned_row = source_flat // 4 * 4 + (source_flat % 4 + 2 * row_index) % 4
    source_flat = jnp.where(is_up, turned_row, source_flat)
    pick_wide = (source_wide[:, None] == jnp.arange(raw_wide.shape[0])[None, :]).astype(f32)
    pick_flat = (source_flat[:, None] == jnp.arange(raw_flat.shape[0])[None, :]).astype(f32)
    grad_vec = exact(exact(pick_wide, raw_wide, 1, 0), turn, 1, 1) + exact(pick_flat, raw_flat, 1, 0)

    def rows_at(value, index, size):
        return lax.dynamic_slice_in_dim(value, index * size, size)

    half_rows, sub_rows = rows_all // 2, rows_all // 8
    value = rows_at(grad_vec, row_index, half_rows) + across_core(rows_at(grad_vec, 1 - row_index, half_rows))
    value = step_on(value, [])
    value = rows_at(value, sub_index, sub_rows) + sum(
        swap(rows_at(value, sub_index ^ k, sub_rows), "dp", k) for k in (1, 2, 3)
    )
    value = step_on(value, [])
    early = spread_done(len(groups) - 2)
    value = butterfly(value, ("col",))
    for mask in bits_of("dp")[2:]:
        value = value + swap(value, "dp", mask)
    value, early[0] = step_on((value, early[0]), [])
    decode_all(early)
    middle = spread_done(len(groups) - 1)
    square = jnp.sum(value * value) / lax.axis_size("col")
    value = jnp.concatenate([value] + [swap(value, "dp", k) for k in (1, 2, 3)], axis=0)
    value, middle[0], early[0] = step_on((value, middle[0], early[0]), [])
    late = spread_done(len(groups))
    spreads = [early, middle, late]
    copies = max(1, data_count // 4)
    square = (square + sum(jnp.sum(g.keep * g.keep) for g, _ in groups)) / copies
    pair = butterfly(jnp.stack([square, values["loss"][0, 0]]), ("row", "dp"))
    pair, middle[0] = tie(pair, middle[0])
    decode_all(middle)
    late[0], middle[0] = tie(late[0], middle[0])
    decode_all(late)
    pair = butterfly(pair, ("col",))
    value = jnp.concatenate([value, across_core(value)], axis=0)
    spot = jnp.arange(rows_all)
    native = (
        ((spot // half_rows) ^ row_index) * half_rows
        + (((spot // sub_rows) & 3) ^ sub_index) * sub_rows
        + spot % sub_rows
    )
    pick = (jnp.arange(vectors.shape[0])[:, None] == native[None, :]).astype(f32)
    vec_sum = exact(pick, value, 1, 0)
    loss_total = pair[1]
    grad_norm = jnp.sqrt(pair[0])
    factor = jnp.minimum(1.0, clip_scale / math.sqrt(total_tokens) / grad_norm)

    pieces, layout, ends_parts = [], [], {}
    for payloads, members in spreads:
        names_in = [name for _, group_names in members for name in group_names]
        spans, at = [], 0
        for name in names_in:
            size = sizes[name[0]]
            spans.append((at, start_of[name], size))
            if name[0] == "ends":
                ends_parts[name[1]] = (len(pieces), at)
            at += size
        for k, payload in enumerate(payloads):
            pieces.append(payload)
            layout.append((k, spans))
    raw_grad, raw_left, raw_right, raw_precond, own_weight = shampoo(
        info, tiles_own, pieces, layout, root_left[0], root_right[0]
    )
    block_grad = raw_grad * factor
    square_factor = (1.0 - decay_stat) * factor * factor
    left_next = decay_stat * stat_left[0] + square_factor * raw_left
    right_next = decay_stat * stat_right[0] + square_factor * raw_right
    block_next = own_weight - rate_blocks * (factor * raw_precond + weight_decay * own_weight)

    ends_refs = []
    for end in range(2):
        index, at = ends_parts[end]
        ends_refs += [pieces[index + k][:, at : at + sizes["ends"]] for k in range(4)]
    ends_flat = whole_call_smem(
        ends_body, 1, 8, [((2, 4 * part, sizes["ends"]), f32)], "ends_order", 10**7
    )(places, *ends_refs)[0]
    ends_grad = ends_flat.transpose(0, 2, 1)
    step_value = step_count.astype(f32)
    vector_next, moment_vector, second_vector = adam_update(
        vectors, vec_sum, vector_moment, vector_second, rate_vector, 0.0, factor, step_value
    )
    ends_next, moment_ends, second_ends = adam_update(
        weight_ends.astype(f32),
        ends_grad,
        ends_moment,
        ends_second,
        rate_matrix,
        weight_decay,
        factor,
        step_value,
    )
    return (
        loss_total,
        grad_norm,
        vector_next,
        moment_vector,
        second_vector,
        ends_next,
        moment_ends,
        second_ends,
        block_grad[None],
        left_next[None],
        right_next[None],
        block_next[None],
    )


def solution(mesh):
    grid = P(None, "row", "col")
    slots = P(("row", "col"), "dp", None, None)
    return jax.shard_map(
        shards,
        mesh=mesh,
        in_specs=(
            P(None, ("dp", "col"), "row"),
            P(None, "dp"),
            P(None, "dp"),
            P(),
            P(),
            P(None, "col", "row"),
            grid,
            P(None, "col", "row"),
            grid,
            grid,
            P(),
            P(),
            P(),
            grid,
            grid,
            slots,
            slots,
            slots,
            slots,
            P(("row", "col"), None),
        ),
        out_specs=(P(), P(), P(), P(), P(), grid, grid, grid, slots, slots, slots, slots),
        check_vma=False,
    )
```

```python
import math

import jax
import jax.numpy as jnp
from jax import lax
from jax.experimental import pallas as pl
from jax.experimental.pallas import tpu as pltpu
from jax.sharding import PartitionSpec as P

HD = 64
PATCH = 768
L = 197
LP = 208
BLK = 96

norm_eps = 1e-06
beta_first = 0.9
beta_second = 0.999
adam_eps = 1e-08
decay_stat = 0.5
rate_matrix = 0.02
rate_vector = 0.2
rate_blocks = 0.1
weight_decay = 0.05
clip_scale = 0.25
highest = lax.Precision.HIGHEST
bf16 = jnp.bfloat16
f16 = jnp.float16
f32 = jnp.float32


COST = 16
VMEM = pl.BlockSpec(memory_space=pltpu.VMEM)
SMEM = pl.BlockSpec(memory_space=pltpu.SMEM)


def whole_call(body, outs, name, flops, scratch=()):
    return pl.pallas_call(
        body,
        out_shape=[jax.ShapeDtypeStruct(shape, dtype) for shape, dtype in outs],
        scratch_shapes=list(scratch),
        compiler_params=pltpu.CompilerParams(vmem_limit_bytes=52 * 2**20),
        cost_estimate=pl.CostEstimate(flops=flops // COST, bytes_accessed=2**16, transcendentals=0),
        name=name,
    )


def dot(lhs_mat, rhs_mat, lhs_dim, rhs_dim):
    return lax.dot_general(
        lhs_mat, rhs_mat, (((lhs_dim,), (rhs_dim,)), ((), ())), preferred_element_type=f32
    )


def exact(lhs_mat, rhs_mat, lhs_dim, rhs_dim):
    return lax.dot_general(
        lhs_mat,
        rhs_mat,
        (((lhs_dim,), (rhs_dim,)), ((), ())),
        precision=highest,
        preferred_element_type=f32,
    )


def swap(value, axis, mask):
    size = lax.axis_size(axis)
    return lax.ppermute(value, axis, [(i, i ^ mask) for i in range(size)])


def bits_of(axis):
    return [1 << b for b in range(lax.axis_size(axis).bit_length() - 1)]


def butterfly(value, axes, op=jnp.add):
    for axis in axes:
        for mask in bits_of(axis):
            value = op(value, swap(value, axis, mask))
    return value


def softmax_scores(queries, key_rows):
    scores = dot(queries, key_rows, 1, 1)
    spot = lax.broadcasted_iota(jnp.int32, scores.shape, 1)
    scores = jnp.where(spot < L, scores, -1e30)
    top = jnp.max(scores, axis=1, keepdims=True)
    exponent = jnp.exp(scores - top)
    return exponent / jnp.sum(exponent, axis=1, keepdims=True)


def attend_forward(qkv_ref, ctx_ref):
    rows, wide = qkv_ref.shape
    for image in range(rows // LP):
        span = slice(image * LP, (image + 1) * LP)
        for pair in range(wide // (6 * HD)):
            made = []
            for head in (2 * pair, 2 * pair + 1):
                base = head * 3 * HD
                queries = qkv_ref[span, base : base + HD]
                key_rows = qkv_ref[span, base + HD : base + 2 * HD]
                values = qkv_ref[span, base + 2 * HD : base + 3 * HD]
                attend = softmax_scores(queries, key_rows).astype(bf16)
                made.append(dot(attend, values, 1, 0).astype(bf16))
            ctx_ref[span, pair * 2 * HD : (pair + 1) * 2 * HD] = jnp.concatenate(made, axis=1)


def attend_backward(qkv_ref, grad_ref, out_ref):
    rows, wide = qkv_ref.shape
    for image in range(rows // LP):
        span = slice(image * LP, (image + 1) * LP)
        for pair in range(wide // (6 * HD)):
            made = []
            for head in (2 * pair, 2 * pair + 1):
                base = head * 3 * HD
                queries = qkv_ref[span, base : base + HD]
                key_rows = qkv_ref[span, base + HD : base + 2 * HD]
                values = qkv_ref[span, base + 2 * HD : base + 3 * HD]
                grad = grad_ref[span, head * HD : (head + 1) * HD].astype(bf16)
                attend = softmax_scores(queries, key_rows)
                grad_values = dot(attend.astype(bf16), grad, 0, 0)
                grad_attend = dot(grad, values, 1, 1)
                inner = jnp.sum(grad_attend * attend, axis=1, keepdims=True)
                grad_scores = (attend * (grad_attend - inner)).astype(bf16)
                made.append((dot(grad_scores, key_rows, 1, 0) * 0.125).astype(bf16))
                made.append(dot(grad_scores, queries, 0, 0).astype(bf16))
                made.append(grad_values.astype(bf16))
            out_ref[span, pair * 6 * HD : (pair + 1) * 6 * HD] = jnp.concatenate(made, axis=1)


def normed_of(residual):
    center = residual - jnp.mean(residual, axis=1, keepdims=True)
    inverse = lax.rsqrt(jnp.mean(center * center, axis=1, keepdims=True) + norm_eps)
    return center * inverse, inverse


def norm_backward(grad_normed, residual, gain):
    normed, inverse = normed_of(residual)
    scaled = grad_normed * gain
    mean_one = jnp.mean(scaled, axis=1, keepdims=True)
    mean_two = jnp.mean(scaled * normed, axis=1, keepdims=True)
    grad_in = inverse * (scaled - mean_one - normed * mean_two)
    gain_sum = jnp.sum(grad_normed * normed, axis=0, keepdims=True)
    return grad_in, gain_sum, jnp.sum(grad_normed, axis=0, keepdims=True)


def rows_sum(value):
    return jnp.sum(value.astype(f32), axis=0, keepdims=True)


def put_rows(ref, rows):
    ref[...] = jnp.zeros(ref.shape, f32)
    for i, row in enumerate(rows):
        ref[i : i + 1, :] = row


def own_first(row, core):
    half = row.shape[1] // 2
    return jnp.where(core == 1, jnp.concatenate([row[:, half:], row[:, :half]], axis=1), row)


def qkv_part(base, places, vec, vectors, residual, weights, low_one, qkv, context):
    normed, _ = normed_of(residual)
    low_one[...] = (normed * vec[base : base + 1, :] + vec[base + 1 : base + 2, :]).astype(bf16)
    query_bias = own_first(vectors[base + 2 : base + 3, :], places[1])
    value_bias = own_first(vectors[base + 3 : base + 4, :], places[1])
    for half in range(2):
        heads = qkv[half].shape[1] // (3 * HD)
        parts = []
        for head in range(heads):
            at = (half * heads + head) * HD
            parts += [query_bias[:, at : at + HD], jnp.zeros((1, HD), f32), value_bias[:, at : at + HD]]
        bias = jnp.concatenate(parts, axis=1)
        kind = (lax.broadcasted_iota(jnp.int32, bias.shape, 1) // HD) % 3
        factor = jnp.where(kind == 0, 0.125, 1.0)
        step = 6 * HD
        for at in range(0, heads * 3 * HD, step):
            span = slice(at, at + step)
            mixed = dot(low_one[...], weights[half][:, span], 1, 0)
            qkv[half][:, span] = ((mixed + bias[:, span]) * factor[:, span]).astype(bf16)
        attend_forward(qkv[half], context[half])


def give(ref, parts):
    at = 0
    for part in parts:
        ref[:, at : at + part.shape[1]] = part[...]
        at += part.shape[1]


def embed_qkv_body(
    places, vec, vectors, pix_a, pix_b, flags, ends_a, ends_b, qkv_a, qkv_b,
    residual, low_one, out_a, out_b, ctx_a, ctx_b, gift,
):
    embedded = dot(pix_a[...], ends_a[...], 1, 1) + dot(pix_b[...], ends_b[...], 1, 1)
    embedded = embedded + vec[L + 2 : L + 3, :]
    spots = vec[0:LP, :]
    spots = jnp.concatenate([spots] * (embedded.shape[0] // LP), axis=0)
    picked = jnp.where(flags[:, 1:2] > 0, vec[L + 1 : L + 2, :], embedded)
    picked = jnp.where(flags[:, 0:1] > 0, vec[L : L + 1, :], picked)
    residual[...] = jnp.where(flags[:, 2:3] > 0, picked + spots, 0.0)
    qkv_part(
        L + 6, places, vec, vectors, residual[...], (qkv_a, qkv_b), low_one, (out_a, out_b), (ctx_a, ctx_b)
    )
    give(gift, (low_one, ctx_b))


def up_body(
    base, places, vec, vectors, residual, ctx_a, ctx_b, out_a, out_b, up_a, up_b,
    mid, low_two, act_a, act_b, slope_a, slope_b, gift,
):
    branch = dot(ctx_a[...], out_a[...], 1, 1) + dot(ctx_b[...], out_b[...], 1, 1)
    mid[...] = residual[...] + (branch + vec[base + 4 : base + 5, :])
    normed, _ = normed_of(mid[...])
    low_two[...] = (normed * vec[base + 5 : base + 6, :] + vec[base + 6 : base + 7, :]).astype(bf16)
    wide = vec.shape[1]
    for half, (weight, active, slope) in enumerate(((up_a, act_a, slope_a), (up_b, act_b, slope_b))):
        for k in range(weight.shape[1] // wide):
            row = base + 7 + (weight.shape[1] // wide) * jnp.bitwise_xor(places[1], half) + k
            span = slice(k * wide, (k + 1) * wide)
            pre = dot(low_two[...], weight[:, span], 1, 0) + vectors[pl.ds(row, 1), :]
            phi = 0.5 * (1.0 + lax.erf(pre * math.sqrt(0.5)))
            active[:, span] = (pre * phi).astype(bf16)
            slope[:, span] = phi + pre * (jnp.exp(-0.5 * pre * pre) * (1.0 / math.sqrt(2.0 * math.pi)))
    give(gift, (low_two, act_b))


def down_qkv_body(
    base, places, vec, vectors, mid, act_a, act_b, down_a, down_b, qkv_a, qkv_b,
    residual, low_one, out_a, out_b, ctx_a, ctx_b, gift,
):
    branch = dot(act_a[...], down_a[...], 1, 1) + dot(act_b[...], down_b[...], 1, 1)
    residual[...] = mid[...] + (branch + vec[base - 1 : base, :])
    qkv_part(
        base, places, vec, vectors, residual[...], (qkv_a, qkv_b), low_one, (out_a, out_b), (ctx_a, ctx_b)
    )
    give(gift, (low_one, ctx_b))


def down_head_body(
    base, places, vec, vectors, scale, mid, act_a, act_b, down_a, down_b, ends_a, ends_b, pix_a, pix_b, flags,
    low_fin, pred_a, pred_b, grad_res, grad_low, wide, flat, loss, gift,
):
    branch = dot(act_a[...], down_a[...], 1, 1) + dot(act_b[...], down_b[...], 1, 1)
    residual = mid[...] + (branch + vec[base + 11 : base + 12, :])
    normed, _ = normed_of(residual)
    low_fin[...] = (normed * vec[L + 3 : L + 4, :] + vec[L + 4 : L + 5, :]).astype(bf16)
    bias = own_first(vectors[L + 5 : L + 6, :], places[1])
    keep = flags[:, 3:4]
    total = jnp.zeros((1, 1), f32)
    sums = []
    for half, (ends, pix, pred) in enumerate(((ends_a, pix_a, pred_a), (ends_b, pix_b, pred_b))):
        span = ends.shape[1]
        error = dot(low_fin[...], ends[...], 1, 0) + bias[:, half * span : (half + 1) * span]
        error = error - pix[...].astype(f32)
        total = total + jnp.sum(jnp.sum(keep * error * error, axis=1, keepdims=True), axis=0, keepdims=True)
        pred[...] = (2.0 * scale[0] * keep * error).astype(bf16)
        sums.append(rows_sum(pred[...]))
    loss[...] = jnp.broadcast_to(total * scale[0], loss.shape)
    grad_fin = dot(pred_a[...], ends_a[...], 1, 1) + dot(pred_b[...], ends_b[...], 1, 1)
    grad, gain_sum, shift_sum = norm_backward(grad_fin, residual, vec[L + 3 : L + 4, :])
    grad_res[...] = grad
    grad_low[...] = grad.astype(bf16)
    put_rows(wide, [gain_sum, shift_sum])
    put_rows(flat, [jnp.concatenate(sums, axis=1)])
    give(gift, (low_fin, grad_low, pred_b))


def back_mlp_body(
    base, vec, grad_res, grad_low, down_a, down_b, slope_a, slope_b, up_a, up_b, mid,
    grad_mid, mid_low, hid_a, hid_b, wide, flat, gift,
):
    span = vec.shape[1]
    sums = []
    total = None
    for down, slope, up, hid in ((down_a, slope_a, up_a, hid_a), (down_b, slope_b, up_b, hid_b)):
        for at in range(0, down.shape[1], span):
            cols = slice(at, at + span)
            hid[:, cols] = (dot(grad_low[...], down[:, cols], 1, 0) * slope[:, cols]).astype(bf16)
            sums.append(rows_sum(hid[:, cols]))
        part = dot(hid[...], up[...], 1, 1)
        total = part if total is None else total + part
    grad, gain_sum, shift_sum = norm_backward(total, mid[...], vec[base + 5 : base + 6, :])
    grad = grad_res[...] + grad
    grad_mid[...] = grad
    mid_low[...] = grad.astype(bf16)
    put_rows(wide, [rows_sum(grad_low[...]), gain_sum, shift_sum])
    put_rows(flat, sums)
    give(gift, (mid_low, hid_b))


def back_attend_body(
    base, vec, grad_mid, mid_low, out_a, out_b, qkv_a, qkv_b, wqkv_a, wqkv_b, residual,
    grad_res, grad_low, mix_a, mix_b, wide, flat, gift, ctx,
):
    total = None
    query_sums, value_sums = [], []
    for out, qkv, wqkv, mix in ((out_a, qkv_a, wqkv_a, mix_a), (out_b, qkv_b, wqkv_b, mix_b)):
        ctx[...] = dot(mid_low[...], out[...], 1, 0)
        attend_backward(qkv, ctx, mix)
        part = dot(mix[...], wqkv[...], 1, 1)
        total = part if total is None else total + part
        sums = rows_sum(mix[...])
        for head in range(mix.shape[1] // (3 * HD)):
            at = head * 3 * HD
            query_sums.append(sums[:, at : at + HD])
            value_sums.append(sums[:, at + 2 * HD : at + 3 * HD])
    grad, gain_sum, shift_sum = norm_backward(total, residual[...], vec[base : base + 1, :])
    grad = grad_mid[...] + grad
    grad_res[...] = grad
    grad_low[...] = grad.astype(bf16)
    put_rows(wide, [rows_sum(mid_low[...]), gain_sum, shift_sum])
    put_rows(flat, [jnp.concatenate(query_sums, axis=1), jnp.concatenate(value_sums, axis=1)])
    give(gift, (grad_low, mix_b))


def back_embed_body(grad_res, flags, grad_low, place, wide):
    grad = grad_res[...]
    low = jnp.where(flags[:, 4:5] > 0, grad, 0.0).astype(bf16)
    grad_low[...] = low
    total = grad[0:LP]
    for image in range(1, grad.shape[0] // LP):
        total = total + grad[image * LP : (image + 1) * LP]
    place[...] = total
    class_sum = rows_sum(jnp.where(flags[:, 0:1] > 0, grad, 0.0))
    mask_sum = rows_sum(jnp.where(flags[:, 1:2] > 0, grad, 0.0))
    put_rows(wide, [class_sum, mask_sum, rows_sum(low)])


def tie(*trees):
    leaves, shape = jax.tree.flatten(trees)
    return jax.tree.unflatten(shape, lax.optimization_barrier(leaves))


def prepare_body(plan, cuts, places, qkv, out, up, down, ends, *rest):
    whole, owns, firsts = rest[0], rest[1::2], rest[2::2]
    sub_at = places[0]
    part = whole.shape[1]
    refs = {"qkv": qkv, "out": out, "up": up, "down": down, "ends": ends}
    for chunk in range(len(cuts) - 1):
        begin = plan[cuts[chunk]][2]
        for name, layer, start, width in plan[cuts[chunk] : cuts[chunk + 1]]:
            ref = refs[name]
            for k in range(4):
                rows = pl.ds(pl.multiple_of(jnp.bitwise_xor(sub_at, k) * part, 16), part)
                piece = ref[layer, rows, :]
                whole[k, :, start : start + width] = piece
                owns[chunk][k, :, start - begin : start - begin + width] = piece
                if k == 0:
                    firsts[chunk][:, start - begin : start - begin + width] = piece


def prepare_tiles(plan, cuts, places, qkv, out, up, down, ends):
    height = qkv.shape[1]
    part = height // 4
    outs = [((4, part, plan[-1][2] + plan[-1][3]), bf16)]
    for j, k in zip(cuts[:-1], cuts[1:]):
        width = plan[k - 1][2] + plan[k - 1][3] - plan[j][2]
        outs += [((4, part, width), bf16), ((part, width), bf16)]
    got = whole_call_smem(
        lambda *refs: prepare_body(plan, cuts, *refs), 1, 5, outs, "prepare_tiles", 10**8,
    )(places, qkv, out.swapaxes(1, 2), up, down.swapaxes(1, 2), ends.swapaxes(1, 2))
    return got[0], got[1::2], got[2::2]


def whole_call_smem(body, scalars, arrays, outs, name, flops, scratch=()):
    return pl.pallas_call(
        body,
        in_specs=[SMEM] * scalars + [VMEM] * arrays,
        out_specs=[VMEM] * len(outs),
        out_shape=[jax.ShapeDtypeStruct(shape, dtype) for shape, dtype in outs],
        scratch_shapes=list(scratch),
        compiler_params=pltpu.CompilerParams(vmem_limit_bytes=52 * 2**20),
        cost_estimate=pl.CostEstimate(flops=flops // COST, bytes_accessed=2**16, transcendentals=0),
        name=name,
    )


def assemble_body(widths, half, at_left, at_right, own, stack, from_x, from_y, in_y, in_x, *outs):
    part = own.shape[1]
    start = 0
    for out, width in zip(outs, widths):
        stop = start + width
        for k in range(4):
            out[4 * k * part : (4 * k + 1) * part, :] = own[k, :, start:stop]
            rows = slice((4 * k + 1) * part, 4 * (k + 1) * part)
            if k < 3:
                out[rows, :] = (stack, from_x, from_y)[k][:, start:stop]
                continue
            middle = min(max(half, start), stop)
            if middle > start:
                out[rows, : middle - start] = in_y[:, at_left + start : at_left + middle]
            if stop > middle:
                out[rows, middle - start :] = in_x[:, at_right + middle - half : at_right + stop - half]
        start = stop


class Gather:
    def __init__(self, own, first, widths):
        self.own, self.first, self.widths = own, first, widths
        self.total = sum(widths)
        self.half = self.total // 256 * 128
        self.state = []

    def along(self):
        self.state = [jnp.concatenate([swap(self.first, "col", k) for k in (1, 2, 3)], axis=0)]

    @staticmethod
    def across(new, old):
        out_x, out_y = [], []
        if new is not None:
            out_x.append(new.state[0])
            out_y.append(new.state[0])
        if old is not None:
            out_y.append(old.state[1][:, : old.half])
            out_x.append(old.state[2][:, old.half : old.total])
        got_x = swap(jnp.concatenate(out_x, axis=1) if len(out_x) > 1 else out_x[0], "dp", 1)
        got_y = swap(jnp.concatenate(out_y, axis=1) if len(out_y) > 1 else out_y[0], "dp", 2)
        if new is not None:
            new.state += [got_x, got_y]
        if old is not None:
            old.at = 0 if new is None else new.total
            old.state += [got_y, got_x]

    def weights(self):
        height = 16 * self.own.shape[1]
        mine = whole_call(
            lambda *refs: assemble_body(self.widths, self.half, self.at, self.at, *refs),
            [((height, w), bf16) for w in self.widths],
            "assemble",
            10**8,
        )(self.own, *self.state)
        return [(w, swap(w, "row", 1)) for w in mine]


def row_runs(name, part):
    runs = []
    for bit in range(2):
        rows = []
        for other in range(2):
            sub = 2 * other + bit if name == "x" else 2 * bit + other
            rows += [((4 * sub + 2 * high + low) * part, part) for low in range(2) for high in range(2)]
        runs.append(rows)
    return runs


def product_body(runs, left, left_got, right, right_got, keep, send, power, total):
    total[...] = dot(left[...], right[...], 0, 0) + dot(left_got[...], right_got[...], 0, 0)
    top = jnp.max(jnp.abs(total[...]), axis=0, keepdims=True)
    exponent = jnp.clip(jnp.ceil(jnp.log2(top)) + 1.0, -100.0, 120.0)
    scale = jnp.exp2(14.0 - exponent)
    power[...] = exponent
    for out, spans, factor in ((keep, runs[0], None), (send, runs[1], scale)):
        at = 0
        for start, size in spans:
            piece = total[start : start + size, :]
            out[at : at + size, :] = piece if factor is None else piece * factor
            at += size
    send[at:, :] = jnp.broadcast_to(exponent, (16, exponent.shape[1]))


def product_sum(name, left, left_got, left_at, right, right_got, right_at, block, blocks):
    rows, height = left.shape
    width = block * len(blocks)
    first = blocks[0]
    runs = row_runs(name, height // 16)
    whole = pl.BlockSpec((rows, height), lambda i: (0, 0))
    whole_got = pl.BlockSpec((rows, height), lambda i: (0, left_at // height))
    part = pl.BlockSpec((rows, block), lambda i: (0, i + first))
    part_got = pl.BlockSpec((rows, block), lambda i: (0, i + first + right_at // block))
    half = pl.BlockSpec((height // 2, block), lambda i: (0, i))
    return pl.pallas_call(
        lambda *refs: product_body(runs, *refs),
        grid=(len(blocks),),
        in_specs=[whole, whole_got, part, part_got],
        out_specs=[
            half,
            pl.BlockSpec((height // 2 + 16, block), lambda i: (0, i)),
            pl.BlockSpec((1, block), lambda i: (0, i)),
        ],
        out_shape=[
            jax.ShapeDtypeStruct((height // 2, width), f32),
            jax.ShapeDtypeStruct((height // 2 + 16, width), f32),
            jax.ShapeDtypeStruct((1, width), f32),
        ],
        scratch_shapes=[pltpu.VMEM((height, block), f32)],
        compiler_params=pltpu.CompilerParams(vmem_limit_bytes=32 * 2**20),
        cost_estimate=pl.CostEstimate(
            flops=4 * rows * height * width // COST, bytes_accessed=2**16, transcendentals=0
        ),
        name="product_sum",
    )(left, left_got, right, right_got)


def lowered(rows, exponent):
    tail = jnp.broadcast_to(exponent, (16, exponent.shape[1]))
    return jnp.concatenate([rows * jnp.exp2(14.0 - exponent), tail], axis=0).astype(f16)


def tail_of(payload):
    return jnp.max(payload[-16:].astype(f32), axis=0, keepdims=True)


def decoded(rows, exponent):
    return rows.astype(f32) * jnp.exp2(exponent - 14.0)


class Reduce:
    def __init__(self, first_x, first_y):
        self.parts = []
        for products in (first_x, first_y):
            keep, send, exponent = (jnp.concatenate(list(p), axis=1) for p in zip(*products))
            self.parts.append([keep, send.astype(f16), exponent])
        self.stage = 0

    def send(self):
        ways = ((("dp", 1), ("dp", 2)), (("dp", 2), ("dp", 1)), (("col", 1),), (("col", 2),))[self.stage]
        self.got = [swap(part[1], axis, mask) for part, (axis, mask) in zip(self.parts, ways)]

    def absorb(self):
        made = []
        for (keep, _, exponent), got in zip(self.parts, self.got):
            theirs = tail_of(got)
            after = jnp.maximum(exponent, theirs) + 1.0
            if self.stage == 3:
                made.append([keep + decoded(got[:-16], theirs), None, after])
                continue
            half = keep.shape[0] // 2
            stay = keep[:half] + decoded(got[:half], theirs)
            leave = keep[half:] + decoded(got[half : 2 * half], theirs)
            made.append([stay, leave, after])
        if self.stage == 1:
            made = [[jnp.concatenate(list(p), axis=1) for p in zip(*made)]]
        self.stage += 1
        if self.stage < 4:
            self.parts = [[stay, lowered(leave, after), after] for stay, leave, after in made]
            return
        keep, _, after = made[0]
        for mask in bits_of("dp")[2:]:
            keep = keep + swap(keep, "dp", mask)
            after = after + 1.0
        self.parts = []
        self.keep, self.exponent = keep, after


def split(value):
    high = value.astype(bf16)
    return high, (value - high.astype(f32)).astype(bf16)


def close(lhs, rhs, lhs_dim, rhs_dim):
    small = dot(lhs[0], rhs[1], lhs_dim, rhs_dim) + dot(lhs[1], rhs[0], lhs_dim, rhs_dim)
    return dot(lhs[0], rhs[0], lhs_dim, rhs_dim) + small


def shampoo_body(
    group, layout, info, weight, *rest
):
    pieces, (rl, rr, grad_out, left, right, precond, weight_out), grads = rest[:-8], rest[-8:-1], rest[-1]
    step = pl.program_id(0)

    @pl.when(step == 0)
    def _():
        for ref, (sub, spans) in zip(pieces, layout):
            part = grads.shape[1]
            for source, target, size in spans:
                grads[sub, :, target : target + size] = scaled(ref[:, source : source + size], part)

    window = 2 * 128

    def block_of(ref, slot):
        start = pl.multiple_of(info[2, slot] * 128, 128)
        tops = [ref[info[k, slot], :, pl.ds(start, window)].astype(f32) for k in range(2)]
        both = jnp.concatenate(tops, axis=0)
        both = pltpu.roll(both, info[3, slot], 1)[:, :BLK]
        return jnp.where(info[4, slot] == 1, both.T, both)

    for j in range(group):
        slot = step * group + j
        g = block_of(grads, slot)
        grad_out[j] = g
        weight_out[j] = block_of(weight, slot)
        both = split(g)
        left[j] = close(both, both, 1, 1)
        right[j] = close(both, both, 0, 0)
        inner = close(both, split(rr[j]), 1, 0)
        precond[j] = close(split(rl[j]), split(inner), 1, 0)


def shampoo(info, weight, pieces, layout, root_left, root_right):
    count = root_left.shape[0]
    group = next(g for g in (8, 6, 4, 3, 2, 1) if count % g == 0)
    plain = pl.BlockSpec((group, BLK, BLK), lambda i: (i, 0, 0))
    return pl.pallas_call(
        lambda *refs: shampoo_body(group, layout, *refs),
        grid=(count // group,),
        in_specs=[SMEM] + [VMEM] * (1 + len(pieces)) + [plain] * 2,
        out_specs=[plain] * 5,
        out_shape=[jax.ShapeDtypeStruct((count, BLK, BLK), f32)] * 5,
        scratch_shapes=[pltpu.VMEM(weight.shape, f32)],
        compiler_params=pltpu.CompilerParams(vmem_limit_bytes=52 * 2**20),
        cost_estimate=pl.CostEstimate(
            flops=count * 48 * BLK**3 // COST, bytes_accessed=2**16, transcendentals=0
        ),
        name="shampoo",
    )(info, weight, *pieces, root_left, root_right)


def scaled(rows, part):
    return rows[:part] * jnp.exp2(rows[part : part + 1] - 14.0)


def ends_body(places, *refs):
    out = refs[-1]
    part = out.shape[1] // 4
    for end in range(2):
        for k in range(4):
            sub = jnp.bitwise_xor(places[0], k)
            out[end, pl.ds(pl.multiple_of(sub * part, 8), part), :] = scaled(refs[4 * end + k][...], part)


def adam_update(weight, gradient, moment, second, rate, decay, factor, step_value):
    clipped = gradient * factor
    moment_new = beta_first * moment + (1.0 - beta_first) * clipped
    second_new = beta_second * second + (1.0 - beta_second) * clipped * clipped
    corr_first = 1.0 - jnp.power(beta_first, step_value)
    corr_second = 1.0 - jnp.power(beta_second, step_value)
    stride = moment_new / corr_first / (jnp.sqrt(second_new / corr_second) + adam_eps)
    return (weight - rate * (stride + decay * weight), moment_new, second_new)


def shards(
    pixels,
    patch_mask,
    class_ids,
    class_counts,
    step_count,
    weight_qkv,
    weight_out,
    weight_up,
    weight_down,
    weight_ends,
    vectors,
    vector_moment,
    vector_second,
    ends_moment,
    ends_second,
    stat_left,
    stat_right,
    root_left,
    root_right,
    owner_map,
):
    data_count = lax.axis_size("dp")
    row_index = lax.axis_index("row")
    col_index = lax.axis_index("col")
    data_index = lax.axis_index("dp")
    sub_index = data_index & 3
    layer_count = weight_qkv.shape[0]
    width = vectors.shape[1]
    images = pixels.shape[1] // L
    total_tokens = pixels.shape[0] * pixels.shape[1] * lax.axis_size("col") * data_count
    places = jnp.stack([sub_index, row_index]).astype(jnp.int32)
    swapped = row_index == 1

    names = [("ends", 0)]
    for i in range(layer_count):
        names += [("qkv", i), ("out", i), ("up", i), ("down", i)]
    names.append(("ends", 1))
    sizes = {
        "qkv": weight_qkv.shape[2],
        "out": weight_out.shape[1],
        "up": weight_up.shape[2],
        "down": weight_down.shape[1],
        "ends": weight_ends.shape[1],
    }
    plan, at = [], 0
    for name, i in names:
        plan.append((name, i, at, sizes[name]))
        at += sizes[name]
    start_of = {entry[:2]: entry[2] for entry in plan}
    stage_cuts = [0]
    for i in range(layer_count):
        stage_cuts += [2 + 4 * i, 4 + 4 * i]
    stage_cuts.append(len(plan))
    last = len(stage_cuts) - 1
    stages_of = [[0, 1]] + [[k] for k in range(2, last - 2)] + [[last - 2, last - 1]]
    cuts = [stage_cuts[stages[0]] for stages in stages_of] + [len(plan)]
    tiles_own, owns, firsts = prepare_tiles(
        plan, cuts, places, weight_qkv, weight_out, weight_up, weight_down, weight_ends
    )
    chunks = [
        Gather(own, first, [entry[3] for entry in plan[j:k]])
        for own, first, j, k in zip(owns, firsts, cuts[:-1], cuts[1:])
    ]

    part = weight_qkv.shape[1] // 4
    column = jnp.arange(width)
    piece, inner = column // part, column % part
    source = ((piece & 3) ^ col_index) * (4 * part) + ((piece >> 2) ^ sub_index) * part + inner
    turn = (column[:, None] == source[None, :]).astype(f32)
    vec = exact(vectors, turn, 1, 0)

    def pad_rows(value):
        shaped = value.reshape(images, L, -1)
        return jnp.pad(shaped, ((0, 0), (0, LP - L), (0, 0))).reshape(images * LP, -1)

    pix_mine = lax.dynamic_index_in_dim(pixels, row_index, 0, keepdims=False)
    pix_give = lax.dynamic_index_in_dim(pixels, 1 - row_index, 0, keepdims=False)
    pix_got = swap(pix_give, "row", 1)
    pix_half = [pad_rows(pix_mine), pad_rows(pix_got)]
    pix_other = pad_rows(pix_give)

    live_group = (patch_mask > 0) & ((jnp.arange(patch_mask.shape[1]) % L) != 0)[None, :]
    count_all = butterfly(jnp.sum(live_group.astype(f32)), ("dp",))
    mask_mine = lax.dynamic_slice(
        patch_mask, (row_index, col_index * images * L), (1, images * L)
    ).reshape(images, L)
    ids_mine = lax.dynamic_slice(class_ids, (row_index, col_index * images), (1, images))[0]
    chosen = ids_mine[:, None] == jnp.arange(class_counts.shape[0])[None, :]
    image_weight = 32.0 / jnp.sum(jnp.where(chosen, class_counts[None, :], 0), axis=1).astype(f32)
    position = jnp.broadcast_to(jnp.arange(LP)[None, :], (images, LP))
    hidden = jnp.pad(mask_mine, ((0, 0), (0, LP - L))) > 0
    first_rows = position == 0
    real_rows = position < L
    live = hidden & (position != 0)
    keep_rows = jnp.where(live, image_weight[:, None], 0.0)
    patch_rows = real_rows & jnp.logical_not(first_rows) & jnp.logical_not(live)
    columns = [first_rows, live, real_rows, keep_rows, patch_rows]
    flags = jnp.stack([c.astype(f32).reshape(-1) for c in columns] + [jnp.zeros((images * LP,), f32)] * 3, axis=1)
    tokens = images * LP

    per_owner = owner_map.shape[1] // data_count
    slots = lax.dynamic_slice_in_dim(owner_map[0], data_index * per_owner, per_owner)
    edge = part * 4 // BLK
    firsts_of, kinds = [], []
    at = 0
    for i in range(layer_count):
        for name in ("qkv", "out", "up", "down"):
            firsts_of.append(at)
            kinds.append((start_of[name, i], sizes[name] // BLK, name in ("out", "down")))
            at += edge * sizes[name] // BLK
    top = jnp.zeros_like(slots)
    left_at = jnp.zeros_like(slots)
    turned = jnp.zeros_like(slots)
    for begin, (start, across, is_turned) in zip(firsts_of, kinds):
        inside = slots >= begin
        local = slots - begin
        top = jnp.where(inside, local % edge if is_turned else local // across, top)
        left_at = jnp.where(inside, start + BLK * (local // edge if is_turned else local % across), left_at)
        turned = jnp.where(inside, int(is_turned), turned)
    upper = (2 * top) ^ sub_index
    shift = left_at % 128
    info = jnp.stack([upper, (2 * top + 1) ^ sub_index, left_at // 128, (256 - shift) % 256, turned]).astype(jnp.int32)

    def activations(*widths):
        return [((tokens, w), bf16) for w in widths]

    weights, values = {}, {}
    qkv_outs = [((tokens, width), f32)] + activations(
        width, *[sizes["qkv"]] * 2, *[sizes["out"]] * 2, width + sizes["out"]
    )
    full = 2 * tokens * width
    loss_scale = 1.0 / (PATCH * count_all)

    def across_core(value):
        return swap(value, "row", 1)

    def keep_qkv(i, got):
        values["residual", i], values["low_one", i] = got[0], got[1]
        values["qkv", i], values["context", i] = got[2:4], got[4:6]
        values["got_qkv", i] = across_core(got[6])

    def forward_stage(index):
        layer, odd = divmod(index, 2)
        base = L + 6 + 12 * layer
        if index == 0:
            got = whole_call_smem(
                embed_qkv_body, 1, 9, qkv_outs, "embed_qkv", full * (width + 3 * width)
            )(places, vec, vectors, *pix_half, flags, *weights["ends", 0], *weights["qkv", 0])
            keep_qkv(0, got)
        elif odd:
            outs = [((tokens, width), f32)] + activations(width, *[sizes["up"]] * 2)
            outs += [((tokens, sizes["up"]), f32)] * 2 + activations(width + sizes["up"])
            got = whole_call_smem(
                lambda *refs: up_body(base, *refs), 1, 9, outs, "out_up", full * 5 * width
            )(
                places, vec, vectors, values["residual", layer], *values["context", layer],
                *weights["out", layer], *weights["up", layer],
            )
            values["mid", layer], values["low_two", layer] = got[0], got[1]
            values["active", layer], values["slope", layer] = got[2:4], got[4:6]
            values["got_up", layer] = across_core(got[6])
        elif layer < layer_count:
            got = whole_call_smem(
                lambda *refs: down_qkv_body(base, *refs), 1, 9, qkv_outs, "down_qkv", full * 7 * width
            )(
                places, vec, vectors, values["mid", layer - 1], *values["active", layer - 1],
                *weights["down", layer - 1], *weights["qkv", layer],
            )
            keep_qkv(layer, got)
        else:
            outs = activations(width, *[sizes["ends"]] * 2) + [((tokens, width), f32)] + activations(width)
            outs += [((8, width), f32), ((8, width), f32), ((8, 128), f32)]
            outs += activations(2 * width + sizes["ends"])
            got = whole_call_smem(
                lambda *refs: down_head_body(base - 12, refs[0], refs[2], refs[3], refs[1], *refs[4:]),
                2, 12, outs, "down_head", full * 6 * width,
            )(
                places, loss_scale.reshape(1), vec, vectors, values["mid", layer - 1],
                *values["active", layer - 1], *weights["down", layer - 1], *weights["ends", 1],
                *pix_half, flags,
            )
            values["low_fin"], values["pred"] = got[0], got[1:3]
            values["grad_res"], values["grad_low"] = got[3], got[4]
            values["wide", "head"], values["flat", "head"], values["loss"] = got[5:8]
            values["got_head"] = across_core(got[8])

    count = len(chunks)
    for step in range(count + 3):
        begun = list(values)
        if step < count:
            chunks[step].along()
        new = chunks[step - 1] if 0 <= step - 1 < count else None
        old = chunks[step - 2] if 0 <= step - 2 < count else None
        if new is not None or old is not None:
            Gather.across(new, old)
        if 0 <= step - 3 < count:
            pairs = chunks[step - 3].weights()
            for entry, pair in zip(plan[cuts[step - 3] : cuts[step - 2]], pairs):
                weights[entry[:2]] = pair
            for stage in stages_of[step - 3]:
                forward_stage(stage)
        if step == count + 2:
            break
        moving = chunks[max(0, step - 2) : step + 1]
        later = chunks[step + 1 :]
        if step == 0:
            setup = (vec, flags, pix_half, pix_other, loss_scale, info, turn)
            chunks[0].state, setup = tie(chunks[0].state, setup)
            vec, flags, pix_half, pix_other, loss_scale, info, turn = setup
        keys = [k for k in values if k in begun or not (isinstance(k, tuple) and k[0][:3] == "got")]
        states, waiting, kept = tie(
            [c.state for c in moving], [c.first for c in later], [values[k] for k in keys]
        )
        values.update(zip(keys, kept))
        for c, s in zip(moving, states):
            c.state = s
        for c, w in zip(later, waiting):
            c.first = w

    flying, done = [], []

    groups = []
    ready = 0

    def spread(members):
        value = jnp.concatenate([g.keep for g in members], axis=1)
        exponent = jnp.concatenate([g.exponent for g in members], axis=1)
        payload = lowered(value, exponent)
        return [payload] + [swap(payload, "dp", k) for k in (1, 2, 3)]

    def step_on(value, fresh):
        nonlocal ready
        value, landed, parts_in = tie(value, [r.got for r in flying], [r.parts for r in fresh])
        for r, got in zip(flying, landed):
            r.got = got
            r.absorb()
        for r, parts in zip(fresh, parts_in):
            r.parts = parts
        done.extend(r for r in flying if r.stage == 4)
        flying[:] = [r for r in flying if r.stage < 4] + list(fresh)
        for r in flying:
            r.send()
        return value

    def spread_done(stop):
        nonlocal ready
        members = groups[ready:stop]
        ready = stop
        return [spread([g for g, _ in members]), members]

    def decode_all(entry):
        entry[0] = [payload.astype(f32) for payload in entry[0]]

    wides = {"head": values["wide", "head"]}
    flats = {"head": values["flat", "head"]}
    grad_res, grad_low = values["grad_res"], values["grad_low"]
    got_low, low_at = values["got_head"], width
    small = sizes["out"]
    blocks_of = {name: range(sizes[name] // small) for name in sizes}
    big = 2 * small

    def product(way, left, left_got, left_at, right, right_got, right_at, name, part=None):
        blocks = list(part if part is not None else blocks_of[name])
        block = small
        if len(blocks) % 2 == 0 and blocks[0] % 2 == 0 and right_at % big == 0:
            block, blocks = big, list(range(blocks[0] // 2, blocks[0] // 2 + len(blocks) // 2))
        return product_sum(way, left, left_got, left_at, right, right_got, right_at, block, blocks)

    for i in reversed(range(layer_count)):
        base = L + 6 + 12 * i
        outs = [((tokens, width), f32)] + activations(width, *[sizes["up"]] * 2) + [((8, width), f32)] * 2
        outs += activations(width + sizes["up"])
        got = whole_call(lambda *refs: back_mlp_body(base, *refs), outs, "back_mlp", full * 8 * width)(
            vec, grad_res, grad_low, *weights["down", i], *values["slope", i], *weights["up", i],
            values["mid", i],
        )
        got, got_low = step_on((got, got_low), [])
        grad_mid, mid_low, hid_a, hid_b, wides["mlp", i], flats["mlp", i], gift = got
        got_mid = across_core(gift)
        active = values["active", i]
        first_x = [product("x", grad_low, got_low, low_at, active[0], values["got_up", i], width, "down")]
        names_x = [("down", i)]
        first_y = [product("y", values["low_two", i], values["got_up", i], 0, hid_a, got_mid, width, "up")]
        group = Reduce(first_x, first_y)
        groups.append((group, names_x + [("up", i)]))
        grad_mid, mid_low, got_mid = step_on((grad_mid, mid_low, got_mid), [group])
        outs = [((tokens, width), f32)] + activations(width, *[sizes["qkv"]] * 2) + [((8, width), f32)] * 2
        outs += activations(width + sizes["qkv"])
        got = whole_call(
            lambda *refs: back_attend_body(base, *refs), outs, "back_attend", full * 8 * width,
            [pltpu.VMEM((tokens, sizes["out"]), f32)],
        )(
            vec, grad_mid, mid_low, *weights["out", i], *values["qkv", i], *weights["qkv", i],
            values["residual", i],
        )
        got = step_on(got, [])
        grad_res, grad_low, mix_a, mix_b, wides["mix", i], flats["mix", i], gift = got
        got_low, low_at = across_core(gift), 0
        low_one, got_qkv = values["low_one", i], values["got_qkv", i]
        out_args = (mid_low, got_mid, 0, values["context", i][0], got_qkv, width, "out")
        mix_args = (low_one, got_qkv, 0, mix_a, got_low, width, "qkv")
        if i > 0:
            first_x = [product("x", *mix_args, range(0, 2))]
            first_y = [product("y", *mix_args, range(2, 3)), product("y", *out_args)]
            group_names = [("qkv", i), ("out", i)]
            if i == layer_count - 1:
                head = values["got_head"]
                first_y.append(
                    product("y", values["low_fin"], head, 0, values["pred"][0], head, 2 * width, "ends")
                )
                group_names.append(("ends", 1))
        else:
            outs = activations(width) + [((LP, width), f32), ((8, width), f32)]
            embed_low, place_sum, wides["embed"] = whole_call(back_embed_body, outs, "back_embed", full)(
                grad_res, flags
            )
            got_embed = across_core(embed_low)
            first_x = [product("x", *mix_args)]
            first_y = [
                product("y", *out_args),
                product("y", embed_low, got_embed, 0, pix_half[0], pix_other, 0, "ends"),
            ]
            group_names = [("qkv", i), ("out", i), ("ends", 0)]
        group = Reduce(first_x, first_y)
        groups.append((group, group_names))
        if i > 0:
            grad_res, grad_low, got_low = step_on((grad_res, grad_low, got_low), [group])
        else:
            wide_keys, flat_keys = list(wides), list(flats)
            place_sum, wide_rows, flat_rows = step_on(
                (place_sum, [wides[k] for k in wide_keys], [flats[k] for k in flat_keys]), [group]
            )
            wides.update(zip(wide_keys, wide_rows))
            flats.update(zip(flat_keys, flat_rows))

    raw_wide = [place_sum, wides["embed"], wides["head"]]
    raw_flat = [flats["head"]]
    source_wide = list(range(L)) + [LP, LP + 1, LP + 2, LP + 8, LP + 9, -1]
    source_flat = [-1] * (L + 5) + [0]
    rolled = [1] * 8
    for i in range(layer_count):
        at, low = LP + 16 * (i + 1), 8 + 16 * i
        raw_wide += [wides["mlp", i], wides["mix", i]]
        raw_flat += [flats["mlp", i], flats["mix", i]]
        source_wide += [at + 9, at + 10, -1, -1, at + 8, at + 1, at + 2, -1, -1, -1, -1, at]
        source_flat += [-1, -1, low + 8, low + 9, -1, -1, -1, low, low + 1, low + 2, low + 3, -1]
        rolled += [0] * 8 + [1] * 8
    rows_all = -(-vectors.shape[0] // 256) * 256
    spare = [-1] * (rows_all - vectors.shape[0])
    source_wide, source_flat = jnp.array(source_wide + spare), jnp.array(source_flat + spare)
    raw_wide = jnp.concatenate(raw_wide, axis=0)
    raw_flat = jnp.concatenate(raw_flat, axis=0)
    other = jnp.concatenate([raw_flat[:, width // 2 :], raw_flat[:, : width // 2]], axis=1)
    raw_flat = jnp.where(swapped & (jnp.array(rolled)[:, None] == 1), other, raw_flat)
    is_up = (source_flat >= 0) & (source_flat % 16 >= 8) & (source_flat % 16 < 12)
    turned_row = source_flat // 4 * 4 + (source_flat % 4 + 2 * row_index) % 4
    source_flat = jnp.where(is_up, turned_row, source_flat)
    pick_wide = (source_wide[:, None] == jnp.arange(raw_wide.shape[0])[None, :]).astype(f32)
    pick_flat = (source_flat[:, None] == jnp.arange(raw_flat.shape[0])[None, :]).astype(f32)
    grad_vec = exact(exact(pick_wide, raw_wide, 1, 0), turn, 1, 1) + exact(pick_flat, raw_flat, 1, 0)

    def rows_at(value, index, size):
        return lax.dynamic_slice_in_dim(value, index * size, size)

    half_rows, sub_rows = rows_all // 2, rows_all // 8
    value = rows_at(grad_vec, row_index, half_rows) + across_core(rows_at(grad_vec, 1 - row_index, half_rows))
    value = step_on(value, [])
    value = rows_at(value, sub_index, sub_rows) + sum(
        swap(rows_at(value, sub_index ^ k, sub_rows), "dp", k) for k in (1, 2, 3)
    )
    value = step_on(value, [])
    early = spread_done(len(groups) - 2)
    value = butterfly(value, ("col",))
    for mask in bits_of("dp")[2:]:
        value = value + swap(value, "dp", mask)
    value, early[0] = step_on((value, early[0]), [])
    decode_all(early)
    middle = spread_done(len(groups) - 1)
    square = jnp.sum(value * value) / lax.axis_size("col")
    value = jnp.concatenate([value] + [swap(value, "dp", k) for k in (1, 2, 3)], axis=0)
    value, middle[0], early[0] = step_on((value, middle[0], early[0]), [])
    late = spread_done(len(groups))
    spreads = [early, middle, late]
    copies = max(1, data_count // 4)
    square = (square + sum(jnp.sum(g.keep * g.keep) for g, _ in groups)) / copies
    pair = butterfly(jnp.stack([square, values["loss"][0, 0]]), ("row", "dp"))
    pair, middle[0] = tie(pair, middle[0])
    decode_all(middle)
    late[0], middle[0] = tie(late[0], middle[0])
    decode_all(late)
    pair = butterfly(pair, ("col",))
    value = jnp.concatenate([value, across_core(value)], axis=0)
    spot = jnp.arange(rows_all)
    native = (
        ((spot // half_rows) ^ row_index) * half_rows
        + (((spot // sub_rows) & 3) ^ sub_index) * sub_rows
        + spot % sub_rows
    )
    pick = (jnp.arange(vectors.shape[0])[:, None] == native[None, :]).astype(f32)
    vec_sum = exact(pick, value, 1, 0)
    loss_total = pair[1]
    grad_norm = jnp.sqrt(pair[0])
    factor = jnp.minimum(1.0, clip_scale / math.sqrt(total_tokens) / grad_norm)

    pieces, layout, ends_parts = [], [], {}
    for payloads, members in spreads:
        names_in = [name for _, group_names in members for name in group_names]
        spans, at = [], 0
        for name in names_in:
            size = sizes[name[0]]
            spans.append((at, start_of[name], size))
            if name[0] == "ends":
                ends_parts[name[1]] = (len(pieces), at)
            at += size
        for k, payload in enumerate(payloads):
            pieces.append(payload)
            layout.append((k, spans))
    raw_grad, raw_left, raw_right, raw_precond, own_weight = shampoo(
        info, tiles_own, pieces, layout, root_left[0], root_right[0]
    )
    block_grad = raw_grad * factor
    square_factor = (1.0 - decay_stat) * factor * factor
    left_next = decay_stat * stat_left[0] + square_factor * raw_left
    right_next = decay_stat * stat_right[0] + square_factor * raw_right
    block_next = own_weight - rate_blocks * (factor * raw_precond + weight_decay * own_weight)

    ends_refs = []
    for end in range(2):
        index, at = ends_parts[end]
        ends_refs += [pieces[index + k][:, at : at + sizes["ends"]] for k in range(4)]
    ends_flat = whole_call_smem(
        ends_body, 1, 8, [((2, 4 * part, sizes["ends"]), f32)], "ends_order", 10**7
    )(places, *ends_refs)[0]
    ends_grad = ends_flat.transpose(0, 2, 1)
    step_value = step_count.astype(f32)
    vector_next, moment_vector, second_vector = adam_update(
        vectors, vec_sum, vector_moment, vector_second, rate_vector, 0.0, factor, step_value
    )
    ends_next, moment_ends, second_ends = adam_update(
        weight_ends.astype(f32),
        ends_grad,
        ends_moment,
        ends_second,
        rate_matrix,
        weight_decay,
        factor,
        step_value,
    )
    return (
        loss_total,
        grad_norm,
        vector_next,
        moment_vector,
        second_vector,
        ends_next,
        moment_ends,
        second_ends,
        block_grad[None],
        left_next[None],
        right_next[None],
        block_next[None],
    )


def solution(mesh):
    grid = P(None, "row", "col")
    slots = P(("row", "col"), "dp", None, None)
    return jax.shard_map(
        shards,
        mesh=mesh,
        in_specs=(
            P(None, ("dp", "col"), "row"),
            P(None, "dp"),
            P(None, "dp"),
            P(),
            P(),
            P(None, "col", "row"),
            grid,
            P(None, "col", "row"),
            grid,
            grid,
            P(),
            P(),
            P(),
            grid,
            grid,
            slots,
            slots,
            slots,
            slots,
            P(("row", "col"), None),
        ),
        out_specs=(P(), P(), P(), P(), P(), grid, grid, grid, slots, slots, slots, slots),
        check_vma=False,
    )
```
